32 devices in a mesh: cell: 8 (over y, x, core), cls: 4 (over z).
Axes of the slice: x: 2, y: 2, z: 4, core: 2. Of those that a mesh axis runs over, the one named last changes fastest.
Arguments:
- melt: float32 [64, 32, 8192], P(None, 'cls', 'cell'), may hold values from 0 to 1
- counts: int32 [32, 8192], P('cls', 'cell'), may hold values from 0 to 800, as said below
- pressure: float32 [32, 256], P(('cell', 'cls')), may hold values from 0.5 to 2
- propagator: float32 [32, 64, 64], replicated, as said below
- coupling: float32 [32, 64], replicated, may hold values from 0.05 to 0.5
- flux_weights: float32 [32, 64], replicated, may hold values from 0.002 to 0.2
Outputs:
- shells_out: float32 [64, 32, 8192], P(None, 'cls', 'cell')
- pressure_out: float32 [32, 256], P(('cell', 'cls'))
The draws below stay inside these ranges and needn't reach their ends.
Inputs may be any that keep to these rules, and one draw needn't show every extreme that they name: counts in layer l are non-negative and below 201 + (600 * l) // 31. Each propagator matrix has a dominant diagonal.
All inputs are finite; a program needn't handle non-finite values.
Results may differ from the reference program's by a relative error of at most 0.0001.
Values sent between devices are 32-bit elements; how exact they have to be, the bound alone decides.
No kernel may reach another device: no remote copies, remote signals or barrier semaphores. Data moves between devices by JAX's collectives and lax.ppermute only.
A program may use at most 64 MiB of HBM per device.

```python
import math
import jax
import jax.numpy as jnp
from jax import lax

NODES = 64
CLASSES = 32
SIDE = 16
SUBSTEPS = 4
PLANE = 256
NZ = 32
NCELLS = 8192


def draw_counts(key, part):
    layer = jnp.arange(NCELLS, dtype=jnp.int32) // PLANE
    upper = 201 + 600 * layer // (NZ - 1)
    upper = jnp.broadcast_to(upper[None, :], (CLASSES, NCELLS))
    values = jax.random.randint(key, (CLASSES, NCELLS), 0, upper).astype(jnp.int32)
    class_idx = jnp.arange(CLASSES, dtype=jnp.int32)[:, None]
    cell_idx = jnp.arange(NCELLS, dtype=jnp.int32)[None, :]
    at_top = jnp.logical_and(class_idx == 0, cell_idx == NCELLS - 1)
    return jnp.where(at_top, jnp.int32(800), values).astype(jnp.int32)


def draw_propagator(key, part):
    first, second = jax.random.split(jax.random.fold_in(key, 7))
    diag_vals = jax.random.uniform(first, (CLASSES, NODES, 1), jnp.float32, 0.5, 0.9)
    off_vals = jnp.clip(0.005 * jax.random.normal(second, (CLASSES, NODES, NODES), jnp.float32), -0.007, 0.007)
    rows = jnp.arange(NODES)[:, None]
    cols = jnp.arange(NODES)[None, :]
    return jnp.where((rows == cols)[None, :, :], diag_vals, off_vals).astype(jnp.float32)


def level_of(own_key, dims, pieces, low, top_value):
    factor_of = 1.0
    for axis_at, blocks in pieces:
        heights = jax.random.uniform(jax.random.fold_in(jax.random.fold_in(own_key, 6), axis_at), (blocks,), jnp.float32, low / len(pieces), top_value / len(pieces))
        factor_of = factor_of * jnp.repeat(jnp.exp(heights), dims[axis_at] // blocks).reshape((-1,) + (1,) * (len(dims) - 1 - axis_at))
    return factor_of


def setup_inputs(seed: int = 0) -> dict:
    seeds = jax.random.split(jax.random.key(seed), 7)
    melt = jnp.clip(1.0 * jax.random.uniform(seeds[0], (NODES, CLASSES, NCELLS), jnp.float32) ** level_of(seeds[0], (NODES, CLASSES, NCELLS), ((1, 4), (2, 8)), -0.2, 0.2), 0.0, 1.0)
    counts = draw_counts(jax.random.fold_in(seeds[6], 71), 0)
    pressure = jnp.clip(0.5 + 1.5 * jax.random.uniform(seeds[2], (NZ, PLANE), jnp.float32) ** level_of(seeds[2], (NZ, PLANE), ((0, 32),), -0.2, 0.2), 0.5, 2.0)
    propagator = draw_propagator(jax.random.fold_in(seeds[6], 71), 0)
    coupling = jnp.clip(jnp.exp(jax.random.uniform(seeds[4], (CLASSES, NODES), jnp.float32, math.log(0.05), math.log(0.5))), 0.05, 0.5)
    flux_weights = jnp.clip(jnp.exp(jax.random.uniform(seeds[5], (CLASSES, NODES), jnp.float32, math.log(0.002), math.log(0.2))), 0.002, 0.2)
    return dict(melt=melt, counts=counts, pressure=pressure, propagator=propagator, coupling=coupling, flux_weights=flux_weights)


count_scale = 400.0


def reference(melt, counts, pressure, propagator, coupling, flux_weights):
    counts_f = counts.astype(jnp.float32)
    for step in range(SUBSTEPS):
        wall = 0.5 * pressure.reshape(NCELLS)
        melt = jnp.einsum('kij,jkc->ikc', propagator, melt, precision=lax.Precision.HIGHEST) + coupling.T[:, :, None] * wall[None, None, :]
        flux = jnp.einsum('ki,ikc->kc', flux_weights, melt, precision=lax.Precision.HIGHEST)
        gas = jnp.sum(counts_f * flux, axis=0) / (count_scale * CLASSES)
        chamber = 1.5 - 0.5 * jnp.sum(gas) / NCELLS
        field = pressure.reshape(NZ, SIDE, SIDE)
        padded = jnp.pad(field, 1)
        lap = padded[2:, 1:-1, 1:-1] + padded[:-2, 1:-1, 1:-1] + padded[1:-1, 2:, 1:-1] + padded[1:-1, :-2, 1:-1] + padded[1:-1, 1:-1, 2:] + padded[1:-1, 1:-1, :-2] - 6.0 * field
        field = field + 0.15 * lap + 0.1 * gas.reshape(NZ, SIDE, SIDE) + 0.2 * (chamber - field)
        pressure = field.reshape(NZ, PLANE)
    return melt, pressure
```

```python
import jax
import jax.numpy as jnp
from jax import lax
from jax.sharding import PartitionSpec as P

CLASSES = 32
SIDE = 16
SUBSTEPS = 4
COUNT_SCALE = 400.0

HIGHEST = lax.Precision.HIGHEST


def chains(prop, coupling, flux_weights):
    scale = jnp.maximum(1.0, jnp.max(jnp.abs(prop), axis=(1, 2)))
    unit = prop / scale[:, None, None]
    square = jnp.einsum("kij,kjl->kil", unit, unit, precision=HIGHEST)
    fourth = jnp.einsum("kij,kjl->kil", square, square, precision=HIGHEST)
    rows = [flux_weights]
    columns = [coupling]
    for _ in range(SUBSTEPS):
        rows.append(jnp.einsum("ki,kij->kj", rows[-1], unit, precision=HIGHEST))
    for _ in range(SUBSTEPS - 1):
        columns.append(jnp.einsum("kij,kj->ki", unit, columns[-1], precision=HIGHEST))
    return scale, fourth, rows[1:], columns


def grow(value, factor, times):
    for _ in range(times):
        value = value * factor
    return value


def partial_fields(melt, counts_n, scale, rows, columns, flux_weights):
    fields = []
    for t in range(SUBSTEPS):
        flux = jnp.einsum("ki,ikc->kc", rows[t], melt, precision=HIGHEST)
        fields.append(jnp.sum(grow(counts_n * flux, scale[:, None], t + 1), axis=0))
    for d in range(SUBSTEPS):
        response = grow(jnp.sum(flux_weights * columns[d], axis=1), scale, d)
        fields.append(jnp.sum(counts_n * response[:, None], axis=0))
    return fields


def laplacian(field):
    padded = jnp.pad(field, 1)
    return (
        padded[2:, 1:-1, 1:-1]
        + padded[:-2, 1:-1, 1:-1]
        + padded[1:-1, 2:, 1:-1]
        + padded[1:-1, :-2, 1:-1]
        + padded[1:-1, 1:-1, 2:]
        + padded[1:-1, 1:-1, :-2]
        - 6.0 * field
    )


def evolve(own, response, field):
    walls = []
    for t in range(SUBSTEPS):
        walls.append(0.5 * field)
        gas = own[t]
        for s in range(t + 1):
            gas = gas + response[t - s] * walls[s]
        chamber = 1.5 - 0.5 * jnp.sum(gas) / gas.size
        field = field + 0.15 * laplacian(field) + 0.1 * gas + 0.2 * (chamber - field)
    return walls, field


def shards(melt, counts, pressure, propagator, coupling, flux_weights):
    nodes, class_count, cells = melt.shape
    plane = pressure.shape[1]
    layers = cells // plane
    cls = lax.axis_index("cls")
    cell = lax.axis_index("cell")
    start = cls * class_count
    prop = lax.dynamic_slice_in_dim(propagator, start, class_count, 0)
    couple = lax.dynamic_slice_in_dim(coupling, start, class_count, 0)
    flux_w = lax.dynamic_slice_in_dim(flux_weights, start, class_count, 0)
    counts_n = counts.astype(jnp.float32) / (COUNT_SCALE * CLASSES)
    scale, fourth, rows, columns = chains(prop, couple, flux_w)
    fields = partial_fields(melt, counts_n, scale, rows, columns, flux_w)
    own_pressure = lax.dynamic_update_slice_in_dim(
        jnp.zeros((cells,), jnp.float32), pressure.reshape(-1), cls * plane * pressure.shape[0], 0
    )
    packed = jnp.stack(fields + [own_pressure])
    shells = grow(
        jnp.einsum("kij,jkc->ikc", fourth, melt, precision=HIGHEST), scale[None, :, None], SUBSTEPS
    )
    packed = lax.psum(packed, "cls")
    window = lax.all_gather(packed, "cell", axis=0)
    window = jnp.moveaxis(window, 1, 0).reshape(packed.shape[0], -1, SIDE, plane // SIDE)
    walls, field = evolve(window[:SUBSTEPS], window[SUBSTEPS : 2 * SUBSTEPS], window[2 * SUBSTEPS])
    for s in range(SUBSTEPS):
        own = lax.dynamic_slice_in_dim(walls[s], cell * layers, layers, 0).reshape(-1)
        column = grow(columns[SUBSTEPS - 1 - s], scale[:, None], SUBSTEPS - 1 - s)
        shells = shells + column.T[:, :, None] * own[None, None, :]
    tile = lax.dynamic_slice_in_dim(
        field, cell * layers + cls * pressure.shape[0], pressure.shape[0], 0
    )
    return shells, tile.reshape(pressure.shape)


def solution(mesh):
    placed = (P(None, "cls", "cell"), P("cls", "cell"), P(("cell", "cls"), None), P(), P(), P())
    return jax.shard_map(
        shards,
        mesh=mesh,
        in_specs=placed,
        out_specs=(P(None, "cls", "cell"), P(("cell", "cls"), None)),
        check_vma=False,
    )
```

```python
import functools

import jax
import jax.numpy as jnp
from jax import lax
from jax.experimental import pallas as pl
from jax.experimental.pallas import tpu as pltpu
from jax.sharding import PartitionSpec as P

CLASSES = 32
SIDE = 16
SUBSTEPS = 4
COUNT_SCALE = 400.0
LANES = 128
GROUP = 8
FIELDS = 2 * SUBSTEPS + 1

HIGHEST = lax.Precision.HIGHEST


def grow(value, factor, times):
    for _ in range(times):
        value = value * factor
    return value


def iota(shape, dim):
    return lax.broadcasted_iota(jnp.int32, shape, dim)


def class_scale(prop):
    rows = [jnp.max(jnp.abs(prop[k]), axis=0, keepdims=True) for k in range(prop.shape[0])]
    return jnp.maximum(1.0, jnp.max(jnp.concatenate(rows, axis=0), axis=1, keepdims=True))


def param_copies(prop_any, coup_any, flux_any, prop, coup, flux, sems):
    own = pl.ds(lax.axis_index("cls") * prop.shape[0], prop.shape[0])
    copies = [
        pltpu.make_async_copy(prop_any.at[own], prop, sems.at[0]),
        pltpu.make_async_copy(coup_any.at[own], coup, sems.at[1]),
    ]
    if flux is not None:
        copies.append(pltpu.make_async_copy(flux_any.at[own], flux, sems.at[2]))
    return copies


def fields_kernel(
    copies_out, melt_any, counts, pressure, prop_any, coup_any, flux_any, out, melt, prop, coup, flux, sems, param_sems
):
    nodes, classes, cells = melt.shape
    params = param_copies(prop_any, coup_any, flux_any, prop, coup, flux, param_sems)
    for copy in params:
        copy.start()
    parts = nodes // GROUP
    pieces = [
        pltpu.make_async_copy(
            melt_any.at[pl.ds(g * GROUP, GROUP)], melt.at[pl.ds(g * GROUP, GROUP)], sems.at[g]
        )
        for g in range(parts)
    ]
    for piece in pieces:
        piece.start()
    for copy in params:
        copy.wait()
    scale = class_scale(prop)
    table = prop[...].reshape(classes * nodes, nodes)
    mask = iota((classes, classes * nodes), 1) // nodes == iota((classes, classes * nodes), 0)
    rows = [flux[...]]
    for _ in range(SUBSTEPS):
        wide = jnp.where(mask, jnp.concatenate([rows[-1]] * classes, axis=1), 0.0)
        rows.append(jnp.dot(wide, table, precision=HIGHEST, preferred_element_type=jnp.float32) / scale)
    counts_n = counts[...].astype(jnp.float32) / (COUNT_SCALE * CLASSES)
    chunks = cells // LANES
    spread = [
        grow(jnp.sum(rows[d] * coup[...], axis=1, keepdims=True), scale, d) for d in range(SUBSTEPS)
    ]
    sums = [[jnp.zeros((classes, LANES), jnp.float32) for _ in range(chunks)] for _ in range(SUBSTEPS)]
    for g in range(parts):
        pieces[g].wait()
        for j in range(g * GROUP, (g + 1) * GROUP):
            weights = [
                jnp.broadcast_to(rows[t + 1][:, j : j + 1], (classes, LANES)) for t in range(SUBSTEPS)
            ]
            for r in range(chunks):
                value = melt[j, :, r * LANES : (r + 1) * LANES]
                for t in range(SUBSTEPS):
                    sums[t][r] = sums[t][r] + weights[t] * value
    tile = pressure.shape[0] * pressure.shape[1] // LANES
    for n in range(copies_out):
        out[n, 2 * SUBSTEPS] = jnp.zeros((chunks, LANES), jnp.float32)
    for r in range(chunks):
        here = counts_n[:, r * LANES : (r + 1) * LANES]
        for t in range(SUBSTEPS):
            row = jnp.sum(grow(here * sums[t][r], scale, t + 1), axis=0, keepdims=True)
            for n in range(copies_out):
                out[n, t, r : r + 1, :] = row
        for d in range(SUBSTEPS):
            row = jnp.sum(here * spread[d], axis=0, keepdims=True)
            for n in range(copies_out):
                out[n, SUBSTEPS + d, r : r + 1, :] = row
    at = lax.axis_index("cls") * tile
    per = pressure.shape[1] // LANES
    for i in range(tile):
        row = pressure[i // per : i // per + 1, (i % per) * LANES : (i % per + 1) * LANES]
        for n in range(copies_out):
            out[n, 2 * SUBSTEPS, pl.ds(at + i, 1), :] = row


def power_kernel(melt_any, prop_any, coup_any, out, columns, melt, prop, coup, sems, param_sems):
    chunks = out.shape[0]
    classes, nodes = prop.shape[:2]
    params = param_copies(prop_any, coup_any, None, prop, coup, None, param_sems)
    for copy in params:
        copy.start()
    loads = [
        pltpu.make_async_copy(
            melt_any.at[:, pl.ds(r * LANES, LANES)], melt.at[r], sems.at[r]
        )
        for r in range(chunks)
    ]
    for load in loads:
        load.start()
    for copy in params:
        copy.wait()
    scale = class_scale(prop)
    unit = [prop[k] / scale[k : k + 1, :] for k in range(classes)]
    table = jnp.concatenate(unit, axis=0)
    column = coup[...]
    columns[0] = column
    for d in range(1, SUBSTEPS):
        pairs = lax.dot_general(
            column, table, (((1,), (1,)), ((), ())), precision=HIGHEST, preferred_element_type=jnp.float32
        )
        column = jnp.concatenate(
            [pairs[k : k + 1, k * nodes : (k + 1) * nodes] for k in range(classes)], axis=0
        )
        columns[d] = grow(column, scale, d)
    for load in loads:
        load.wait()
    together = 4
    width = together * nodes
    mask = iota((width, width), 0) // nodes == iota((width, width), 1) // nodes
    for first in range(0, classes, together):
        some = jnp.concatenate(unit[first : first + together], axis=0)
        block = jnp.where(mask, jnp.concatenate([some] * together, axis=1), 0.0)
        for _ in range(2):
            block = jnp.dot(block, block, precision=HIGHEST, preferred_element_type=jnp.float32)
        x = jnp.concatenate(
            [
                jnp.concatenate(
                    [
                        melt[r, pl.ds(first + k, nodes, stride=classes), :]
                        for k in range(together)
                    ],
                    axis=0,
                )
                for r in range(chunks)
            ],
            axis=1,
        )
        y = jnp.dot(block, x, precision=HIGHEST, preferred_element_type=jnp.float32)
        for k in range(together):
            part = grow(
                y[k * nodes : (k + 1) * nodes], scale[first + k : first + k + 1, :], SUBSTEPS
            )
            for r in range(chunks):
                out[r, pl.ds(first + k, nodes, stride=classes), :] = part[
                    :, r * LANES : (r + 1) * LANES
                ]


def laplacian(x, plane):
    rows = x.shape[0]
    row = iota(x.shape, 0)
    lane = iota(x.shape, 1)
    per = plane // LANES
    inside = row % per * LANES + lane
    col = lane % SIDE
    total = jnp.where(col == 0, 0.0, pltpu.roll(x, 1, 1))
    total += jnp.where(col == SIDE - 1, 0.0, pltpu.roll(x, LANES - 1, 1))
    up = pltpu.roll(x, SIDE, 1)
    up = jnp.where(lane < SIDE, pltpu.roll(up, 1, 0), up)
    total += jnp.where(inside < SIDE, 0.0, up)
    down = pltpu.roll(x, LANES - SIDE, 1)
    down = jnp.where(lane >= LANES - SIDE, pltpu.roll(down, rows - 1, 0), down)
    total += jnp.where(inside >= plane - SIDE, 0.0, down)
    total += jnp.where(row < per, 0.0, pltpu.roll(x, per, 0))
    total += jnp.where(row >= rows - per, 0.0, pltpu.roll(x, rows - per, 0))
    return total - 6.0 * x


def finish_kernel(window, shells_any, columns, out_any, pressure_out, shells, out, walls_all, last, sems, out_sems):
    nodes, classes, cells = out.shape
    chunks = cells // LANES
    parts = nodes // GROUP

    def piece(g):
        return pl.ds(g * GROUP, GROUP)

    loads = [
        pltpu.make_async_copy(
            shells_any.at[:, pl.ds(g * GROUP * classes, GROUP * classes)],
            shells.at[:, pl.ds(g * GROUP * classes, GROUP * classes)],
            sems.at[g],
        )
        for g in range(parts)
    ]
    for load in loads:
        load.start()
    plane = pressure_out.shape[1]
    blocks = window.shape[0]
    rows = blocks * chunks

    def field_of(f):
        return window[:, f].reshape(rows, LANES)

    field = field_of(2 * SUBSTEPS)
    walls = []
    for t in range(SUBSTEPS):
        walls.append(0.5 * field)
        walls_all[t] = walls[t]
        gas = field_of(t)
        for s in range(t + 1):
            gas = gas + field_of(SUBSTEPS + t - s) * walls[s]
        chamber = 1.5 - 0.5 * jnp.sum(gas) / (rows * LANES)
        field = field + 0.15 * laplacian(field, plane) + 0.1 * gas + 0.2 * (chamber - field)
    last[...] = field
    cell = lax.axis_index("cell")
    first = cell * chunks
    tile = pressure_out.shape[0] * plane // LANES
    per = plane // LANES
    at = first + lax.axis_index("cls") * tile
    for i in range(tile):
        pressure_out[i // per : i // per + 1, (i % per) * LANES : (i % per + 1) * LANES] = last[
            pl.ds(at + i, 1), :
        ]
    walls_here = [
        [
            jnp.broadcast_to(walls_all[s, pl.ds(first + r, 1), :], (classes, LANES))
            for r in range(chunks)
        ]
        for s in range(SUBSTEPS)
    ]
    stores = [
        pltpu.make_async_copy(out.at[piece(g)], out_any.at[piece(g)], out_sems.at[g]) for g in range(parts)
    ]
    cols = [columns[SUBSTEPS - 1 - s] for s in range(SUBSTEPS)]
    for g in range(parts):
        loads[g].wait()
        for i in range(g * GROUP, (g + 1) * GROUP):
            weights = [jnp.broadcast_to(cols[s][:, i : i + 1], (classes, LANES)) for s in range(SUBSTEPS)]
            for r in range(chunks):
                value = shells[r, i * classes : (i + 1) * classes, :]
                for s in range(SUBSTEPS):
                    value = value + weights[s] * walls_here[s][r]
                out[i, :, r * LANES : (r + 1) * LANES] = value
        stores[g].start()
    for store in stores:
        store.wait()


ANY = pl.BlockSpec(memory_space=pl.ANY)
VMEM = pl.BlockSpec(memory_space=pltpu.VMEM)
DMA = pltpu.SemaphoreType.DMA


def exchange(copies, axis):
    return lax.all_to_all(copies, axis, split_axis=0, concat_axis=0, tiled=True)


def shards(melt, counts, pressure, propagator, coupling, flux_weights):
    nodes, classes, cells = melt.shape
    chunks = cells // LANES
    f32 = jnp.float32
    split = (chunks, nodes * classes, LANES)
    params = pltpu.CompilerParams(vmem_limit_bytes=32 * 2**20)
    cls_count = lax.axis_size("cls")
    cell_count = lax.axis_size("cell")
    prop_v = pltpu.VMEM((classes, nodes, nodes), f32)
    small = pltpu.VMEM((classes, nodes), f32)
    parts = nodes // GROUP
    packed = pl.pallas_call(
        functools.partial(fields_kernel, cls_count),
        out_shape=jax.ShapeDtypeStruct((cls_count, FIELDS, chunks, LANES), f32),
        in_specs=[ANY, VMEM, VMEM, ANY, ANY, ANY],
        out_specs=VMEM,
        scratch_shapes=[pltpu.VMEM(melt.shape, f32), prop_v, small, small, DMA((parts,)), DMA((3,))],
        compiler_params=params,
        name="fields",
    )(melt, counts, pressure, propagator, coupling, flux_weights)
    shells, columns = pl.pallas_call(
        power_kernel,
        out_shape=[
            jax.ShapeDtypeStruct(split, f32),
            jax.ShapeDtypeStruct((SUBSTEPS, classes, nodes), f32),
        ],
        in_specs=[ANY, ANY, ANY],
        out_specs=[VMEM, VMEM],
        scratch_shapes=[pltpu.VMEM(split, f32), prop_v, small, DMA((chunks,)), DMA((2,))],
        compiler_params=params,
        name="power",
    )(melt.reshape(nodes * classes, cells), propagator, coupling)
    packed = jnp.sum(exchange(packed, "cls"), axis=0)
    window = exchange(jnp.broadcast_to(packed[None], (cell_count,) + packed.shape), "cell")
    rows = cell_count * chunks
    return pl.pallas_call(
        finish_kernel,
        out_shape=[jax.ShapeDtypeStruct(melt.shape, f32), jax.ShapeDtypeStruct(pressure.shape, f32)],
        in_specs=[VMEM, ANY, VMEM],
        out_specs=[ANY, VMEM],
        scratch_shapes=[
            pltpu.VMEM(split, f32),
            pltpu.VMEM(melt.shape, f32),
            pltpu.VMEM((SUBSTEPS, rows, LANES), f32),
            pltpu.VMEM((rows, LANES), f32),
            DMA((parts,)),
            DMA((parts,)),
        ],
        compiler_params=params,
        name="finish",
    )(window, shells, columns)


def solution(mesh):
    placed = (P(None, "cls", "cell"), P("cls", "cell"), P(("cell", "cls"), None), P(), P(), P())
    return jax.shard_map(
        shards,
        mesh=mesh,
        in_specs=placed,
        out_specs=(P(None, "cls", "cell"), P(("cell", "cls"), None)),
        check_vma=False,
    )
```

```python
import functools

import jax
import jax.numpy as jnp
from jax import lax
from jax.experimental import pallas as pl
from jax.experimental.pallas import tpu as pltpu
from jax.sharding import PartitionSpec as P

CLASSES = 32
SIDE = 16
SUBSTEPS = 4
COUNT_SCALE = 400.0
LANES = 128
GROUP = 8
FIELDS = 2 * SUBSTEPS + 1

HIGHEST = lax.Precision.HIGHEST


def grow(value, factor, times):
    for _ in range(times):
        value = value * factor
    return value


def iota(shape, dim):
    return lax.broadcasted_iota(jnp.int32, shape, dim)


def split3(x):
    high = x.astype(jnp.bfloat16)
    rest = x - high.astype(jnp.float32)
    middle = rest.astype(jnp.bfloat16)
    low = (rest - middle.astype(jnp.float32)).astype(jnp.bfloat16)
    return high, middle, low


def split2(x):
    high = x.astype(jnp.bfloat16)
    return high, (x - high.astype(jnp.float32)).astype(jnp.bfloat16)


def dot(a, b):
    return jnp.dot(a, b, preferred_element_type=jnp.float32)


def square(a):
    high, middle, low = split3(a)
    left = jnp.concatenate([high, high, middle, high, low, middle], axis=1)
    right = jnp.concatenate([high, middle, high, low, high, middle], axis=0)
    return dot(left, right)


def class_scale(prop):
    rows = [jnp.max(jnp.abs(prop[k]), axis=0, keepdims=True) for k in range(prop.shape[0])]
    return jnp.maximum(1.0, jnp.max(jnp.concatenate(rows, axis=0), axis=1, keepdims=True))


def param_copies(pairs, sems):
    copies = []
    for n, (source, target) in enumerate(pairs):
        own = pl.ds(lax.axis_index("cls") * target.shape[0], target.shape[0])
        copies.append(pltpu.make_async_copy(source.at[own], target, sems.at[n]))
    return copies


def fields_kernel(
    melt_hbm, counts_hbm, pressure_hbm, prop_hbm, coup_hbm, flux_hbm, out, melt, counts, pressure, prop, coup, flux, sems, other_sems
):
    nodes, classes, cells = melt.shape
    first = param_copies([(prop_hbm, prop), (flux_hbm, flux), (coup_hbm, coup)], other_sems)
    for copy in first:
        copy.start()
    parts = nodes // GROUP
    pieces = [
        pltpu.make_async_copy(
            melt_hbm.at[pl.ds(g * GROUP, GROUP)], melt.at[pl.ds(g * GROUP, GROUP)], sems.at[g]
        )
        for g in range(parts)
    ]
    for piece in pieces:
        piece.start()
    rest = [
        pltpu.make_async_copy(counts_hbm, counts, other_sems.at[3]),
        pltpu.make_async_copy(pressure_hbm, pressure, other_sems.at[4]),
    ]
    for copy in rest:
        copy.start()
    for copy in first:
        copy.wait()
    scale = class_scale(prop)
    width = classes * nodes
    table = jnp.concatenate(split3(prop[...].reshape(width, nodes)), axis=1)
    mask = iota((classes, width), 1) // nodes == iota((classes, width), 0)
    rows = [flux[...]]
    for _ in range(SUBSTEPS):
        wide = jnp.where(mask, jnp.concatenate([rows[-1]] * classes, axis=1), 0.0)
        pairs = dot(jnp.concatenate(split3(wide), axis=0), table)
        row = pairs[:classes] + pairs[classes : 2 * classes] + pairs[2 * classes :]
        rows.append((row[:, :nodes] + row[:, nodes : 2 * nodes] + row[:, 2 * nodes :]) / scale)
    spread = [
        grow(jnp.sum(rows[d] * coup[...], axis=1, keepdims=True), scale, d) for d in range(SUBSTEPS)
    ]
    for copy in rest:
        copy.wait()
    counts_n = counts[...].astype(jnp.float32) / (COUNT_SCALE * CLASSES)
    chunks = cells // LANES
    sums = [[jnp.zeros((classes, LANES), jnp.float32) for _ in range(chunks)] for _ in range(SUBSTEPS)]
    for g in range(parts):
        pieces[g].wait()
        for j in range(g * GROUP, (g + 1) * GROUP):
            weights = [
                jnp.broadcast_to(rows[t + 1][:, j : j + 1], (classes, LANES)) for t in range(SUBSTEPS)
            ]
            for r in range(chunks):
                value = melt[j, :, r * LANES : (r + 1) * LANES]
                for t in range(SUBSTEPS):
                    sums[t][r] = sums[t][r] + weights[t] * value
    out[2 * SUBSTEPS] = jnp.zeros((chunks, LANES), jnp.float32)
    for r in range(chunks):
        here = counts_n[:, r * LANES : (r + 1) * LANES]
        for t in range(SUBSTEPS):
            out[t, r : r + 1, :] = jnp.sum(grow(here * sums[t][r], scale, t + 1), axis=0, keepdims=True)
        for d in range(SUBSTEPS):
            out[SUBSTEPS + d, r : r + 1, :] = jnp.sum(here * spread[d], axis=0, keepdims=True)
    per = pressure.shape[1] // LANES
    tile = pressure.shape[0] * per
    at = lax.axis_index("cls") * tile
    for i in range(tile):
        out[2 * SUBSTEPS, pl.ds(at + i, 1), :] = pressure[
            i // per : i // per + 1, (i % per) * LANES : (i % per + 1) * LANES
        ]


def power_kernel(melt_hbm, prop_hbm, coup_hbm, out_hbm, columns, melt, out, prop, coup, sems, out_sems, param_sems):
    chunks = out.shape[0]
    classes, nodes = prop.shape[:2]
    params = param_copies([(prop_hbm, prop), (coup_hbm, coup)], param_sems)
    for copy in params:
        copy.start()
    loads = [
        pltpu.make_async_copy(melt_hbm.at[:, pl.ds(r * LANES, LANES)], melt.at[r], sems.at[r])
        for r in range(chunks)
    ]
    stores = [pltpu.make_async_copy(out.at[r], out_hbm.at[r], out_sems.at[r]) for r in range(chunks)]
    for load in loads:
        load.start()
    for copy in params:
        copy.wait()
    scale = class_scale(prop)
    unit = [prop[k] / scale[k : k + 1, :] for k in range(classes)]
    table = jnp.concatenate(unit, axis=0)
    column = coup[...]
    columns[0] = column
    for d in range(1, SUBSTEPS):
        pairs = lax.dot_general(
            column, table, (((1,), (1,)), ((), ())), precision=HIGHEST, preferred_element_type=jnp.float32
        )
        column = jnp.concatenate(
            [pairs[k : k + 1, k * nodes : (k + 1) * nodes] for k in range(classes)], axis=0
        )
        columns[d] = grow(column, scale, d)
    lefts = []
    for k in range(classes):
        high, low = split2(square(square(unit[k])))
        lefts.append(jnp.concatenate([high, high, low], axis=1))
    together = 2 if chunks % 2 == 0 else 1
    for r in range(0, chunks, together):
        for n in range(together):
            loads[r + n].wait()
        for k in range(classes):
            own = pl.ds(k, nodes, stride=classes)
            high, low = split2(jnp.concatenate([melt[r + n, own, :] for n in range(together)], axis=1))
            part = dot(lefts[k], jnp.concatenate([high, low, high], axis=0))
            part = grow(part, scale[k : k + 1, :], SUBSTEPS)
            for n in range(together):
                out[r + n, own, :] = part[:, n * LANES : (n + 1) * LANES]
        for n in range(together):
            stores[r + n].start()
    for store in stores:
        store.wait()


def combine_kernel(mine, theirs, out):
    total = mine[...] + theirs[...]
    wall = 0.5 * total[2 * SUBSTEPS]
    for n in range(out.shape[0]):
        for t in range(SUBSTEPS):
            out[n, t] = total[t] + total[SUBSTEPS + t] * wall
        for d in range(SUBSTEPS - 1):
            out[n, SUBSTEPS + d] = total[SUBSTEPS + d]
        out[n, 2 * SUBSTEPS - 1] = total[2 * SUBSTEPS]


def laplacian(x, plane):
    rows = x.shape[0]
    row = iota(x.shape, 0)
    lane = iota(x.shape, 1)
    per = plane // LANES
    inside = row % per * LANES + lane
    col = lane % SIDE
    total = jnp.where(col == 0, 0.0, pltpu.roll(x, 1, 1))
    total += jnp.where(col == SIDE - 1, 0.0, pltpu.roll(x, LANES - 1, 1))
    up = pltpu.roll(x, SIDE, 1)
    up = jnp.where(lane < SIDE, pltpu.roll(up, 1, 0), up)
    total += jnp.where(inside < SIDE, 0.0, up)
    down = pltpu.roll(x, LANES - SIDE, 1)
    down = jnp.where(lane >= LANES - SIDE, pltpu.roll(down, rows - 1, 0), down)
    total += jnp.where(inside >= plane - SIDE, 0.0, down)
    total += jnp.where(row < per, 0.0, pltpu.roll(x, per, 0))
    total += jnp.where(row >= rows - per, 0.0, pltpu.roll(x, rows - per, 0))
    return total - 6.0 * x


def finish_kernel(window, shells_hbm, columns, out_hbm, pressure_out, shells, out, walls_all, last, sems, out_sems):
    nodes, classes, cells = out.shape
    chunks = cells // LANES
    parts = nodes // GROUP

    def piece(g):
        return pl.ds(g * GROUP, GROUP)

    loads = [
        pltpu.make_async_copy(
            shells_hbm.at[:, pl.ds(g * GROUP * classes, GROUP * classes)],
            shells.at[:, pl.ds(g * GROUP * classes, GROUP * classes)],
            sems.at[g],
        )
        for g in range(parts)
    ]
    for load in loads:
        load.start()
    plane = pressure_out.shape[1]
    blocks = window.shape[0]
    rows = blocks * chunks

    def field_of(f):
        return window[:, f].reshape(rows, LANES)

    field = field_of(2 * SUBSTEPS - 1)
    walls = []
    for t in range(SUBSTEPS):
        walls.append(0.5 * field)
        walls_all[t] = walls[t]
        gas = field_of(t)
        for s in range(1, t + 1):
            gas = gas + field_of(SUBSTEPS + t - s) * walls[s]
        chamber = 1.5 - 0.5 * jnp.sum(gas) / (rows * LANES)
        field = field + 0.15 * laplacian(field, plane) + 0.1 * gas + 0.2 * (chamber - field)
    last[...] = field
    cell = lax.axis_index("cell")
    first = cell * chunks
    tile = pressure_out.shape[0] * plane // LANES
    per = plane // LANES
    at = first + lax.axis_index("cls") * tile
    for i in range(tile):
        pressure_out[i // per : i // per + 1, (i % per) * LANES : (i % per + 1) * LANES] = last[
            pl.ds(at + i, 1), :
        ]
    walls_here = [
        [
            jnp.broadcast_to(walls_all[s, pl.ds(first + r, 1), :], (classes, LANES))
            for r in range(chunks)
        ]
        for s in range(SUBSTEPS)
    ]
    stores = [
        pltpu.make_async_copy(out.at[piece(g)], out_hbm.at[piece(g)], out_sems.at[g]) for g in range(parts)
    ]
    cols = [columns[SUBSTEPS - 1 - s] for s in range(SUBSTEPS)]
    for g in range(parts):
        loads[g].wait()
        for i in range(g * GROUP, (g + 1) * GROUP):
            weights = [jnp.broadcast_to(cols[s][:, i : i + 1], (classes, LANES)) for s in range(SUBSTEPS)]
            for r in range(chunks):
                value = shells[r, i * classes : (i + 1) * classes, :]
                for s in range(SUBSTEPS):
                    value = value + weights[s] * walls_here[s][r]
                out[i, :, r * LANES : (r + 1) * LANES] = value
        stores[g].start()
    for store in stores:
        store.wait()


HBM = pl.BlockSpec(memory_space=pltpu.HBM)
VMEM = pl.BlockSpec(memory_space=pltpu.VMEM)
DMA = pltpu.SemaphoreType.DMA


def partner(value, axis, distance):
    count = lax.axis_size(axis)
    return lax.ppermute(value, axis, [(i, i ^ distance) for i in range(count)])


def shards(melt, counts, pressure, propagator, coupling, flux_weights):
    nodes, classes, cells = melt.shape
    chunks = cells // LANES
    f32 = jnp.float32
    split = (chunks, nodes * classes, LANES)
    params = pltpu.CompilerParams(vmem_limit_bytes=32 * 2**20)
    cls_count = lax.axis_size("cls")
    cell_count = lax.axis_size("cell")
    prop_v = pltpu.VMEM((classes, nodes, nodes), f32)
    small = pltpu.VMEM((classes, nodes), f32)
    parts = nodes // GROUP
    packed = pl.pallas_call(
        fields_kernel,
        out_shape=jax.ShapeDtypeStruct((FIELDS, chunks, LANES), f32),
        in_specs=[HBM] * 6,
        out_specs=VMEM,
        scratch_shapes=[
            pltpu.VMEM(melt.shape, f32),
            pltpu.VMEM(counts.shape, counts.dtype),
            pltpu.VMEM(pressure.shape, f32),
            prop_v,
            small,
            small,
            DMA((parts,)),
            DMA((5,)),
        ],
        compiler_params=params,
        name="fields",
    )(melt, counts, pressure, propagator, coupling, flux_weights)
    shells, columns = pl.pallas_call(
        power_kernel,
        out_shape=[
            jax.ShapeDtypeStruct(split, f32),
            jax.ShapeDtypeStruct((SUBSTEPS, classes, nodes), f32),
        ],
        in_specs=[HBM] * 3,
        out_specs=[HBM, VMEM],
        scratch_shapes=[
            pltpu.VMEM(split, f32),
            pltpu.VMEM(split, f32),
            prop_v,
            small,
            DMA((chunks,)),
            DMA((chunks,)),
            DMA((2,)),
        ],
        compiler_params=params,
        cost_estimate=pl.CostEstimate(flops=2 * 10**9, bytes_accessed=2 * melt.size * 4, transcendentals=0),
        name="power",
    )(melt.reshape(nodes * classes, cells), propagator, coupling)
    distance = 1
    theirs = partner(packed, "cls", distance)
    while 2 * distance < cls_count:
        distance *= 2
        packed = packed + theirs
        theirs = partner(packed, "cls", distance)
    copies = pl.pallas_call(
        combine_kernel,
        out_shape=jax.ShapeDtypeStruct((cell_count, FIELDS - 1, chunks, LANES), f32),
        in_specs=[VMEM, VMEM],
        out_specs=VMEM,
        compiler_params=params,
        name="combine",
    )(packed, theirs)
    window = lax.all_to_all(copies, "cell", split_axis=0, concat_axis=0, tiled=True)
    rows = cell_count * chunks
    return pl.pallas_call(
        finish_kernel,
        out_shape=[jax.ShapeDtypeStruct(melt.shape, f32), jax.ShapeDtypeStruct(pressure.shape, f32)],
        in_specs=[VMEM, HBM, VMEM],
        out_specs=[HBM, VMEM],
        scratch_shapes=[
            pltpu.VMEM(split, f32),
            pltpu.VMEM(melt.shape, f32),
            pltpu.VMEM((SUBSTEPS, rows, LANES), f32),
            pltpu.VMEM((rows, LANES), f32),
            DMA((parts,)),
            DMA((parts,)),
        ],
        compiler_params=params,
        name="finish",
    )(window, shells, columns)


def solution(mesh):
    placed = (P(None, "cls", "cell"), P("cls", "cell"), P(("cell", "cls"), None), P(), P(), P())
    return jax.shard_map(
        shards,
        mesh=mesh,
        in_specs=placed,
        out_specs=(P(None, "cls", "cell"), P(("cell", "cls"), None)),
        check_vma=False,
    )
```

```python
import functools

import jax
import jax.numpy as jnp
from jax import lax
from jax.experimental import pallas as pl
from jax.experimental.pallas import tpu as pltpu
from jax.sharding import PartitionSpec as P

CLASSES = 32
SIDE = 16
SUBSTEPS = 4
COUNT_SCALE = 400.0
LANES = 128
GROUP = 8
FIELDS = 2 * SUBSTEPS + 1

HIGHEST = lax.Precision.HIGHEST


def grow(value, factor, times):
    for _ in range(times):
        value = value * factor
    return value


def iota(shape, dim):
    return lax.broadcasted_iota(jnp.int32, shape, dim)


def split3(x):
    high = x.astype(jnp.bfloat16)
    rest = x - high.astype(jnp.float32)
    middle = rest.astype(jnp.bfloat16)
    low = (rest - middle.astype(jnp.float32)).astype(jnp.bfloat16)
    return high, middle, low


def split2(x):
    high = x.astype(jnp.bfloat16)
    return high, (x - high.astype(jnp.float32)).astype(jnp.bfloat16)


def dot(a, b):
    return jnp.dot(a, b, preferred_element_type=jnp.float32)


def square(a):
    high, middle, low = split3(a)
    left = jnp.concatenate([high, high, middle, high, low, middle], axis=1)
    right = jnp.concatenate([high, middle, high, low, high, middle], axis=0)
    return dot(left, right)


def class_scale(prop):
    rows = [jnp.max(jnp.abs(prop[k]), axis=0, keepdims=True) for k in range(prop.shape[0])]
    return jnp.maximum(1.0, jnp.max(jnp.concatenate(rows, axis=0), axis=1, keepdims=True))


def param_copies(pairs, sems):
    copies = []
    for n, (source, target) in enumerate(pairs):
        own = pl.ds(lax.axis_index("cls") * target.shape[0], target.shape[0])
        copies.append(pltpu.make_async_copy(source.at[own], target, sems.at[n]))
    return copies


def fields_kernel(
    melt_hbm, counts_hbm, pressure_hbm, prop_hbm, coup_hbm, flux_hbm, out, melt, counts, pressure, prop, coup, flux, sems, other_sems
):
    nodes, classes, cells = melt.shape
    first = param_copies([(prop_hbm, prop), (flux_hbm, flux), (coup_hbm, coup)], other_sems)
    for copy in first:
        copy.start()
    parts = nodes // GROUP
    pieces = [
        pltpu.make_async_copy(
            melt_hbm.at[pl.ds(g * GROUP, GROUP)], melt.at[pl.ds(g * GROUP, GROUP)], sems.at[g]
        )
        for g in range(parts)
    ]
    for piece in pieces:
        piece.start()
    rest = [
        pltpu.make_async_copy(counts_hbm, counts, other_sems.at[3]),
        pltpu.make_async_copy(pressure_hbm, pressure, other_sems.at[4]),
    ]
    for copy in rest:
        copy.start()
    for copy in first:
        copy.wait()
    scale = class_scale(prop)
    width = classes * nodes
    table = jnp.concatenate(split3(prop[...].reshape(width, nodes)), axis=1)
    mask = iota((classes, width), 1) // nodes == iota((classes, width), 0)
    rows = [flux[...]]
    for _ in range(SUBSTEPS):
        wide = jnp.where(mask, jnp.concatenate([rows[-1]] * classes, axis=1), 0.0)
        pairs = dot(jnp.concatenate(split3(wide), axis=0), table)
        row = pairs[:classes] + pairs[classes : 2 * classes] + pairs[2 * classes :]
        rows.append((row[:, :nodes] + row[:, nodes : 2 * nodes] + row[:, 2 * nodes :]) / scale)
    spread = [
        grow(jnp.sum(rows[d] * coup[...], axis=1, keepdims=True), scale, d) for d in range(SUBSTEPS)
    ]
    for copy in rest:
        copy.wait()
    counts_n = counts[...].astype(jnp.float32) / (COUNT_SCALE * CLASSES)
    chunks = cells // LANES
    sums = [[jnp.zeros((classes, LANES), jnp.float32) for _ in range(chunks)] for _ in range(SUBSTEPS)]
    for g in range(parts):
        pieces[g].wait()
        for j in range(g * GROUP, (g + 1) * GROUP):
            weights = [
                jnp.broadcast_to(rows[t + 1][:, j : j + 1], (classes, LANES)) for t in range(SUBSTEPS)
            ]
            for r in range(chunks):
                value = melt[j, :, r * LANES : (r + 1) * LANES]
                for t in range(SUBSTEPS):
                    sums[t][r] = sums[t][r] + weights[t] * value
    every = range(out.shape[0])
    for n in every:
        out[n, 2 * SUBSTEPS] = jnp.zeros((chunks, LANES), jnp.float32)
    for r in range(chunks):
        here = counts_n[:, r * LANES : (r + 1) * LANES]
        for t in range(SUBSTEPS):
            row = jnp.sum(grow(here * sums[t][r], scale, t + 1), axis=0, keepdims=True)
            for n in every:
                out[n, t, r : r + 1, :] = row
        for d in range(SUBSTEPS):
            row = jnp.sum(here * spread[d], axis=0, keepdims=True)
            for n in every:
                out[n, SUBSTEPS + d, r : r + 1, :] = row
    per = pressure.shape[1] // LANES
    tile = pressure.shape[0] * per
    at = lax.axis_index("cls") * tile
    for i in range(tile):
        row = pressure[i // per : i // per + 1, (i % per) * LANES : (i % per + 1) * LANES]
        for n in every:
            out[n, 2 * SUBSTEPS, pl.ds(at + i, 1), :] = row


def power_kernel(melt_hbm, prop_hbm, coup_hbm, out_hbm, melt, out, columns, prop, coup, sems, out_sems, param_sems):
    chunks = out.shape[0]
    classes, nodes = prop.shape[:2]
    params = param_copies([(prop_hbm, prop), (coup_hbm, coup)], param_sems)
    for copy in params:
        copy.start()
    loads = [
        pltpu.make_async_copy(melt_hbm.at[:, pl.ds(r * LANES, LANES)], melt.at[r], sems.at[r])
        for r in range(chunks)
    ]
    width = classes * nodes
    stores = [
        pltpu.make_async_copy(out.at[r], out_hbm.at[pl.ds(r * width, width)], out_sems.at[r])
        for r in range(chunks)
    ]
    stores.append(
        pltpu.make_async_copy(
            columns, out_hbm.at[pl.ds(chunks * width, columns.shape[0])], out_sems.at[chunks]
        )
    )
    for load in loads:
        load.start()
    for copy in params:
        copy.wait()
    scale = class_scale(prop)
    unit = [prop[k] / scale[k : k + 1, :] for k in range(classes)]
    table = jnp.concatenate(unit, axis=0)
    column = coup[...]
    columns[:, nodes:] = jnp.zeros((columns.shape[0], LANES - nodes), jnp.float32)
    columns[:classes, :nodes] = column
    for d in range(1, SUBSTEPS):
        pairs = lax.dot_general(
            column, table, (((1,), (1,)), ((), ())), precision=HIGHEST, preferred_element_type=jnp.float32
        )
        column = jnp.concatenate(
            [pairs[k : k + 1, k * nodes : (k + 1) * nodes] for k in range(classes)], axis=0
        )
        columns[d * classes : (d + 1) * classes, :nodes] = grow(column, scale, d)
    stores[chunks].start()
    lefts = []
    for k in range(classes):
        high, low = split2(square(square(unit[k])))
        lefts.append(jnp.concatenate([high, high, low], axis=1))
    together = 2 if chunks % 2 == 0 else 1
    for r in range(0, chunks, together):
        for n in range(together):
            loads[r + n].wait()
        for k in range(classes):
            own = pl.ds(k, nodes, stride=classes)
            high, low = split2(jnp.concatenate([melt[r + n, own, :] for n in range(together)], axis=1))
            part = dot(lefts[k], jnp.concatenate([high, low, high], axis=0))
            part = grow(part, scale[k : k + 1, :], SUBSTEPS)
            for n in range(together):
                out[r + n, own, :] = part[:, n * LANES : (n + 1) * LANES]
        for n in range(together):
            stores[r + n].start()
    for store in stores:
        store.wait()


def combine_kernel(parts, _, out):
    total = parts[0]
    for n in range(1, parts.shape[0]):
        total = total + parts[n]
    wall = 0.5 * total[2 * SUBSTEPS]
    for n in range(out.shape[0]):
        for t in range(SUBSTEPS):
            out[n, t] = total[t] + total[SUBSTEPS + t] * wall
        for d in range(SUBSTEPS - 1):
            out[n, SUBSTEPS + d] = total[SUBSTEPS + d]
        out[n, 2 * SUBSTEPS - 1] = total[2 * SUBSTEPS]


def laplacian(x, plane):
    rows = x.shape[0]
    row = iota(x.shape, 0)
    lane = iota(x.shape, 1)
    per = plane // LANES
    inside = row % per * LANES + lane
    col = lane % SIDE
    total = jnp.where(col == 0, 0.0, pltpu.roll(x, 1, 1))
    total += jnp.where(col == SIDE - 1, 0.0, pltpu.roll(x, LANES - 1, 1))
    up = pltpu.roll(x, SIDE, 1)
    up = jnp.where(lane < SIDE, pltpu.roll(up, 1, 0), up)
    total += jnp.where(inside < SIDE, 0.0, up)
    down = pltpu.roll(x, LANES - SIDE, 1)
    down = jnp.where(lane >= LANES - SIDE, pltpu.roll(down, rows - 1, 0), down)
    total += jnp.where(inside >= plane - SIDE, 0.0, down)
    total += jnp.where(row < per, 0.0, pltpu.roll(x, per, 0))
    total += jnp.where(row >= rows - per, 0.0, pltpu.roll(x, rows - per, 0))
    return total - 6.0 * x


def finish_kernel(
    window, shells_hbm, out_hbm, pressure_out, shells, out, columns, walls_all, last, sems, out_sems, column_sem
):
    nodes, classes, cells = out.shape
    chunks = cells // LANES
    parts = nodes // GROUP

    def piece(g):
        return pl.ds(g * GROUP, GROUP)

    loads = [
        pltpu.make_async_copy(
            shells_hbm.at[pl.ds((r * nodes + g * GROUP) * classes, GROUP * classes)],
            shells.at[r, pl.ds(g * GROUP * classes, GROUP * classes)],
            sems.at[g, r],
        )
        for g in range(parts)
        for r in range(chunks)
    ]
    for load in loads:
        load.start()
    column_load = pltpu.make_async_copy(
        shells_hbm.at[pl.ds(chunks * nodes * classes, columns.shape[0])], columns, column_sem
    )
    column_load.start()
    plane = pressure_out.shape[1]
    blocks = window.shape[0]
    rows = blocks * chunks

    def field_of(f):
        return window[:, f].reshape(rows, LANES)

    field = field_of(2 * SUBSTEPS - 1)
    walls = []
    for t in range(SUBSTEPS):
        walls.append(0.5 * field)
        walls_all[t] = walls[t]
        gas = field_of(t)
        for s in range(1, t + 1):
            gas = gas + field_of(SUBSTEPS + t - s) * walls[s]
        chamber = 1.5 - 0.5 * jnp.sum(gas) / (rows * LANES)
        field = field + 0.15 * laplacian(field, plane) + 0.1 * gas + 0.2 * (chamber - field)
    last[...] = field
    cell = lax.axis_index("cell")
    first = cell * chunks
    tile = pressure_out.shape[0] * plane // LANES
    per = plane // LANES
    at = first + lax.axis_index("cls") * tile
    for i in range(tile):
        pressure_out[i // per : i // per + 1, (i % per) * LANES : (i % per + 1) * LANES] = last[
            pl.ds(at + i, 1), :
        ]
    walls_here = [
        [
            jnp.broadcast_to(walls_all[s, pl.ds(first + r, 1), :], (classes, LANES))
            for r in range(chunks)
        ]
        for s in range(SUBSTEPS)
    ]
    stores = [
        pltpu.make_async_copy(out.at[piece(g)], out_hbm.at[piece(g)], out_sems.at[g]) for g in range(parts)
    ]
    column_load.wait()
    cols = [
        columns[(SUBSTEPS - 1 - s) * classes : (SUBSTEPS - s) * classes, :] for s in range(SUBSTEPS)
    ]
    for g in range(parts):
        for load in loads[g * chunks : (g + 1) * chunks]:
            load.wait()
        for i in range(g * GROUP, (g + 1) * GROUP):
            weights = [jnp.broadcast_to(cols[s][:, i : i + 1], (classes, LANES)) for s in range(SUBSTEPS)]
            for r in range(chunks):
                value = shells[r, i * classes : (i + 1) * classes, :]
                for s in range(SUBSTEPS):
                    value = value + weights[s] * walls_here[s][r]
                out[i, :, r * LANES : (r + 1) * LANES] = value
        stores[g].start()
    for store in stores:
        store.wait()


HBM = pl.BlockSpec(memory_space=pltpu.HBM)
VMEM = pl.BlockSpec(memory_space=pltpu.VMEM)
DMA = pltpu.SemaphoreType.DMA


def exchange(copies, axis):
    return lax.all_to_all(copies, axis, split_axis=0, concat_axis=0, tiled=True)


def shards(melt, counts, pressure, propagator, coupling, flux_weights):
    nodes, classes, cells = melt.shape
    chunks = cells // LANES
    f32 = jnp.float32
    split = (chunks, nodes * classes, LANES)
    whole = pltpu.CompilerParams(vmem_limit_bytes=60 * 2**20)
    most = pltpu.CompilerParams(vmem_limit_bytes=52 * 2**20)
    cls_count = lax.axis_size("cls")
    cell_count = lax.axis_size("cell")
    prop_v = pltpu.VMEM((classes, nodes, nodes), f32)
    small = pltpu.VMEM((classes, nodes), f32)
    parts = nodes // GROUP
    packed = pl.pallas_call(
        fields_kernel,
        out_shape=jax.ShapeDtypeStruct((cls_count, FIELDS, chunks, LANES), f32),
        in_specs=[HBM] * 6,
        out_specs=VMEM,
        scratch_shapes=[
            pltpu.VMEM(melt.shape, f32),
            pltpu.VMEM(counts.shape, counts.dtype),
            pltpu.VMEM(pressure.shape, f32),
            prop_v,
            small,
            small,
            DMA((parts,)),
            DMA((5,)),
        ],
        compiler_params=whole,
        name="fields",
    )(melt, counts, pressure, propagator, coupling, flux_weights)
    columns_v = pltpu.VMEM((SUBSTEPS * classes, LANES), f32)
    shells = pl.pallas_call(
        power_kernel,
        out_shape=jax.ShapeDtypeStruct(((chunks * nodes + SUBSTEPS) * classes, LANES), f32),
        in_specs=[HBM] * 3,
        out_specs=HBM,
        scratch_shapes=[
            pltpu.VMEM(split, f32),
            pltpu.VMEM(split, f32),
            columns_v,
            prop_v,
            small,
            DMA((chunks,)),
            DMA((chunks + 1,)),
            DMA((2,)),
        ],
        compiler_params=whole,
        cost_estimate=pl.CostEstimate(flops=2 * 10**9, bytes_accessed=2 * melt.size * 4, transcendentals=0),
        name="power",
    )(melt.reshape(nodes * classes, cells), propagator, coupling)
    copies = pl.pallas_call(
        combine_kernel,
        out_shape=jax.ShapeDtypeStruct((cell_count, FIELDS - 1, chunks, LANES), f32),
        in_specs=[VMEM, HBM],
        out_specs=VMEM,
        compiler_params=most,
        name="combine",
    )(exchange(packed, "cls"), shells)
    window = exchange(copies, "cell")
    rows = cell_count * chunks
    return pl.pallas_call(
        finish_kernel,
        out_shape=[jax.ShapeDtypeStruct(melt.shape, f32), jax.ShapeDtypeStruct(pressure.shape, f32)],
        in_specs=[VMEM, HBM],
        out_specs=[HBM, VMEM],
        scratch_shapes=[
            pltpu.VMEM(split, f32),
            pltpu.VMEM(melt.shape, f32),
            columns_v,
            pltpu.VMEM((SUBSTEPS, rows, LANES), f32),
            pltpu.VMEM((rows, LANES), f32),
            DMA((parts, chunks)),
            DMA((parts,)),
            DMA(()),
        ],
        compiler_params=most,
        name="finish",
    )(window, shells)


def solution(mesh):
    placed = (P(None, "cls", "cell"), P("cls", "cell"), P(("cell", "cls"), None), P(), P(), P())
    return jax.shard_map(
        shards,
        mesh=mesh,
        in_specs=placed,
        out_specs=(P(None, "cls", "cell"), P(("cell", "cls"), None)),
        check_vma=False,
    )
```

```python
import functools

import jax
import jax.numpy as jnp
from jax import lax
from jax.experimental import pallas as pl
from jax.experimental.pallas import tpu as pltpu
from jax.sharding import PartitionSpec as P

CLASSES = 32
SIDE = 16
SUBSTEPS = 4
COUNT_SCALE = 400.0
LANES = 128
GROUP = 8
FIELDS = 2 * SUBSTEPS + 1

HIGHEST = lax.Precision.HIGHEST


def grow(value, factor, times):
    for _ in range(times):
        value = value * factor
    return value


def iota(shape, dim):
    return lax.broadcasted_iota(jnp.int32, shape, dim)


def split3(x):
    high = x.astype(jnp.bfloat16)
    rest = x - high.astype(jnp.float32)
    middle = rest.astype(jnp.bfloat16)
    low = (rest - middle.astype(jnp.float32)).astype(jnp.bfloat16)
    return high, middle, low


def split2(x):
    high = x.astype(jnp.bfloat16)
    return high, (x - high.astype(jnp.float32)).astype(jnp.bfloat16)


def dot(a, b):
    return jnp.dot(a, b, preferred_element_type=jnp.float32)


def square(a):
    high, middle, low = split3(a)
    left = jnp.concatenate([high, high, middle, high, low, middle], axis=1)
    right = jnp.concatenate([high, middle, high, low, high, middle], axis=0)
    return dot(left, right)


def class_scale(prop):
    rows = [jnp.max(jnp.abs(prop[k]), axis=0, keepdims=True) for k in range(prop.shape[0])]
    return jnp.maximum(1.0, jnp.max(jnp.concatenate(rows, axis=0), axis=1, keepdims=True))


def param_copies(pairs, sems):
    copies = []
    for n, (source, target) in enumerate(pairs):
        own = pl.ds(lax.axis_index("cls") * target.shape[0], target.shape[0])
        copies.append(pltpu.make_async_copy(source.at[own], target, sems.at[n]))
    return copies


def fields_kernel(
    melt_hbm, counts_hbm, pressure_hbm, prop_hbm, coup_hbm, flux_hbm, out, melt, counts, pressure, prop, coup, flux, sems, other_sems
):
    nodes, classes, cells = melt.shape
    first = param_copies([(prop_hbm, prop), (flux_hbm, flux), (coup_hbm, coup)], other_sems)
    for copy in first:
        copy.start()
    parts = nodes // GROUP
    pieces = [
        pltpu.make_async_copy(
            melt_hbm.at[pl.ds(g * GROUP, GROUP)], melt.at[pl.ds(g * GROUP, GROUP)], sems.at[g]
        )
        for g in range(parts)
    ]
    for piece in pieces:
        piece.start()
    rest = [
        pltpu.make_async_copy(counts_hbm, counts, other_sems.at[3]),
        pltpu.make_async_copy(pressure_hbm, pressure, other_sems.at[4]),
    ]
    for copy in rest:
        copy.start()
    for copy in first:
        copy.wait()
    scale = class_scale(prop)
    width = classes * nodes
    table = jnp.concatenate(split3(prop[...].reshape(width, nodes)), axis=1)
    mask = iota((classes, width), 1) // nodes == iota((classes, width), 0)
    rows = [flux[...]]
    for _ in range(SUBSTEPS):
        wide = jnp.where(mask, jnp.concatenate([rows[-1]] * classes, axis=1), 0.0)
        pairs = dot(jnp.concatenate(split3(wide), axis=0), table)
        row = pairs[:classes] + pairs[classes : 2 * classes] + pairs[2 * classes :]
        rows.append((row[:, :nodes] + row[:, nodes : 2 * nodes] + row[:, 2 * nodes :]) / scale)
    spread = [
        grow(jnp.sum(rows[d] * coup[...], axis=1, keepdims=True), scale, d) for d in range(SUBSTEPS)
    ]
    for copy in rest:
        copy.wait()
    counts_n = counts[...].astype(jnp.float32) / (COUNT_SCALE * CLASSES)
    chunks = cells // LANES
    sums = [[jnp.zeros((classes, LANES), jnp.float32) for _ in range(chunks)] for _ in range(SUBSTEPS)]
    for g in range(parts):
        pieces[g].wait()
        for j in range(g * GROUP, (g + 1) * GROUP):
            weights = [
                jnp.broadcast_to(rows[t + 1][:, j : j + 1], (classes, LANES)) for t in range(SUBSTEPS)
            ]
            for r in range(chunks):
                value = melt[j, :, r * LANES : (r + 1) * LANES]
                for t in range(SUBSTEPS):
                    sums[t][r] = sums[t][r] + weights[t] * value
    every = range(out.shape[0])
    for n in every:
        out[n, 2 * SUBSTEPS] = jnp.zeros((chunks, LANES), jnp.float32)
    for r in range(chunks):
        here = counts_n[:, r * LANES : (r + 1) * LANES]
        for t in range(SUBSTEPS):
            row = jnp.sum(grow(here * sums[t][r], scale, t + 1), axis=0, keepdims=True)
            for n in every:
                out[n, t, r : r + 1, :] = row
        for d in range(SUBSTEPS):
            row = jnp.sum(here * spread[d], axis=0, keepdims=True)
            for n in every:
                out[n, SUBSTEPS + d, r : r + 1, :] = row
    per = pressure.shape[1] // LANES
    tile = pressure.shape[0] * per
    at = lax.axis_index("cls") * tile
    for i in range(tile):
        row = pressure[i // per : i // per + 1, (i % per) * LANES : (i % per + 1) * LANES]
        for n in every:
            out[n, 2 * SUBSTEPS, pl.ds(at + i, 1), :] = row


def apply_power(lefts, scale, melt, out, loads, stores):
    chunks = out.shape[0]
    classes = scale.shape[0]
    nodes = out.shape[1] // classes
    together = 2 if chunks % 2 == 0 else 1
    for r in range(0, chunks, together):
        for n in range(together):
            loads[r + n].wait()
        for k in range(classes):
            own = pl.ds(k, nodes, stride=classes)
            high, low = split2(jnp.concatenate([melt[r + n, own, :] for n in range(together)], axis=1))
            part = dot(lefts[k], jnp.concatenate([high, low, high], axis=0))
            part = grow(part, scale[k : k + 1, :1], SUBSTEPS)
            for n in range(together):
                out[r + n, own, :] = part[:, n * LANES : (n + 1) * LANES]
        for n in range(together):
            stores[r + n].start()
    for store in stores:
        store.wait()


def chunk_copies(first, melt_hbm, shells_hbm, melt, out, sems, out_sems):
    chunks, width = out.shape[:2]
    loads = [
        pltpu.make_async_copy(
            melt_hbm.at[:, pl.ds((first + r) * LANES, LANES)], melt.at[r], sems.at[r]
        )
        for r in range(chunks)
    ]
    stores = [
        pltpu.make_async_copy(
            out.at[r], shells_hbm.at[first + r, pl.ds(0, width)], out_sems.at[r]
        )
        for r in range(chunks)
    ]
    return loads, stores


def power_kernel(
    melt_hbm, prop_hbm, coup_hbm, shells_hbm, lefts_hbm, melt, out, extra, lefts, prop, coup, sems, out_sems, other_sems
):
    classes, nodes = prop.shape[:2]
    params = param_copies([(prop_hbm, prop), (coup_hbm, coup)], other_sems)
    for copy in params:
        copy.start()
    loads, stores = chunk_copies(0, melt_hbm, shells_hbm, melt, out, sems, out_sems)
    for load in loads:
        load.start()
    extra_store = pltpu.make_async_copy(
        extra, shells_hbm.at[0, pl.ds(classes * nodes, extra.shape[0])], other_sems.at[2]
    )
    lefts_store = pltpu.make_async_copy(lefts, lefts_hbm, other_sems.at[3])
    for copy in params:
        copy.wait()
    scale = class_scale(prop)
    unit = [prop[k] / scale[k : k + 1, :] for k in range(classes)]
    for k in range(classes):
        high, low = split2(square(square(unit[k])))
        lefts[k] = jnp.concatenate([high, high, low], axis=1)
    lefts_store.start()
    table = jnp.concatenate(unit, axis=0)
    column = coup[...]
    extra[:, nodes:] = jnp.zeros((extra.shape[0], LANES - nodes), jnp.float32)
    extra[:classes, :nodes] = column
    for d in range(1, SUBSTEPS):
        pairs = lax.dot_general(
            column, table, (((1,), (1,)), ((), ())), precision=HIGHEST, preferred_element_type=jnp.float32
        )
        column = jnp.concatenate(
            [pairs[k : k + 1, k * nodes : (k + 1) * nodes] for k in range(classes)], axis=0
        )
        extra[d * classes : (d + 1) * classes, :nodes] = grow(column, scale, d)
    extra[SUBSTEPS * classes :, :] = jnp.broadcast_to(scale, (classes, LANES))
    extra_store.start()
    apply_power(lefts, scale, melt, out, loads, stores)
    extra_store.wait()
    lefts_store.wait()


def rest_kernel(first, melt_hbm, lefts_hbm, shells_in, _, shells_hbm, melt, out, scale, lefts, sems, out_sems, other_sems):
    classes, nodes = lefts.shape[:2]
    params = [
        pltpu.make_async_copy(lefts_hbm, lefts, other_sems.at[0]),
        pltpu.make_async_copy(
            shells_in.at[0, pl.ds((nodes + SUBSTEPS) * classes, classes)], scale, other_sems.at[1]
        ),
    ]
    loads, stores = chunk_copies(first, melt_hbm, shells_hbm, melt, out, sems, out_sems)
    for copy in params + loads:
        copy.start()
    for copy in params:
        copy.wait()
    apply_power(lefts, scale, melt, out, loads, stores)


def combine_kernel(parts, _, out):
    total = parts[0]
    for n in range(1, parts.shape[0]):
        total = total + parts[n]
    wall = 0.5 * total[2 * SUBSTEPS]
    for n in range(out.shape[0]):
        for t in range(SUBSTEPS):
            out[n, t] = total[t] + total[SUBSTEPS + t] * wall
        for d in range(SUBSTEPS - 1):
            out[n, SUBSTEPS + d] = total[SUBSTEPS + d]
        out[n, 2 * SUBSTEPS - 1] = total[2 * SUBSTEPS]


def laplacian(x, plane):
    rows = x.shape[0]
    row = iota(x.shape, 0)
    lane = iota(x.shape, 1)
    per = plane // LANES
    inside = row % per * LANES + lane
    col = lane % SIDE
    total = jnp.where(col == 0, 0.0, pltpu.roll(x, 1, 1))
    total += jnp.where(col == SIDE - 1, 0.0, pltpu.roll(x, LANES - 1, 1))
    up = pltpu.roll(x, SIDE, 1)
    up = jnp.where(lane < SIDE, pltpu.roll(up, 1, 0), up)
    total += jnp.where(inside < SIDE, 0.0, up)
    down = pltpu.roll(x, LANES - SIDE, 1)
    down = jnp.where(lane >= LANES - SIDE, pltpu.roll(down, rows - 1, 0), down)
    total += jnp.where(inside >= plane - SIDE, 0.0, down)
    total += jnp.where(row < per, 0.0, pltpu.roll(x, per, 0))
    total += jnp.where(row >= rows - per, 0.0, pltpu.roll(x, rows - per, 0))
    return total - 6.0 * x


def finish_kernel(
    window, shells_hbm, out_hbm, pressure_out, shells, out, columns, walls_all, last, sems, out_sems, column_sem
):
    nodes, classes, cells = out.shape
    chunks = cells // LANES
    parts = nodes // GROUP

    def piece(g):
        return pl.ds(g * GROUP, GROUP)

    width = GROUP * classes
    loads = [
        pltpu.make_async_copy(
            shells_hbm.at[:, pl.ds(g * 2 * width, 2 * width)],
            shells.at[:, pl.ds(g * 2 * width, 2 * width)],
            sems.at[g],
        )
        for g in range(parts // 2)
    ]
    column_load = pltpu.make_async_copy(
        shells_hbm.at[0, pl.ds(nodes * classes, columns.shape[0])], columns, column_sem
    )
    column_load.start()
    for load in loads:
        load.start()
    plane = pressure_out.shape[1]
    blocks = window.shape[0]
    rows = blocks * chunks

    def field_of(f):
        return window[:, f].reshape(rows, LANES)

    field = field_of(2 * SUBSTEPS - 1)
    walls = []
    for t in range(SUBSTEPS):
        walls.append(0.5 * field)
        walls_all[t] = walls[t]
        gas = field_of(t)
        for s in range(1, t + 1):
            gas = gas + field_of(SUBSTEPS + t - s) * walls[s]
        chamber = 1.5 - 0.5 * jnp.sum(gas) / (rows * LANES)
        field = field + 0.15 * laplacian(field, plane) + 0.1 * gas + 0.2 * (chamber - field)
    last[...] = field
    cell = lax.axis_index("cell")
    first = cell * chunks
    tile = pressure_out.shape[0] * plane // LANES
    per = plane // LANES
    at = first + lax.axis_index("cls") * tile
    for i in range(tile):
        pressure_out[i // per : i // per + 1, (i % per) * LANES : (i % per + 1) * LANES] = last[
            pl.ds(at + i, 1), :
        ]
    walls_here = [
        [
            jnp.broadcast_to(walls_all[s, pl.ds(first + r, 1), :], (classes, LANES))
            for r in range(chunks)
        ]
        for s in range(SUBSTEPS)
    ]
    stores = [
        pltpu.make_async_copy(out.at[piece(g)], out_hbm.at[piece(g)], out_sems.at[g]) for g in range(parts)
    ]
    column_load.wait()
    cols = [
        columns[(SUBSTEPS - 1 - s) * classes : (SUBSTEPS - s) * classes, :] for s in range(SUBSTEPS)
    ]
    for g in range(parts):
        if g % 2 == 0:
            loads[g // 2].wait()
        for i in range(g * GROUP, (g + 1) * GROUP):
            weights = [jnp.broadcast_to(cols[s][:, i : i + 1], (classes, LANES)) for s in range(SUBSTEPS)]
            for r in range(chunks):
                value = shells[r, i * classes : (i + 1) * classes, :]
                for s in range(SUBSTEPS):
                    value = value + weights[s] * walls_here[s][r]
                out[i, :, r * LANES : (r + 1) * LANES] = value
        stores[g].start()
    for store in stores:
        store.wait()


HBM = pl.BlockSpec(memory_space=pltpu.HBM)
VMEM = pl.BlockSpec(memory_space=pltpu.VMEM)
DMA = pltpu.SemaphoreType.DMA


def exchange(copies, axis):
    return lax.all_to_all(copies, axis, split_axis=0, concat_axis=0, tiled=True)


def shards(melt, counts, pressure, propagator, coupling, flux_weights):
    nodes, classes, cells = melt.shape
    chunks = cells // LANES
    f32 = jnp.float32
    split = (chunks, nodes * classes, LANES)
    whole = pltpu.CompilerParams(vmem_limit_bytes=60 * 2**20)
    most = pltpu.CompilerParams(vmem_limit_bytes=52 * 2**20)
    cls_count = lax.axis_size("cls")
    cell_count = lax.axis_size("cell")
    prop_v = pltpu.VMEM((classes, nodes, nodes), f32)
    small = pltpu.VMEM((classes, nodes), f32)
    parts = nodes // GROUP
    packed = pl.pallas_call(
        fields_kernel,
        out_shape=jax.ShapeDtypeStruct((cls_count, FIELDS, chunks, LANES), f32),
        in_specs=[HBM] * 6,
        out_specs=VMEM,
        scratch_shapes=[
            pltpu.VMEM(melt.shape, f32),
            pltpu.VMEM(counts.shape, counts.dtype),
            pltpu.VMEM(pressure.shape, f32),
            prop_v,
            small,
            small,
            DMA((parts,)),
            DMA((5,)),
        ],
        compiler_params=whole,
        name="fields",
    )(melt, counts, pressure, propagator, coupling, flux_weights)
    height = (nodes + SUBSTEPS + 1) * classes
    half = (chunks + 1) // 2
    melt_flat = melt.reshape(nodes * classes, cells)
    shells_shape = jax.ShapeDtypeStruct((chunks, height, LANES), f32)
    lefts_shape = (classes, nodes, 3 * nodes)
    cost = pl.CostEstimate(flops=10**9, bytes_accessed=melt.size * 4, transcendentals=0)
    shells, lefts = pl.pallas_call(
        power_kernel,
        out_shape=[shells_shape, jax.ShapeDtypeStruct(lefts_shape, jnp.bfloat16)],
        in_specs=[HBM] * 3,
        out_specs=[HBM] * 2,
        scratch_shapes=[
            pltpu.VMEM((half,) + split[1:], f32),
            pltpu.VMEM((half,) + split[1:], f32),
            pltpu.VMEM(((SUBSTEPS + 1) * classes, LANES), f32),
            pltpu.VMEM(lefts_shape, jnp.bfloat16),
            prop_v,
            small,
            DMA((half,)),
            DMA((half,)),
            DMA((4,)),
        ],
        compiler_params=whole,
        cost_estimate=cost,
        name="power",
    )(melt_flat, propagator, coupling)
    copies = pl.pallas_call(
        combine_kernel,
        out_shape=jax.ShapeDtypeStruct((cell_count, FIELDS - 1, chunks, LANES), f32),
        in_specs=[VMEM, HBM],
        out_specs=VMEM,
        compiler_params=most,
        name="combine",
    )(exchange(packed, "cls"), shells)
    left = chunks - half
    shells = pl.pallas_call(
        functools.partial(rest_kernel, half),
        out_shape=shells_shape,
        in_specs=[HBM] * 4,
        out_specs=HBM,
        scratch_shapes=[
            pltpu.VMEM((left,) + split[1:], f32),
            pltpu.VMEM((left,) + split[1:], f32),
            pltpu.VMEM((classes, LANES), f32),
            pltpu.VMEM(lefts_shape, jnp.bfloat16),
            DMA((left,)),
            DMA((left,)),
            DMA((2,)),
        ],
        input_output_aliases={2: 0},
        compiler_params=whole,
        cost_estimate=cost,
        name="rest",
    )(melt_flat, lefts, shells, copies)
    window = exchange(copies, "cell")
    rows = cell_count * chunks
    return pl.pallas_call(
        finish_kernel,
        out_shape=[jax.ShapeDtypeStruct(melt.shape, f32), jax.ShapeDtypeStruct(pressure.shape, f32)],
        in_specs=[VMEM, HBM],
        out_specs=[HBM, VMEM],
        scratch_shapes=[
            pltpu.VMEM(split, f32),
            pltpu.VMEM(melt.shape, f32),
            pltpu.VMEM((SUBSTEPS * classes, LANES), f32),
            pltpu.VMEM((SUBSTEPS, rows, LANES), f32),
            pltpu.VMEM((rows, LANES), f32),
            DMA((parts // 2,)),
            DMA((parts,)),
            DMA(()),
        ],
        compiler_params=most,
        name="finish",
    )(window, shells)


def solution(mesh):
    placed = (P(None, "cls", "cell"), P("cls", "cell"), P(("cell", "cls"), None), P(), P(), P())
    return jax.shard_map(
        shards,
        mesh=mesh,
        in_specs=placed,
        out_specs=(P(None, "cls", "cell"), P(("cell", "cls"), None)),
        check_vma=False,
    )
```

```python
import functools

import jax
import jax.numpy as jnp
from jax import lax
from jax.experimental import pallas as pl
from jax.experimental.pallas import tpu as pltpu
from jax.sharding import PartitionSpec as P

CLASSES = 32
SIDE = 16
SUBSTEPS = 4
COUNT_SCALE = 400.0
LANES = 128
GROUP = 8
FIELDS = 2 * SUBSTEPS + 1

HIGHEST = lax.Precision.HIGHEST


def grow(value, factor, times):
    for _ in range(times):
        value = value * factor
    return value


def iota(shape, dim):
    return lax.broadcasted_iota(jnp.int32, shape, dim)


def split2(x):
    high = x.astype(jnp.bfloat16)
    return high, (x - high.astype(jnp.float32)).astype(jnp.bfloat16)


def dot(a, b):
    return jnp.dot(a, b, preferred_element_type=jnp.float32)


def left_of(x):
    high, low = split2(x)
    return jnp.concatenate([high, high, low], axis=1)


def right_of(x):
    high, low = split2(x)
    return jnp.concatenate([high, low, high], axis=0)


def class_scale(prop):
    rows = [jnp.max(jnp.abs(prop[k]), axis=0, keepdims=True) for k in range(prop.shape[0])]
    return jnp.maximum(1.0, jnp.max(jnp.concatenate(rows, axis=0), axis=1, keepdims=True))


def param_copies(pairs, sems):
    copies = []
    for n, (source, target) in enumerate(pairs):
        own = pl.ds(lax.axis_index("cls") * target.shape[0], target.shape[0])
        copies.append(pltpu.make_async_copy(source.at[own], target, sems.at[n]))
    return copies


def fields_kernel(
    melt_hbm, counts_hbm, pressure_hbm, prop_hbm, coup_hbm, flux_hbm, out, melt, counts, pressure, prop, coup, flux, sems, other_sems
):
    nodes, classes, cells = melt.shape
    first = param_copies([(prop_hbm, prop), (flux_hbm, flux), (coup_hbm, coup)], other_sems)
    for copy in first:
        copy.start()
    parts = nodes // GROUP
    pieces = [
        pltpu.make_async_copy(
            melt_hbm.at[pl.ds(g * GROUP, GROUP)], melt.at[pl.ds(g * GROUP, GROUP)], sems.at[g]
        )
        for g in range(parts)
    ]
    for piece in pieces:
        piece.start()
    rest = [
        pltpu.make_async_copy(counts_hbm, counts, other_sems.at[3]),
        pltpu.make_async_copy(pressure_hbm, pressure, other_sems.at[4]),
    ]
    for copy in rest:
        copy.start()
    for copy in first:
        copy.wait()
    scale = class_scale(prop)
    width = classes * nodes
    table = jnp.concatenate(split2(prop[...].reshape(width, nodes)), axis=1)
    inverse = 1.0 / scale
    mask = iota((classes, width), 1) // nodes == iota((classes, width), 0)
    rows = [flux[...]]
    for _ in range(SUBSTEPS):
        wide = jnp.where(mask, jnp.concatenate([rows[-1]] * classes, axis=1), 0.0)
        pairs = dot(jnp.concatenate(split2(wide), axis=0), table)
        row = pairs[:classes] + pairs[classes:]
        rows.append((row[:, :nodes] + row[:, nodes:]) * inverse)
    spread = [
        grow(jnp.sum(rows[d] * coup[...], axis=1, keepdims=True), scale, d) for d in range(SUBSTEPS)
    ]
    for copy in rest:
        copy.wait()
    counts_n = counts[...].astype(jnp.float32) / (COUNT_SCALE * CLASSES)
    chunks = cells // LANES
    sums = [[jnp.zeros((classes, LANES), jnp.float32) for _ in range(chunks)] for _ in range(SUBSTEPS)]
    for g in range(parts):
        pieces[g].wait()
        for j in range(g * GROUP, (g + 1) * GROUP):
            weights = [
                jnp.broadcast_to(rows[t + 1][:, j : j + 1], (classes, LANES)) for t in range(SUBSTEPS)
            ]
            for r in range(chunks):
                value = melt[j, :, r * LANES : (r + 1) * LANES]
                for t in range(SUBSTEPS):
                    sums[t][r] = sums[t][r] + weights[t] * value
    every = range(out.shape[0])
    for n in every:
        out[n, 2 * SUBSTEPS] = jnp.zeros((chunks, LANES), jnp.float32)
    for r in range(chunks):
        here = counts_n[:, r * LANES : (r + 1) * LANES]
        for t in range(SUBSTEPS):
            row = jnp.sum(grow(here * sums[t][r], scale, t + 1), axis=0, keepdims=True)
            for n in every:
                out[n, t, r : r + 1, :] = row
        for d in range(SUBSTEPS):
            row = jnp.sum(here * spread[d], axis=0, keepdims=True)
            for n in every:
                out[n, SUBSTEPS + d, r : r + 1, :] = row
    per = pressure.shape[1] // LANES
    tile = pressure.shape[0] * per
    at = lax.axis_index("cls") * tile
    for i in range(tile):
        row = pressure[i // per : i // per + 1, (i % per) * LANES : (i % per + 1) * LANES]
        for n in every:
            out[n, 2 * SUBSTEPS, pl.ds(at + i, 1), :] = row


def power_kernel(melt_hbm, prop_hbm, coup_hbm, out_hbm, melt, out, prop, coup, sems, out_sems, param_sems):
    chunks = melt.shape[0]
    classes, nodes = prop.shape[:2]
    params = param_copies([(prop_hbm, prop), (coup_hbm, coup)], param_sems)
    for copy in params:
        copy.start()
    loads = [
        pltpu.make_async_copy(melt_hbm.at[:, pl.ds(r * LANES, LANES)], melt.at[r], sems.at[r])
        for r in range(chunks)
    ]
    stores = [
        pltpu.make_async_copy(out.at[r], out_hbm.at[r], out_sems.at[r]) for r in range(chunks + 1)
    ]
    for load in loads:
        load.start()
    for copy in params:
        copy.wait()
    scale = class_scale(prop)
    inverse = 1.0 / scale
    every = range(classes)
    factors = [scale[k : k + 1, :] for k in every]
    unit = [prop[k] * inverse[k : k + 1, :] for k in every]
    first = [left_of(unit[k]) for k in every]
    square = [dot(first[k], right_of(unit[k])) for k in every]
    second = [left_of(square[k]) for k in every]
    lefts = [left_of(dot(second[k], right_of(square[k]))) for k in every]
    start = jnp.concatenate(
        [jnp.transpose(coup[...]), jnp.zeros((nodes, LANES - classes), jnp.float32)], axis=1
    )
    once = [dot(first[k], right_of(start)) for k in every]
    start = start[:, :classes]
    twice = [
        dot(second[k], right_of(jnp.concatenate([start, once[k][:, :classes]], axis=1))) for k in every
    ]
    lane = iota((nodes, LANES), 1)
    for k in every:
        powers = [
            start[:, k : k + 1],
            once[k][:, k : k + 1],
            twice[k][:, k : k + 1],
            twice[k][:, classes + k : classes + k + 1],
        ]
        value = jnp.zeros((nodes, LANES), jnp.float32)
        for d in range(SUBSTEPS):
            value = jnp.where(lane % SUBSTEPS == SUBSTEPS - 1 - d, grow(powers[d], factors[k], d), value)
        high = value.astype(jnp.bfloat16).astype(jnp.float32)
        value = jnp.where(lane < 2 * SUBSTEPS, high, jnp.where(lane < 3 * SUBSTEPS, value - high, 0.0))
        out[chunks, pl.ds(k, nodes, stride=classes), :] = value
    stores[chunks].start()
    together = 2 if chunks % 2 == 0 else 1
    for r in range(0, chunks, together):
        for n in range(together):
            loads[r + n].wait()
        for k in every:
            own = pl.ds(k, nodes, stride=classes)
            x = jnp.concatenate([melt[r + n, own, :] for n in range(together)], axis=1)
            part = grow(dot(lefts[k], right_of(x)), factors[k], SUBSTEPS)
            for n in range(together):
                out[r + n, own, :] = part[:, n * LANES : (n + 1) * LANES]
        for n in range(together):
            stores[r + n].start()
    for store in stores:
        store.wait()


def combine_kernel(parts, _, out):
    total = parts[0]
    for n in range(1, parts.shape[0]):
        total = total + parts[n]
    wall = 0.5 * total[2 * SUBSTEPS]
    for n in range(out.shape[0]):
        for t in range(SUBSTEPS):
            out[n, t] = total[t] + total[SUBSTEPS + t] * wall
        for d in range(SUBSTEPS - 1):
            out[n, SUBSTEPS + d] = total[SUBSTEPS + d]
        out[n, 2 * SUBSTEPS - 1] = total[2 * SUBSTEPS]


def laplacian(x, plane):
    rows = x.shape[0]
    row = iota(x.shape, 0)
    lane = iota(x.shape, 1)
    per = plane // LANES
    inside = row % per * LANES + lane
    col = lane % SIDE
    total = jnp.where(col == 0, 0.0, pltpu.roll(x, 1, 1))
    total += jnp.where(col == SIDE - 1, 0.0, pltpu.roll(x, LANES - 1, 1))
    up = pltpu.roll(x, SIDE, 1)
    up = jnp.where(lane < SIDE, pltpu.roll(up, 1, 0), up)
    total += jnp.where(inside < SIDE, 0.0, up)
    down = pltpu.roll(x, LANES - SIDE, 1)
    down = jnp.where(lane >= LANES - SIDE, pltpu.roll(down, rows - 1, 0), down)
    total += jnp.where(inside >= plane - SIDE, 0.0, down)
    total += jnp.where(row < per, 0.0, pltpu.roll(x, per, 0))
    total += jnp.where(row >= rows - per, 0.0, pltpu.roll(x, rows - per, 0))
    return total - 6.0 * x


def finish_kernel(
    window, shells_hbm, out_hbm, pressure_out, shells, out, columns, walls_all, last, sems, out_sems, column_sem
):
    nodes, classes, cells = out.shape
    chunks = cells // LANES
    parts = nodes // GROUP
    width = GROUP * classes

    def piece(g):
        return pl.ds(g * GROUP, GROUP)

    column_load = pltpu.make_async_copy(shells_hbm.at[chunks], columns, column_sem)
    column_load.start()
    loads = [
        pltpu.make_async_copy(
            shells_hbm.at[pl.ds(0, chunks), pl.ds(g * 2 * width, 2 * width)],
            shells.at[:, pl.ds(g * 2 * width, 2 * width)],
            sems.at[g],
        )
        for g in range(parts // 2)
    ]
    for load in loads:
        load.start()
    plane = pressure_out.shape[1]
    blocks = window.shape[0]
    rows = blocks * chunks

    def field_of(f):
        return window[:, f].reshape(rows, LANES)

    field = field_of(2 * SUBSTEPS - 1)
    walls = []
    for t in range(SUBSTEPS):
        walls.append(0.5 * field)
        walls_all[t] = walls[t]
        gas = field_of(t)
        for s in range(1, t + 1):
            gas = gas + field_of(SUBSTEPS + t - s) * walls[s]
        chamber = 1.5 - 0.5 * jnp.sum(gas) / (rows * LANES)
        field = field + 0.15 * laplacian(field, plane) + 0.1 * gas + 0.2 * (chamber - field)
    last[...] = field
    cell = lax.axis_index("cell")
    first = cell * chunks
    tile = pressure_out.shape[0] * plane // LANES
    per = plane // LANES
    at = first + lax.axis_index("cls") * tile
    for i in range(tile):
        pressure_out[i // per : i // per + 1, (i % per) * LANES : (i % per + 1) * LANES] = last[
            pl.ds(at + i, 1), :
        ]
    right = []
    for r in range(chunks):
        wall = jnp.concatenate([walls_all[s, pl.ds(first + r, 1), :] for s in range(SUBSTEPS)], axis=0)
        high = wall.astype(jnp.bfloat16).astype(jnp.float32)
        right.append(jnp.concatenate([high, wall - high, high, jnp.zeros_like(high)], axis=0))
    right = jnp.concatenate(right, axis=1).astype(jnp.bfloat16)
    stores = [
        pltpu.make_async_copy(out.at[piece(g)], out_hbm.at[piece(g)], out_sems.at[g]) for g in range(parts)
    ]
    column_load.wait()
    for g in range(parts):
        here = slice(g * width, (g + 1) * width)
        change = dot(columns[here, : 4 * SUBSTEPS].astype(jnp.bfloat16), right)
        if g % 2 == 0:
            loads[g // 2].wait()
        for r in range(chunks):
            lanes = slice(r * LANES, (r + 1) * LANES)
            value = shells[r, here, :] + change[:, lanes]
            out[g * GROUP : (g + 1) * GROUP, :, lanes] = value.reshape(GROUP, classes, LANES)
        stores[g].start()
    for store in stores:
        store.wait()


HBM = pl.BlockSpec(memory_space=pltpu.HBM)
VMEM = pl.BlockSpec(memory_space=pltpu.VMEM)
DMA = pltpu.SemaphoreType.DMA


def exchange(copies, axis):
    return lax.all_to_all(copies, axis, split_axis=0, concat_axis=0, tiled=True)


def shards(melt, counts, pressure, propagator, coupling, flux_weights):
    nodes, classes, cells = melt.shape
    chunks = cells // LANES
    f32 = jnp.float32
    split = (chunks, nodes * classes, LANES)
    whole = pltpu.CompilerParams(vmem_limit_bytes=60 * 2**20)
    most = pltpu.CompilerParams(vmem_limit_bytes=52 * 2**20)
    cls_count = lax.axis_size("cls")
    cell_count = lax.axis_size("cell")
    prop_v = pltpu.VMEM((classes, nodes, nodes), f32)
    small = pltpu.VMEM((classes, nodes), f32)
    parts = nodes // GROUP
    packed = pl.pallas_call(
        fields_kernel,
        out_shape=jax.ShapeDtypeStruct((cls_count, FIELDS, chunks, LANES), f32),
        in_specs=[HBM] * 6,
        out_specs=VMEM,
        scratch_shapes=[
            pltpu.VMEM(melt.shape, f32),
            pltpu.VMEM(counts.shape, counts.dtype),
            pltpu.VMEM(pressure.shape, f32),
            prop_v,
            small,
            small,
            DMA((parts,)),
            DMA((5,)),
        ],
        compiler_params=whole,
        name="fields",
    )(melt, counts, pressure, propagator, coupling, flux_weights)
    shells = pl.pallas_call(
        power_kernel,
        out_shape=jax.ShapeDtypeStruct((chunks + 1,) + split[1:], f32),
        in_specs=[HBM] * 3,
        out_specs=HBM,
        scratch_shapes=[
            pltpu.VMEM(split, f32),
            pltpu.VMEM((chunks + 1,) + split[1:], f32),
            prop_v,
            small,
            DMA((chunks,)),
            DMA((chunks + 1,)),
            DMA((2,)),
        ],
        compiler_params=whole,
        cost_estimate=pl.CostEstimate(flops=2 * 10**9, bytes_accessed=2 * melt.size * 4, transcendentals=0),
        name="power",
    )(melt.reshape(nodes * classes, cells), propagator, coupling)
    copies = pl.pallas_call(
        combine_kernel,
        out_shape=jax.ShapeDtypeStruct((cell_count, FIELDS - 1, chunks, LANES), f32),
        in_specs=[VMEM, HBM],
        out_specs=VMEM,
        compiler_params=most,
        name="combine",
    )(exchange(packed, "cls"), shells)
    window = exchange(copies, "cell")
    rows = cell_count * chunks
    return pl.pallas_call(
        finish_kernel,
        out_shape=[jax.ShapeDtypeStruct(melt.shape, f32), jax.ShapeDtypeStruct(pressure.shape, f32)],
        in_specs=[VMEM, HBM],
        out_specs=[HBM, VMEM],
        scratch_shapes=[
            pltpu.VMEM(split, f32),
            pltpu.VMEM(melt.shape, f32),
            pltpu.VMEM(split[1:], f32),
            pltpu.VMEM((SUBSTEPS, rows, LANES), f32),
            pltpu.VMEM((rows, LANES), f32),
            DMA((parts // 2,)),
            DMA((parts,)),
            DMA(()),
        ],
        compiler_params=most,
        name="finish",
    )(window, shells)


def solution(mesh):
    placed = (P(None, "cls", "cell"), P("cls", "cell"), P(("cell", "cls"), None), P(), P(), P())
    return jax.shard_map(
        shards,
        mesh=mesh,
        in_specs=placed,
        out_specs=(P(None, "cls", "cell"), P(("cell", "cls"), None)),
        check_vma=False,
    )
```

```python
import functools

import jax
import jax.numpy as jnp
from jax import lax
from jax.experimental import pallas as pl
from jax.experimental.pallas import tpu as pltpu
from jax.sharding import PartitionSpec as P

CLASSES = 32
SIDE = 16
SUBSTEPS = 4
COUNT_SCALE = 400.0
LANES = 128
GROUP = 8
FIELDS = 2 * SUBSTEPS + 1

HIGHEST = lax.Precision.HIGHEST


def grow(value, factor, times):
    for _ in range(times):
        value = value * factor
    return value


def iota(shape, dim):
    return lax.broadcasted_iota(jnp.int32, shape, dim)


def split2(x):
    high = x.astype(jnp.bfloat16)
    return high, (x - high.astype(jnp.float32)).astype(jnp.bfloat16)


def dot(a, b):
    return jnp.dot(a, b, preferred_element_type=jnp.float32)


def left_of(x):
    high, low = split2(x)
    return jnp.concatenate([high, high, low], axis=1)


def right_of(x):
    high, low = split2(x)
    return jnp.concatenate([high, low, high], axis=0)


def class_scale(prop):
    rows = [jnp.max(jnp.abs(prop[k]), axis=0, keepdims=True) for k in range(prop.shape[0])]
    return jnp.maximum(1.0, jnp.max(jnp.concatenate(rows, axis=0), axis=1, keepdims=True))


def param_copies(pairs, sems):
    copies = []
    for n, (source, target) in enumerate(pairs):
        own = pl.ds(lax.axis_index("cls") * target.shape[0], target.shape[0])
        copies.append(pltpu.make_async_copy(source.at[own], target, sems.at[n]))
    return copies


def fields_kernel(
    melt_hbm, counts_hbm, pressure_hbm, prop_hbm, coup_hbm, flux_hbm, out, melt, counts, pressure, prop, coup, flux, sems, other_sems
):
    nodes, classes, cells = melt.shape
    first = param_copies([(prop_hbm, prop), (flux_hbm, flux), (coup_hbm, coup)], other_sems)
    for copy in first:
        copy.start()
    parts = nodes // GROUP
    pieces = [
        pltpu.make_async_copy(
            melt_hbm.at[pl.ds(g * GROUP, GROUP)], melt.at[pl.ds(g * GROUP, GROUP)], sems.at[g]
        )
        for g in range(parts)
    ]
    for piece in pieces:
        piece.start()
    rest = [
        pltpu.make_async_copy(counts_hbm, counts, other_sems.at[3]),
        pltpu.make_async_copy(pressure_hbm, pressure, other_sems.at[4]),
    ]
    for copy in rest:
        copy.start()
    for copy in first:
        copy.wait()
    scale = class_scale(prop)
    width = classes * nodes
    table = jnp.concatenate(split2(prop[...].reshape(width, nodes)), axis=1)
    inverse = 1.0 / scale
    mask = iota((classes, width), 1) // nodes == iota((classes, width), 0)
    rows = [flux[...]]
    for _ in range(SUBSTEPS):
        wide = jnp.where(mask, jnp.concatenate([rows[-1]] * classes, axis=1), 0.0)
        pairs = dot(jnp.concatenate(split2(wide), axis=0), table)
        row = pairs[:classes] + pairs[classes:]
        rows.append((row[:, :nodes] + row[:, nodes:]) * inverse)
    spread = [
        grow(jnp.sum(rows[d] * coup[...], axis=1, keepdims=True), scale, d) for d in range(SUBSTEPS)
    ]
    for copy in rest:
        copy.wait()
    counts_n = counts[...].astype(jnp.float32) / (COUNT_SCALE * CLASSES)
    chunks = cells // LANES
    sums = [[jnp.zeros((classes, LANES), jnp.float32) for _ in range(chunks)] for _ in range(SUBSTEPS)]
    for g in range(parts):
        pieces[g].wait()
        for j in range(g * GROUP, (g + 1) * GROUP):
            weights = [
                jnp.broadcast_to(rows[t + 1][:, j : j + 1], (classes, LANES)) for t in range(SUBSTEPS)
            ]
            for r in range(chunks):
                value = melt[j, :, r * LANES : (r + 1) * LANES]
                for t in range(SUBSTEPS):
                    sums[t][r] = sums[t][r] + weights[t] * value
    every = range(out.shape[0])
    for n in every:
        out[n, 2 * SUBSTEPS] = jnp.zeros((chunks, LANES), jnp.float32)
    for r in range(chunks):
        here = counts_n[:, r * LANES : (r + 1) * LANES]
        for t in range(SUBSTEPS):
            row = jnp.sum(grow(here * sums[t][r], scale, t + 1), axis=0, keepdims=True)
            for n in every:
                out[n, t, r : r + 1, :] = row
        for d in range(SUBSTEPS):
            row = jnp.sum(here * spread[d], axis=0, keepdims=True)
            for n in every:
                out[n, SUBSTEPS + d, r : r + 1, :] = row
    per = pressure.shape[1] // LANES
    tile = pressure.shape[0] * per
    at = lax.axis_index("cls") * tile
    for i in range(tile):
        row = pressure[i // per : i // per + 1, (i % per) * LANES : (i % per + 1) * LANES]
        for n in every:
            out[n, 2 * SUBSTEPS, pl.ds(at + i, 1), :] = row


def power_kernel(melt_hbm, prop_hbm, coup_hbm, out_hbm, melt, out, prop, coup, sems, out_sems, param_sems):
    chunks = melt.shape[0]
    classes, nodes = prop.shape[:2]
    params = param_copies([(prop_hbm, prop), (coup_hbm, coup)], param_sems)
    for copy in params:
        copy.start()
    loads = [
        pltpu.make_async_copy(melt_hbm.at[:, pl.ds(r * LANES, LANES)], melt.at[r], sems.at[r])
        for r in range(chunks)
    ]
    stores = [
        pltpu.make_async_copy(out.at[r], out_hbm.at[r], out_sems.at[r]) for r in range(chunks + 1)
    ]
    for load in loads:
        load.start()
    for copy in params:
        copy.wait()
    scale = class_scale(prop)
    inverse = 1.0 / scale
    every = range(classes)
    factors = [scale[k : k + 1, :] for k in every]
    unit = [prop[k] * inverse[k : k + 1, :] for k in every]
    first = [left_of(unit[k]) for k in every]
    square = [dot(first[k], right_of(unit[k])) for k in every]
    second = [left_of(square[k]) for k in every]
    lefts = [left_of(dot(second[k], right_of(square[k]))) for k in every]
    start = jnp.concatenate(
        [jnp.transpose(coup[...]), jnp.zeros((nodes, LANES - classes), jnp.float32)], axis=1
    )
    once = [dot(first[k], right_of(start)) for k in every]
    start = start[:, :classes]
    twice = [
        dot(second[k], right_of(jnp.concatenate([start, once[k][:, :classes]], axis=1))) for k in every
    ]
    lane = iota((nodes, LANES), 1)
    for k in every:
        powers = [
            start[:, k : k + 1],
            once[k][:, k : k + 1],
            twice[k][:, k : k + 1],
            twice[k][:, classes + k : classes + k + 1],
        ]
        value = jnp.zeros((nodes, LANES), jnp.float32)
        for d in range(SUBSTEPS):
            value = jnp.where(lane % SUBSTEPS == SUBSTEPS - 1 - d, grow(powers[d], factors[k], d), value)
        high = value.astype(jnp.bfloat16).astype(jnp.float32)
        value = jnp.where(lane < 2 * SUBSTEPS, high, jnp.where(lane < 3 * SUBSTEPS, value - high, 0.0))
        out[chunks, pl.ds(k, nodes, stride=classes), :] = value
    stores[chunks].start()
    together = 2 if chunks % 2 == 0 else 1
    for r in range(0, chunks, together):
        for n in range(together):
            loads[r + n].wait()
        for k in every:
            own = pl.ds(k, nodes, stride=classes)
            x = jnp.concatenate([melt[r + n, own, :] for n in range(together)], axis=1)
            part = grow(dot(lefts[k], right_of(x)), factors[k], SUBSTEPS)
            for n in range(together):
                out[r + n, own, :] = part[:, n * LANES : (n + 1) * LANES]
        for n in range(together):
            stores[r + n].start()
    for store in stores:
        store.wait()


def combine_kernel(parts, _, out):
    total = parts[0]
    for n in range(1, parts.shape[0]):
        total = total + parts[n]
    wall = 0.5 * total[2 * SUBSTEPS]
    for t in range(SUBSTEPS):
        out[t] = total[t] + total[SUBSTEPS + t] * wall
    for d in range(SUBSTEPS - 1):
        out[SUBSTEPS + d] = total[SUBSTEPS + d]
    out[2 * SUBSTEPS - 1] = total[2 * SUBSTEPS]


def total_of(x):
    tiles = jnp.sum(x.reshape(-1, GROUP, LANES), axis=0)
    return jnp.sum(jnp.sum(tiles, axis=1, keepdims=True), axis=0, keepdims=True)


def laplacian(x, plane):
    rows = x.shape[0]
    row = iota(x.shape, 0)
    lane = iota(x.shape, 1)
    per = plane // LANES
    inside = row % per * LANES + lane
    col = lane % SIDE
    total = jnp.where(col == 0, 0.0, pltpu.roll(x, 1, 1))
    total += jnp.where(col == SIDE - 1, 0.0, pltpu.roll(x, LANES - 1, 1))
    up = pltpu.roll(x, SIDE, 1)
    up = jnp.where(lane < SIDE, pltpu.roll(up, 1, 0), up)
    total += jnp.where(inside < SIDE, 0.0, up)
    down = pltpu.roll(x, LANES - SIDE, 1)
    down = jnp.where(lane >= LANES - SIDE, pltpu.roll(down, rows - 1, 0), down)
    total += jnp.where(inside >= plane - SIDE, 0.0, down)
    total += jnp.where(row < per, 0.0, pltpu.roll(x, per, 0))
    total += jnp.where(row >= rows - per, 0.0, pltpu.roll(x, rows - per, 0))
    return total - 6.0 * x


def finish_kernel(
    window, shells_hbm, out_hbm, pressure_out, shells, out, columns, walls_all, last, sems, out_sems, column_sem
):
    nodes, classes, cells = out.shape
    chunks = cells // LANES
    parts = nodes // GROUP
    width = GROUP * classes

    def piece(g):
        return pl.ds(g * GROUP, GROUP)

    column_load = pltpu.make_async_copy(shells_hbm.at[chunks], columns, column_sem)
    column_load.start()
    loads = [
        pltpu.make_async_copy(
            shells_hbm.at[pl.ds(0, chunks), pl.ds(g * 2 * width, 2 * width)],
            shells.at[:, pl.ds(g * 2 * width, 2 * width)],
            sems.at[g],
        )
        for g in range(parts // 2)
    ]
    for load in loads:
        load.start()
    plane = pressure_out.shape[1]
    blocks = window.shape[0]
    rows = blocks * chunks

    def field_of(f):
        return window[:, f].reshape(rows, LANES)

    field = field_of(2 * SUBSTEPS - 1)
    answer = field_of(SUBSTEPS)
    answer_total = total_of(answer)
    chamber = None
    walls = []
    for t in range(SUBSTEPS):
        gas = field_of(t)
        for s in range(1, t):
            gas = gas + field_of(SUBSTEPS + t - s) * walls[s]
        if t:
            gas = gas + answer * (0.5 * field)
        total = total_of(gas)
        if t:
            field = field + 0.2 * chamber
            gas = gas + answer * (0.1 * chamber)
            total = total + answer_total * (0.1 * chamber)
        walls.append(0.5 * field)
        walls_all[t] = walls[t]
        field = 0.8 * field + 0.15 * laplacian(field, plane) + 0.1 * gas
        chamber = 1.5 - 0.5 * total / (rows * LANES)
    last[...] = field + 0.2 * chamber
    cell = lax.axis_index("cell")
    first = cell * chunks
    tile = pressure_out.shape[0] * plane // LANES
    per = plane // LANES
    at = first + lax.axis_index("cls") * tile
    for i in range(tile):
        pressure_out[i // per : i // per + 1, (i % per) * LANES : (i % per + 1) * LANES] = last[
            pl.ds(at + i, 1), :
        ]
    right = []
    for r in range(chunks):
        wall = jnp.concatenate([walls_all[s, pl.ds(first + r, 1), :] for s in range(SUBSTEPS)], axis=0)
        high = wall.astype(jnp.bfloat16).astype(jnp.float32)
        right.append(jnp.concatenate([high, wall - high, high, jnp.zeros_like(high)], axis=0))
    right = jnp.concatenate(right, axis=1).astype(jnp.bfloat16)
    stores = [
        pltpu.make_async_copy(out.at[piece(g)], out_hbm.at[piece(g)], out_sems.at[g]) for g in range(parts)
    ]
    column_load.wait()
    for g in range(parts):
        here = slice(g * width, (g + 1) * width)
        change = dot(columns[here, : 4 * SUBSTEPS].astype(jnp.bfloat16), right)
        if g % 2 == 0:
            loads[g // 2].wait()
        for r in range(chunks):
            lanes = slice(r * LANES, (r + 1) * LANES)
            value = shells[r, here, :] + change[:, lanes]
            out[g * GROUP : (g + 1) * GROUP, :, lanes] = value.reshape(GROUP, classes, LANES)
        stores[g].start()
    for store in stores:
        store.wait()


HBM = pl.BlockSpec(memory_space=pltpu.HBM)
VMEM = pl.BlockSpec(memory_space=pltpu.VMEM)
DMA = pltpu.SemaphoreType.DMA


def exchange(copies, axis):
    return lax.all_to_all(copies, axis, split_axis=0, concat_axis=0, tiled=True)


def shards(melt, counts, pressure, propagator, coupling, flux_weights):
    nodes, classes, cells = melt.shape
    chunks = cells // LANES
    f32 = jnp.float32
    split = (chunks, nodes * classes, LANES)
    whole = pltpu.CompilerParams(vmem_limit_bytes=60 * 2**20)
    most = pltpu.CompilerParams(vmem_limit_bytes=52 * 2**20)
    cls_count = lax.axis_size("cls")
    cell_count = lax.axis_size("cell")
    prop_v = pltpu.VMEM((classes, nodes, nodes), f32)
    small = pltpu.VMEM((classes, nodes), f32)
    parts = nodes // GROUP
    packed = pl.pallas_call(
        fields_kernel,
        out_shape=jax.ShapeDtypeStruct((cls_count, FIELDS, chunks, LANES), f32),
        in_specs=[HBM] * 6,
        out_specs=VMEM,
        scratch_shapes=[
            pltpu.VMEM(melt.shape, f32),
            pltpu.VMEM(counts.shape, counts.dtype),
            pltpu.VMEM(pressure.shape, f32),
            prop_v,
            small,
            small,
            DMA((parts,)),
            DMA((5,)),
        ],
        compiler_params=whole,
        name="fields",
    )(melt, counts, pressure, propagator, coupling, flux_weights)
    shells = pl.pallas_call(
        power_kernel,
        out_shape=jax.ShapeDtypeStruct((chunks + 1,) + split[1:], f32),
        in_specs=[HBM] * 3,
        out_specs=HBM,
        scratch_shapes=[
            pltpu.VMEM(split, f32),
            pltpu.VMEM((chunks + 1,) + split[1:], f32),
            prop_v,
            small,
            DMA((chunks,)),
            DMA((chunks + 1,)),
            DMA((2,)),
        ],
        compiler_params=whole,
        cost_estimate=pl.CostEstimate(flops=2 * 10**9, bytes_accessed=2 * melt.size * 4, transcendentals=0),
        name="power",
    )(melt.reshape(nodes * classes, cells), propagator, coupling)
    fields = pl.pallas_call(
        combine_kernel,
        out_shape=jax.ShapeDtypeStruct((FIELDS - 1, chunks, LANES), f32),
        in_specs=[VMEM, HBM],
        out_specs=VMEM,
        compiler_params=most,
        name="combine",
    )(exchange(packed, "cls"), shells)
    window = lax.all_gather(fields, "cell", axis=0)
    rows = cell_count * chunks
    return pl.pallas_call(
        finish_kernel,
        out_shape=[jax.ShapeDtypeStruct(melt.shape, f32), jax.ShapeDtypeStruct(pressure.shape, f32)],
        in_specs=[VMEM, HBM],
        out_specs=[HBM, VMEM],
        scratch_shapes=[
            pltpu.VMEM(split, f32),
            pltpu.VMEM(melt.shape, f32),
            pltpu.VMEM(split[1:], f32),
            pltpu.VMEM((SUBSTEPS, rows, LANES), f32),
            pltpu.VMEM((rows, LANES), f32),
            DMA((parts // 2,)),
            DMA((parts,)),
            DMA(()),
        ],
        compiler_params=most,
        name="finish",
    )(window, shells)


def solution(mesh):
    placed = (P(None, "cls", "cell"), P("cls", "cell"), P(("cell", "cls"), None), P(), P(), P())
    return jax.shard_map(
        shards,
        mesh=mesh,
        in_specs=placed,
        out_specs=(P(None, "cls", "cell"), P(("cell", "cls"), None)),
        check_vma=False,
    )
```

```python
import functools

import jax
import jax.numpy as jnp
from jax import lax
from jax.experimental import pallas as pl
from jax.experimental.pallas import tpu as pltpu
from jax.sharding import PartitionSpec as P

CLASSES = 32
SIDE = 16
SUBSTEPS = 4
COUNT_SCALE = 400.0
LANES = 128
GROUP = 8
FIELDS = 2 * SUBSTEPS + 1


def grow(value, factor, times):
    for _ in range(times):
        value = value * factor
    return value


def iota(shape, dim):
    return lax.broadcasted_iota(jnp.int32, shape, dim)


def split2(x):
    high = x.astype(jnp.bfloat16)
    return high, (x - high.astype(jnp.float32)).astype(jnp.bfloat16)


def dot(a, b):
    return jnp.dot(a, b, preferred_element_type=jnp.float32)


def left_of(x):
    high, low = split2(x)
    return jnp.concatenate([high, high, low], axis=1)


def right_of(x):
    high, low = split2(x)
    return jnp.concatenate([high, low, high], axis=0)


def class_scale(prop):
    rows = [jnp.max(jnp.abs(prop[k]), axis=0, keepdims=True) for k in range(prop.shape[0])]
    return jnp.maximum(1.0, jnp.max(jnp.concatenate(rows, axis=0), axis=1, keepdims=True))


def param_copies(pairs, sems):
    copies = []
    for n, (source, target) in enumerate(pairs):
        own = pl.ds(lax.axis_index("cls") * target.shape[0], target.shape[0])
        copies.append(pltpu.make_async_copy(source.at[own], target, sems.at[n]))
    return copies


def fields_kernel(
    melt_hbm, counts_hbm, pressure_hbm, prop_hbm, coup_hbm, flux_hbm, out, melt, counts, pressure, prop, coup, flux, sems, other_sems
):
    nodes, classes, cells = melt.shape
    first = param_copies([(prop_hbm, prop), (flux_hbm, flux), (coup_hbm, coup)], other_sems)
    for copy in first:
        copy.start()
    parts = nodes // GROUP
    pieces = [
        pltpu.make_async_copy(
            melt_hbm.at[pl.ds(g * GROUP, GROUP)], melt.at[pl.ds(g * GROUP, GROUP)], sems.at[g]
        )
        for g in range(parts)
    ]
    for piece in pieces:
        piece.start()
    rest = [
        pltpu.make_async_copy(counts_hbm, counts, other_sems.at[3]),
        pltpu.make_async_copy(pressure_hbm, pressure, other_sems.at[4]),
    ]
    for copy in rest:
        copy.start()
    for copy in first:
        copy.wait()
    scale = class_scale(prop)
    width = classes * nodes
    table = jnp.concatenate(split2(prop[...].reshape(width, nodes)), axis=1)
    inverse = 1.0 / scale
    mask = iota((classes, width), 1) // nodes == iota((classes, width), 0)
    rows = [flux[...]]
    for _ in range(SUBSTEPS):
        wide = jnp.where(mask, jnp.concatenate([rows[-1]] * classes, axis=1), 0.0)
        pairs = dot(jnp.concatenate(split2(wide), axis=0), table)
        row = pairs[:classes] + pairs[classes:]
        rows.append((row[:, :nodes] + row[:, nodes:]) * inverse)
    spread = [
        grow(jnp.sum(rows[d] * coup[...], axis=1, keepdims=True), scale, d) for d in range(SUBSTEPS)
    ]
    for copy in rest:
        copy.wait()
    counts_n = counts[...].astype(jnp.float32) / (COUNT_SCALE * CLASSES)
    chunks = cells // LANES
    sums = [[jnp.zeros((classes, LANES), jnp.float32) for _ in range(chunks)] for _ in range(SUBSTEPS)]
    for g in range(parts):
        pieces[g].wait()
        for j in range(g * GROUP, (g + 1) * GROUP):
            weights = [
                jnp.broadcast_to(rows[t + 1][:, j : j + 1], (classes, LANES)) for t in range(SUBSTEPS)
            ]
            for r in range(chunks):
                value = melt[j, :, r * LANES : (r + 1) * LANES]
                for t in range(SUBSTEPS):
                    sums[t][r] = sums[t][r] + weights[t] * value
    every = range(out.shape[0])
    for n in every:
        out[n, 2 * SUBSTEPS] = jnp.zeros((chunks, LANES), jnp.float32)
    for r in range(chunks):
        here = counts_n[:, r * LANES : (r + 1) * LANES]
        for t in range(SUBSTEPS):
            row = jnp.sum(grow(here * sums[t][r], scale, t + 1), axis=0, keepdims=True)
            for n in every:
                out[n, t, r : r + 1, :] = row
        for d in range(SUBSTEPS):
            row = jnp.sum(here * spread[d], axis=0, keepdims=True)
            for n in every:
                out[n, SUBSTEPS + d, r : r + 1, :] = row
    per = pressure.shape[1] // LANES
    tile = pressure.shape[0] * per
    at = lax.axis_index("cls") * tile
    for i in range(tile):
        row = pressure[i // per : i // per + 1, (i % per) * LANES : (i % per + 1) * LANES]
        for n in every:
            out[n, 2 * SUBSTEPS, pl.ds(at + i, 1), :] = row


def power_kernel(melt_hbm, prop_hbm, coup_hbm, out_hbm, done, melt, out, prop, coup, sems, out_sems, param_sems):
    chunks = melt.shape[0]
    classes, nodes = prop.shape[:2]
    params = param_copies([(prop_hbm, prop), (coup_hbm, coup)], param_sems)
    for copy in params:
        copy.start()
    loads = [
        pltpu.make_async_copy(melt_hbm.at[:, pl.ds(r * LANES, LANES)], melt.at[r], sems.at[r])
        for r in range(chunks)
    ]
    stores = [
        pltpu.make_async_copy(out.at[r], out_hbm.at[r], out_sems.at[r]) for r in range(chunks + 1)
    ]
    for load in loads:
        load.start()
    for copy in params:
        copy.wait()
    scale = class_scale(prop)
    inverse = 1.0 / scale
    every = range(classes)
    factors = [scale[k : k + 1, :] for k in every]
    unit = [prop[k] * inverse[k : k + 1, :] for k in every]
    first = [left_of(unit[k]) for k in every]
    square = [dot(first[k], right_of(unit[k])) for k in every]
    second = [left_of(square[k]) for k in every]
    lefts = [left_of(dot(second[k], right_of(square[k]))) for k in every]
    start = jnp.concatenate(
        [jnp.transpose(coup[...]), jnp.zeros((nodes, LANES - classes), jnp.float32)], axis=1
    )
    once = [dot(first[k], right_of(start)) for k in every]
    start = start[:, :classes]
    twice = [
        dot(second[k], right_of(jnp.concatenate([start, once[k][:, :classes]], axis=1))) for k in every
    ]
    lane = iota((nodes, LANES), 1)
    for k in every:
        powers = [
            start[:, k : k + 1],
            once[k][:, k : k + 1],
            twice[k][:, k : k + 1],
            twice[k][:, classes + k : classes + k + 1],
        ]
        value = jnp.zeros((nodes, LANES), jnp.float32)
        for d in range(SUBSTEPS):
            value = jnp.where(lane % SUBSTEPS == SUBSTEPS - 1 - d, grow(powers[d], factors[k], d), value)
        high = value.astype(jnp.bfloat16).astype(jnp.float32)
        value = jnp.where(lane < 2 * SUBSTEPS, high, jnp.where(lane < 3 * SUBSTEPS, value - high, 0.0))
        out[chunks, pl.ds(k, nodes, stride=classes), :] = value
    stores[chunks].start()
    together = 2 if chunks % 2 == 0 else 1
    for r in range(0, chunks, together):
        for n in range(together):
            loads[r + n].wait()
        for k in every:
            own = pl.ds(k, nodes, stride=classes)
            x = jnp.concatenate([melt[r + n, own, :] for n in range(together)], axis=1)
            part = grow(dot(lefts[k], right_of(x)), factors[k], SUBSTEPS)
            for n in range(together):
                out[r + n, own, :] = part[:, n * LANES : (n + 1) * LANES]
        for n in range(together):
            stores[r + n].start()
    for store in stores:
        store.wait()
    done[...] = jnp.zeros_like(done)


def combine_kernel(parts, _, out):
    total = parts[0]
    for n in range(1, parts.shape[0]):
        total = total + parts[n]
    wall = 0.5 * total[2 * SUBSTEPS]
    for t in range(SUBSTEPS):
        out[t] = total[t] + total[SUBSTEPS + t] * wall
    for d in range(SUBSTEPS - 1):
        out[SUBSTEPS + d] = total[SUBSTEPS + d]
    out[2 * SUBSTEPS - 1] = total[2 * SUBSTEPS]


def total_of(x):
    tiles = jnp.sum(x.reshape(-1, GROUP, LANES), axis=0)
    return jnp.sum(jnp.sum(tiles, axis=1, keepdims=True), axis=0, keepdims=True)


def laplacian(x, plane):
    rows = x.shape[0]
    row = iota(x.shape, 0)
    lane = iota(x.shape, 1)
    per = plane // LANES
    inside = row % per * LANES + lane
    col = lane % SIDE
    total = jnp.where(col == 0, 0.0, pltpu.roll(x, 1, 1))
    total += jnp.where(col == SIDE - 1, 0.0, pltpu.roll(x, LANES - 1, 1))
    up = pltpu.roll(x, SIDE, 1)
    up = jnp.where(lane < SIDE, pltpu.roll(up, 1, 0), up)
    total += jnp.where(inside < SIDE, 0.0, up)
    down = pltpu.roll(x, LANES - SIDE, 1)
    down = jnp.where(lane >= LANES - SIDE, pltpu.roll(down, rows - 1, 0), down)
    total += jnp.where(inside >= plane - SIDE, 0.0, down)
    total += jnp.where(row < per, 0.0, pltpu.roll(x, per, 0))
    total += jnp.where(row >= rows - per, 0.0, pltpu.roll(x, rows - per, 0))
    return total - 6.0 * x


def finish_kernel(
    window, shells, out_hbm, pressure_out, out, walls_all, last, out_sems
):
    nodes, classes, cells = out.shape
    chunks = cells // LANES
    parts = nodes // GROUP
    width = GROUP * classes

    def piece(g):
        return pl.ds(g * GROUP, GROUP)

    plane = pressure_out.shape[1]
    blocks = window.shape[0]
    rows = blocks * chunks

    def field_of(f):
        return window[:, f].reshape(rows, LANES)

    field = field_of(2 * SUBSTEPS - 1)
    answer = field_of(SUBSTEPS)
    answer_total = total_of(answer)
    chamber = None
    walls = []
    for t in range(SUBSTEPS):
        gas = field_of(t)
        for s in range(1, t):
            gas = gas + field_of(SUBSTEPS + t - s) * walls[s]
        if t:
            gas = gas + answer * (0.5 * field)
        total = total_of(gas)
        if t:
            field = field + 0.2 * chamber
            gas = gas + answer * (0.1 * chamber)
            total = total + answer_total * (0.1 * chamber)
        walls.append(0.5 * field)
        walls_all[t] = walls[t]
        field = 0.8 * field + 0.15 * laplacian(field, plane) + 0.1 * gas
        chamber = 1.5 - 0.5 * total / (rows * LANES)
    last[...] = field + 0.2 * chamber
    cell = lax.axis_index("cell")
    first = cell * chunks
    tile = pressure_out.shape[0] * plane // LANES
    per = plane // LANES
    at = first + lax.axis_index("cls") * tile
    for i in range(tile):
        pressure_out[i // per : i // per + 1, (i % per) * LANES : (i % per + 1) * LANES] = last[
            pl.ds(at + i, 1), :
        ]
    right = []
    for r in range(chunks):
        wall = jnp.concatenate([walls_all[s, pl.ds(first + r, 1), :] for s in range(SUBSTEPS)], axis=0)
        high = wall.astype(jnp.bfloat16).astype(jnp.float32)
        right.append(jnp.concatenate([high, wall - high, high, jnp.zeros_like(high)], axis=0))
    right = jnp.concatenate(right, axis=1).astype(jnp.bfloat16)
    stores = [
        pltpu.make_async_copy(out.at[piece(g)], out_hbm.at[piece(g)], out_sems.at[g]) for g in range(parts)
    ]
    for g in range(parts):
        here = slice(g * width, (g + 1) * width)
        change = dot(shells[chunks, here, : 4 * SUBSTEPS].astype(jnp.bfloat16), right)
        for r in range(chunks):
            lanes = slice(r * LANES, (r + 1) * LANES)
            value = shells[r, here, :] + change[:, lanes]
            out[g * GROUP : (g + 1) * GROUP, :, lanes] = value.reshape(GROUP, classes, LANES)
        stores[g].start()
    for store in stores:
        store.wait()


HBM = pl.BlockSpec(memory_space=pltpu.HBM)
VMEM = pl.BlockSpec(memory_space=pltpu.VMEM)
DMA = pltpu.SemaphoreType.DMA


def exchange(copies, axis):
    return lax.all_to_all(copies, axis, split_axis=0, concat_axis=0, tiled=True)


def shards(melt, counts, pressure, propagator, coupling, flux_weights):
    nodes, classes, cells = melt.shape
    chunks = cells // LANES
    f32 = jnp.float32
    split = (chunks, nodes * classes, LANES)
    whole = pltpu.CompilerParams(vmem_limit_bytes=60 * 2**20)
    little = pltpu.CompilerParams(vmem_limit_bytes=32 * 2**20)
    cls_count = lax.axis_size("cls")
    cell_count = lax.axis_size("cell")
    prop_v = pltpu.VMEM((classes, nodes, nodes), f32)
    small = pltpu.VMEM((classes, nodes), f32)
    parts = nodes // GROUP
    packed = pl.pallas_call(
        fields_kernel,
        out_shape=jax.ShapeDtypeStruct((cls_count, FIELDS, chunks, LANES), f32),
        in_specs=[HBM] * 6,
        out_specs=VMEM,
        scratch_shapes=[
            pltpu.VMEM(melt.shape, f32),
            pltpu.VMEM(counts.shape, counts.dtype),
            pltpu.VMEM(pressure.shape, f32),
            prop_v,
            small,
            small,
            DMA((parts,)),
            DMA((5,)),
        ],
        compiler_params=whole,
        name="fields",
    )(melt, counts, pressure, propagator, coupling, flux_weights)
    shells, done = pl.pallas_call(
        power_kernel,
        out_shape=[
            jax.ShapeDtypeStruct((chunks + 1,) + split[1:], f32),
            jax.ShapeDtypeStruct((GROUP, LANES), f32),
        ],
        in_specs=[HBM] * 3,
        out_specs=[HBM, VMEM],
        scratch_shapes=[
            pltpu.VMEM(split, f32),
            pltpu.VMEM((chunks + 1,) + split[1:], f32),
            prop_v,
            small,
            DMA((chunks,)),
            DMA((chunks + 1,)),
            DMA((2,)),
        ],
        compiler_params=whole,
        cost_estimate=pl.CostEstimate(flops=2 * 10**9, bytes_accessed=2 * melt.size * 4, transcendentals=0),
        name="power",
    )(melt.reshape(nodes * classes, cells), propagator, coupling)
    fields = pl.pallas_call(
        combine_kernel,
        out_shape=jax.ShapeDtypeStruct((FIELDS - 1, chunks, LANES), f32),
        in_specs=[VMEM, VMEM],
        out_specs=VMEM,
        compiler_params=little,
        name="combine",
    )(exchange(packed, "cls"), done)
    window = lax.all_gather(fields, "cell", axis=0)
    rows = cell_count * chunks
    return pl.pallas_call(
        finish_kernel,
        out_shape=[jax.ShapeDtypeStruct(melt.shape, f32), jax.ShapeDtypeStruct(pressure.shape, f32)],
        in_specs=[VMEM, VMEM],
        out_specs=[HBM, VMEM],
        scratch_shapes=[
            pltpu.VMEM(melt.shape, f32),
            pltpu.VMEM((SUBSTEPS, rows, LANES), f32),
            pltpu.VMEM((rows, LANES), f32),
            DMA((parts,)),
        ],
        compiler_params=little,
        name="finish",
    )(window, shells)


def solution(mesh):
    placed = (P(None, "cls", "cell"), P("cls", "cell"), P(("cell", "cls"), None), P(), P(), P())
    return jax.shard_map(
        shards,
        mesh=mesh,
        in_specs=placed,
        out_specs=(P(None, "cls", "cell"), P(("cell", "cls"), None)),
        check_vma=False,
    )
```

```python
import functools

import jax
import jax.numpy as jnp
from jax import lax
from jax.experimental import pallas as pl
from jax.experimental.pallas import tpu as pltpu
from jax.sharding import PartitionSpec as P

CLASSES = 32
SIDE = 16
SUBSTEPS = 4
COUNT_SCALE = 400.0
LANES = 128
GROUP = 8
FIELDS = 2 * SUBSTEPS + 1


def grow(value, factor, times):
    for _ in range(times):
        value = value * factor
    return value


def iota(shape, dim):
    return lax.broadcasted_iota(jnp.int32, shape, dim)


def split2(x):
    high = x.astype(jnp.bfloat16)
    return high, (x - high.astype(jnp.float32)).astype(jnp.bfloat16)


def dot(a, b):
    return jnp.dot(a, b, preferred_element_type=jnp.float32)


def left_of(x):
    high, low = split2(x)
    return jnp.concatenate([high, high, low], axis=1)


def right_of(x):
    high, low = split2(x)
    return jnp.concatenate([high, low, high], axis=0)


def class_scale(prop):
    rows = [jnp.max(jnp.abs(prop[k]), axis=0, keepdims=True) for k in range(prop.shape[0])]
    return jnp.maximum(1.0, jnp.max(jnp.concatenate(rows, axis=0), axis=1, keepdims=True))


def param_copies(pairs, sems):
    copies = []
    for n, (source, target) in enumerate(pairs):
        own = pl.ds(lax.axis_index("cls") * target.shape[0], target.shape[0])
        copies.append(pltpu.make_async_copy(source.at[own], target, sems.at[n]))
    return copies


def fields_kernel(
    melt_hbm, counts_hbm, pressure_hbm, prop_hbm, coup_hbm, flux_hbm, out, melt, counts, pressure, prop, coup, flux, sems, other_sems
):
    nodes, classes, cells = melt.shape
    first = param_copies([(prop_hbm, prop), (flux_hbm, flux), (coup_hbm, coup)], other_sems)
    for copy in first:
        copy.start()
    parts = nodes // GROUP
    pieces = [
        pltpu.make_async_copy(
            melt_hbm.at[pl.ds(g * GROUP, GROUP)], melt.at[pl.ds(g * GROUP, GROUP)], sems.at[g]
        )
        for g in range(parts)
    ]
    for piece in pieces:
        piece.start()
    rest = [
        pltpu.make_async_copy(counts_hbm, counts, other_sems.at[3]),
        pltpu.make_async_copy(pressure_hbm, pressure, other_sems.at[4]),
    ]
    for copy in rest:
        copy.start()
    for copy in first:
        copy.wait()
    scale = class_scale(prop)
    width = classes * nodes
    table = jnp.concatenate(split2(prop[...].reshape(width, nodes)), axis=1)
    inverse = 1.0 / scale
    mask = iota((classes, width), 1) // nodes == iota((classes, width), 0)
    rows = [flux[...]]
    for _ in range(SUBSTEPS):
        wide = jnp.where(mask, jnp.concatenate([rows[-1]] * classes, axis=1), 0.0)
        pairs = dot(jnp.concatenate(split2(wide), axis=0), table)
        row = pairs[:classes] + pairs[classes:]
        rows.append((row[:, :nodes] + row[:, nodes:]) * inverse)
    spread = [
        grow(jnp.sum(rows[d] * coup[...], axis=1, keepdims=True), scale, d) for d in range(SUBSTEPS)
    ]
    for copy in rest:
        copy.wait()
    counts_n = counts[...].astype(jnp.float32) / (COUNT_SCALE * CLASSES)
    chunks = cells // LANES
    sums = [[jnp.zeros((classes, LANES), jnp.float32) for _ in range(chunks)] for _ in range(SUBSTEPS)]
    for g in range(parts):
        pieces[g].wait()
        for j in range(g * GROUP, (g + 1) * GROUP):
            weights = [
                jnp.broadcast_to(rows[t + 1][:, j : j + 1], (classes, LANES)) for t in range(SUBSTEPS)
            ]
            for r in range(chunks):
                value = melt[j, :, r * LANES : (r + 1) * LANES]
                for t in range(SUBSTEPS):
                    sums[t][r] = sums[t][r] + weights[t] * value
    every = range(out.shape[0])
    for n in every:
        out[n, 2 * SUBSTEPS] = jnp.zeros((chunks, LANES), jnp.float32)
    for r in range(chunks):
        here = counts_n[:, r * LANES : (r + 1) * LANES]
        for t in range(SUBSTEPS):
            row = jnp.sum(grow(here * sums[t][r], scale, t + 1), axis=0, keepdims=True)
            for n in every:
                out[n, t, r : r + 1, :] = row
        for d in range(SUBSTEPS):
            row = jnp.sum(here * spread[d], axis=0, keepdims=True)
            for n in every:
                out[n, SUBSTEPS + d, r : r + 1, :] = row
    per = pressure.shape[1] // LANES
    tile = pressure.shape[0] * per
    at = lax.axis_index("cls") * tile
    for i in range(tile):
        row = pressure[i // per : i // per + 1, (i % per) * LANES : (i % per + 1) * LANES]
        for n in every:
            out[n, 2 * SUBSTEPS, pl.ds(at + i, 1), :] = row


def power_kernel(melt_hbm, prop_hbm, coup_hbm, out, melt, prop, coup, sems, param_sems):
    chunks = melt.shape[0]
    classes, nodes = prop.shape[:2]
    params = param_copies([(prop_hbm, prop), (coup_hbm, coup)], param_sems)
    for copy in params:
        copy.start()
    loads = [
        pltpu.make_async_copy(melt_hbm.at[:, pl.ds(r * LANES, LANES)], melt.at[r], sems.at[r])
        for r in range(chunks)
    ]
    for load in loads:
        load.start()
    for copy in params:
        copy.wait()
    scale = class_scale(prop)
    inverse = 1.0 / scale
    every = range(classes)
    factors = [scale[k : k + 1, :] for k in every]
    unit = [prop[k] * inverse[k : k + 1, :] for k in every]
    first = [left_of(unit[k]) for k in every]
    square = [dot(first[k], right_of(unit[k])) for k in every]
    second = [left_of(square[k]) for k in every]
    lefts = [left_of(dot(second[k], right_of(square[k]))) for k in every]
    start = jnp.concatenate(
        [jnp.transpose(coup[...]), jnp.zeros((nodes, LANES - classes), jnp.float32)], axis=1
    )
    once = [dot(first[k], right_of(start)) for k in every]
    start = start[:, :classes]
    twice = [
        dot(second[k], right_of(jnp.concatenate([start, once[k][:, :classes]], axis=1))) for k in every
    ]
    lane = iota((nodes, LANES), 1)
    for k in every:
        powers = [
            start[:, k : k + 1],
            once[k][:, k : k + 1],
            twice[k][:, k : k + 1],
            twice[k][:, classes + k : classes + k + 1],
        ]
        value = jnp.zeros((nodes, LANES), jnp.float32)
        for d in range(SUBSTEPS):
            value = jnp.where(lane % SUBSTEPS == SUBSTEPS - 1 - d, grow(powers[d], factors[k], d), value)
        high = value.astype(jnp.bfloat16).astype(jnp.float32)
        value = jnp.where(lane < 2 * SUBSTEPS, high, jnp.where(lane < 3 * SUBSTEPS, value - high, 0.0))
        out[chunks, pl.ds(k, nodes, stride=classes), :] = value
    together = 2 if chunks % 2 == 0 else 1
    for r in range(0, chunks, together):
        for n in range(together):
            loads[r + n].wait()
        for k in every:
            own = pl.ds(k, nodes, stride=classes)
            x = jnp.concatenate([melt[r + n, own, :] for n in range(together)], axis=1)
            part = grow(dot(lefts[k], right_of(x)), factors[k], SUBSTEPS)
            for n in range(together):
                out[r + n, own, :] = part[:, n * LANES : (n + 1) * LANES]


def combine_kernel(parts, _, out):
    total = parts[0]
    for n in range(1, parts.shape[0]):
        total = total + parts[n]
    wall = 0.5 * total[2 * SUBSTEPS]
    for t in range(SUBSTEPS):
        out[t] = total[t] + total[SUBSTEPS + t] * wall
    for d in range(SUBSTEPS - 1):
        out[SUBSTEPS + d] = total[SUBSTEPS + d]
    out[2 * SUBSTEPS - 1] = total[2 * SUBSTEPS]


def total_of(x):
    tiles = jnp.sum(x.reshape(-1, GROUP, LANES), axis=0)
    return jnp.sum(jnp.sum(tiles, axis=1, keepdims=True), axis=0, keepdims=True)


def laplacian(x, plane):
    rows = x.shape[0]
    row = iota(x.shape, 0)
    lane = iota(x.shape, 1)
    per = plane // LANES
    inside = row % per * LANES + lane
    col = lane % SIDE
    total = jnp.where(col == 0, 0.0, pltpu.roll(x, 1, 1))
    total += jnp.where(col == SIDE - 1, 0.0, pltpu.roll(x, LANES - 1, 1))
    up = pltpu.roll(x, SIDE, 1)
    up = jnp.where(lane < SIDE, pltpu.roll(up, 1, 0), up)
    total += jnp.where(inside < SIDE, 0.0, up)
    down = pltpu.roll(x, LANES - SIDE, 1)
    down = jnp.where(lane >= LANES - SIDE, pltpu.roll(down, rows - 1, 0), down)
    total += jnp.where(inside >= plane - SIDE, 0.0, down)
    total += jnp.where(row < per, 0.0, pltpu.roll(x, per, 0))
    total += jnp.where(row >= rows - per, 0.0, pltpu.roll(x, rows - per, 0))
    return total - 6.0 * x


def finish_kernel(
    window, shells, out_hbm, pressure_out, out, walls_all, last, out_sems
):
    nodes, classes, cells = out.shape
    chunks = cells // LANES
    parts = nodes // GROUP
    width = GROUP * classes

    def piece(g):
        return pl.ds(g * GROUP, GROUP)

    plane = pressure_out.shape[1]
    blocks = window.shape[0]
    rows = blocks * chunks

    def field_of(f):
        return window[:, f].reshape(rows, LANES)

    field = field_of(2 * SUBSTEPS - 1)
    answer = field_of(SUBSTEPS)
    answer_total = total_of(answer)
    chamber = None
    walls = []
    for t in range(SUBSTEPS):
        gas = field_of(t)
        for s in range(1, t):
            gas = gas + field_of(SUBSTEPS + t - s) * walls[s]
        if t:
            gas = gas + answer * (0.5 * field)
        total = total_of(gas)
        if t:
            field = field + 0.2 * chamber
            gas = gas + answer * (0.1 * chamber)
            total = total + answer_total * (0.1 * chamber)
        walls.append(0.5 * field)
        walls_all[t] = walls[t]
        field = 0.8 * field + 0.15 * laplacian(field, plane) + 0.1 * gas
        chamber = 1.5 - 0.5 * total / (rows * LANES)
    last[...] = field + 0.2 * chamber
    cell = lax.axis_index("cell")
    first = cell * chunks
    tile = pressure_out.shape[0] * plane // LANES
    per = plane // LANES
    at = first + lax.axis_index("cls") * tile
    for i in range(tile):
        pressure_out[i // per : i // per + 1, (i % per) * LANES : (i % per + 1) * LANES] = last[
            pl.ds(at + i, 1), :
        ]
    right = []
    for r in range(chunks):
        wall = jnp.concatenate([walls_all[s, pl.ds(first + r, 1), :] for s in range(SUBSTEPS)], axis=0)
        high = wall.astype(jnp.bfloat16).astype(jnp.float32)
        right.append(jnp.concatenate([high, wall - high, high, jnp.zeros_like(high)], axis=0))
    right = jnp.concatenate(right, axis=1).astype(jnp.bfloat16)
    stores = [
        pltpu.make_async_copy(out.at[piece(g)], out_hbm.at[piece(g)], out_sems.at[g]) for g in range(parts)
    ]
    for g in range(parts):
        here = slice(g * width, (g + 1) * width)
        change = dot(shells[chunks, here, : 4 * SUBSTEPS].astype(jnp.bfloat16), right)
        for r in range(chunks):
            lanes = slice(r * LANES, (r + 1) * LANES)
            value = shells[r, here, :] + change[:, lanes]
            out[g * GROUP : (g + 1) * GROUP, :, lanes] = value.reshape(GROUP, classes, LANES)
        stores[g].start()
    for store in stores:
        store.wait()


HBM = pl.BlockSpec(memory_space=pltpu.HBM)
VMEM = pl.BlockSpec(memory_space=pltpu.VMEM)
DMA = pltpu.SemaphoreType.DMA


def exchange(copies, axis):
    return lax.all_to_all(copies, axis, split_axis=0, concat_axis=0, tiled=True)


def shards(melt, counts, pressure, propagator, coupling, flux_weights):
    nodes, classes, cells = melt.shape
    chunks = cells // LANES
    f32 = jnp.float32
    split = (chunks, nodes * classes, LANES)
    whole = pltpu.CompilerParams(vmem_limit_bytes=60 * 2**20)
    most = pltpu.CompilerParams(vmem_limit_bytes=48 * 2**20)
    little = pltpu.CompilerParams(vmem_limit_bytes=32 * 2**20)
    cls_count = lax.axis_size("cls")
    cell_count = lax.axis_size("cell")
    prop_v = pltpu.VMEM((classes, nodes, nodes), f32)
    small = pltpu.VMEM((classes, nodes), f32)
    parts = nodes // GROUP
    packed = pl.pallas_call(
        fields_kernel,
        out_shape=jax.ShapeDtypeStruct((cls_count, FIELDS, chunks, LANES), f32),
        in_specs=[HBM] * 6,
        out_specs=VMEM,
        scratch_shapes=[
            pltpu.VMEM(melt.shape, f32),
            pltpu.VMEM(counts.shape, counts.dtype),
            pltpu.VMEM(pressure.shape, f32),
            prop_v,
            small,
            small,
            DMA((parts,)),
            DMA((5,)),
        ],
        compiler_params=whole,
        name="fields",
    )(melt, counts, pressure, propagator, coupling, flux_weights)
    shells = pl.pallas_call(
        power_kernel,
        out_shape=jax.ShapeDtypeStruct((chunks + 1,) + split[1:], f32),
        in_specs=[HBM] * 3,
        out_specs=VMEM,
        scratch_shapes=[
            pltpu.VMEM(split, f32),
            prop_v,
            small,
            DMA((chunks,)),
            DMA((2,)),
        ],
        compiler_params=most,
        cost_estimate=pl.CostEstimate(flops=2 * 10**9, bytes_accessed=2 * melt.size * 4, transcendentals=0),
        name="power",
    )(melt.reshape(nodes * classes, cells), propagator, coupling)
    fields = pl.pallas_call(
        combine_kernel,
        out_shape=jax.ShapeDtypeStruct((FIELDS - 1, chunks, LANES), f32),
        in_specs=[VMEM, VMEM],
        out_specs=VMEM,
        compiler_params=little,
        name="combine",
    )(exchange(packed, "cls"), shells)
    window = lax.all_gather(fields, "cell", axis=0)
    rows = cell_count * chunks
    return pl.pallas_call(
        finish_kernel,
        out_shape=[jax.ShapeDtypeStruct(melt.shape, f32), jax.ShapeDtypeStruct(pressure.shape, f32)],
        in_specs=[VMEM, VMEM],
        out_specs=[HBM, VMEM],
        scratch_shapes=[
            pltpu.VMEM(melt.shape, f32),
            pltpu.VMEM((SUBSTEPS, rows, LANES), f32),
            pltpu.VMEM((rows, LANES), f32),
            DMA((parts,)),
        ],
        compiler_params=little,
        name="finish",
    )(window, shells)


def solution(mesh):
    placed = (P(None, "cls", "cell"), P("cls", "cell"), P(("cell", "cls"), None), P(), P(), P())
    return jax.shard_map(
        shards,
        mesh=mesh,
        in_specs=placed,
        out_specs=(P(None, "cls", "cell"), P(("cell", "cls"), None)),
        check_vma=False,
    )
```

```python
import functools

import jax
import jax.numpy as jnp
from jax import lax
from jax.experimental import pallas as pl
from jax.experimental.pallas import tpu as pltpu
from jax.sharding import PartitionSpec as P

CLASSES = 32
SIDE = 16
SUBSTEPS = 4
COUNT_SCALE = 400.0
LANES = 128
GROUP = 8
FIELDS = 2 * SUBSTEPS + 1


def grow(value, factor, times):
    for _ in range(times):
        value = value * factor
    return value


def iota(shape, dim):
    return lax.broadcasted_iota(jnp.int32, shape, dim)


def split2(x):
    high = x.astype(jnp.bfloat16)
    return high, (x - high.astype(jnp.float32)).astype(jnp.bfloat16)


def dot(a, b):
    return jnp.dot(a, b, preferred_element_type=jnp.float32)


def left_of(x):
    high, low = split2(x)
    return jnp.concatenate([high, high, low], axis=1)


def right_of(x):
    high, low = split2(x)
    return jnp.concatenate([high, low, high], axis=0)


def class_scale(prop):
    rows = [jnp.max(jnp.abs(prop[k]), axis=0, keepdims=True) for k in range(prop.shape[0])]
    return jnp.maximum(1.0, jnp.max(jnp.concatenate(rows, axis=0), axis=1, keepdims=True))


def param_copies(pairs, sems):
    copies = []
    for n, (source, target) in enumerate(pairs):
        own = pl.ds(lax.axis_index("cls") * target.shape[0], target.shape[0])
        copies.append(pltpu.make_async_copy(source.at[own], target, sems.at[n]))
    return copies


def fields_kernel(
    melt_hbm, counts_hbm, pressure_hbm, prop_hbm, coup_hbm, flux_hbm, out, melt, highs, lows, counts, pressure, prop, coup, flux, sems, other_sems
):
    nodes, classes, cells = melt.shape
    first = param_copies([(prop_hbm, prop), (flux_hbm, flux), (coup_hbm, coup)], other_sems)
    for copy in first:
        copy.start()
    parts = nodes // GROUP
    pieces = [
        pltpu.make_async_copy(
            melt_hbm.at[pl.ds(g * GROUP, GROUP)], melt.at[pl.ds(g * GROUP, GROUP)], sems.at[g]
        )
        for g in range(parts)
    ]
    for piece in pieces:
        piece.start()
    rest = [
        pltpu.make_async_copy(counts_hbm, counts, other_sems.at[3]),
        pltpu.make_async_copy(pressure_hbm, pressure, other_sems.at[4]),
    ]
    for copy in rest:
        copy.start()
    for copy in first:
        copy.wait()
    scale = class_scale(prop)
    width = classes * nodes
    table = jnp.concatenate(split2(prop[...].reshape(width, nodes)), axis=1)
    inverse = 1.0 / scale
    mask = iota((classes, width), 1) // nodes == iota((classes, width), 0)
    rows = [flux[...]]
    tall = GROUP * classes
    each = parts // SUBSTEPS
    for t in range(SUBSTEPS):
        wide = jnp.where(mask, jnp.concatenate([rows[-1]] * classes, axis=1), 0.0)
        pairs = dot(jnp.concatenate(split2(wide), axis=0), table)
        row = pairs[:classes] + pairs[classes:]
        rows.append((row[:, :nodes] + row[:, nodes:]) * inverse)
        for g in range(t * each, parts if t == SUBSTEPS - 1 else (t + 1) * each):
            pieces[g].wait()
            here = slice(g * tall, (g + 1) * tall)
            highs[here, :], lows[here, :] = split2(
                melt[g * GROUP : (g + 1) * GROUP].reshape(tall, cells)
            )
    spread_out = (iota((nodes, width), 1) // classes == iota((nodes, width), 0)).astype(jnp.bfloat16)
    parts_of_rows = jnp.concatenate(split2(jnp.concatenate(rows[1:], axis=0)), axis=0)
    dense = dot(parts_of_rows, spread_out)
    same = iota(dense.shape, 0) % classes == iota(dense.shape, 1) % classes
    dense = jnp.where(same, dense, 0.0).astype(jnp.bfloat16)
    count = SUBSTEPS * classes
    fluxes = dot(dense, highs[...])
    fluxes = fluxes[:count] + fluxes[count:] + dot(dense[:count], lows[...])
    spread = [
        grow(jnp.sum(rows[d] * coup[...], axis=1, keepdims=True), scale, d) for d in range(SUBSTEPS)
    ]
    for copy in rest:
        copy.wait()
    counts_n = counts[...].astype(jnp.float32) / (COUNT_SCALE * CLASSES)
    chunks = cells // LANES
    every = range(out.shape[0])
    for n in every:
        out[n, 2 * SUBSTEPS] = jnp.zeros((chunks, LANES), jnp.float32)
    for r in range(chunks):
        here = counts_n[:, r * LANES : (r + 1) * LANES]
        for t in range(SUBSTEPS):
            part = fluxes[t * classes : (t + 1) * classes, r * LANES : (r + 1) * LANES]
            row = jnp.sum(grow(here * part, scale, t + 1), axis=0, keepdims=True)
            for n in every:
                out[n, t, r : r + 1, :] = row
        for d in range(SUBSTEPS):
            row = jnp.sum(here * spread[d], axis=0, keepdims=True)
            for n in every:
                out[n, SUBSTEPS + d, r : r + 1, :] = row
    per = pressure.shape[1] // LANES
    tile = pressure.shape[0] * per
    at = lax.axis_index("cls") * tile
    for i in range(tile):
        row = pressure[i // per : i // per + 1, (i % per) * LANES : (i % per + 1) * LANES]
        for n in every:
            out[n, 2 * SUBSTEPS, pl.ds(at + i, 1), :] = row


def power_kernel(melt_hbm, prop_hbm, coup_hbm, out, melt, prop, coup, sems, param_sems):
    chunks = melt.shape[0]
    classes, nodes = prop.shape[:2]
    params = param_copies([(prop_hbm, prop), (coup_hbm, coup)], param_sems)
    for copy in params:
        copy.start()
    loads = [
        pltpu.make_async_copy(melt_hbm.at[:, pl.ds(r * LANES, LANES)], melt.at[r], sems.at[r])
        for r in range(chunks)
    ]
    for load in loads:
        load.start()
    for copy in params:
        copy.wait()
    scale = class_scale(prop)
    inverse = 1.0 / scale
    every = range(classes)
    factors = [scale[k : k + 1, :] for k in every]
    unit = [prop[k] * inverse[k : k + 1, :] for k in every]
    first = [left_of(unit[k]) for k in every]
    square = [dot(first[k], right_of(unit[k])) for k in every]
    second = [left_of(square[k]) for k in every]
    lefts = [left_of(dot(second[k], right_of(square[k]))) for k in every]
    start = jnp.concatenate(
        [jnp.transpose(coup[...]), jnp.zeros((nodes, LANES - classes), jnp.float32)], axis=1
    )
    once = [dot(first[k], right_of(start)) for k in every]
    start = start[:, :classes]
    twice = [
        dot(second[k], right_of(jnp.concatenate([start, once[k][:, :classes]], axis=1))) for k in every
    ]
    lane = iota((nodes, LANES), 1)
    for k in every:
        powers = [
            start[:, k : k + 1],
            once[k][:, k : k + 1],
            twice[k][:, k : k + 1],
            twice[k][:, classes + k : classes + k + 1],
        ]
        value = jnp.zeros((nodes, LANES), jnp.float32)
        for d in range(SUBSTEPS):
            value = jnp.where(lane % SUBSTEPS == SUBSTEPS - 1 - d, grow(powers[d], factors[k], d), value)
        high = value.astype(jnp.bfloat16).astype(jnp.float32)
        value = jnp.where(lane < 2 * SUBSTEPS, high, jnp.where(lane < 3 * SUBSTEPS, value - high, 0.0))
        out[chunks, pl.ds(k, nodes, stride=classes), :] = value
    together = 2 if chunks % 2 == 0 else 1
    for r in range(0, chunks, together):
        for n in range(together):
            loads[r + n].wait()
        for k in every:
            own = pl.ds(k, nodes, stride=classes)
            x = jnp.concatenate([melt[r + n, own, :] for n in range(together)], axis=1)
            part = grow(dot(lefts[k], right_of(x)), factors[k], SUBSTEPS)
            for n in range(together):
                out[r + n, own, :] = part[:, n * LANES : (n + 1) * LANES]


def combine_kernel(parts, _, out):
    total = parts[0]
    for n in range(1, parts.shape[0]):
        total = total + parts[n]
    wall = 0.5 * total[2 * SUBSTEPS]
    for t in range(SUBSTEPS):
        out[t] = total[t] + total[SUBSTEPS + t] * wall
    for d in range(SUBSTEPS - 1):
        out[SUBSTEPS + d] = total[SUBSTEPS + d]
    out[2 * SUBSTEPS - 1] = total[2 * SUBSTEPS]


def total_of(x):
    tiles = jnp.sum(x.reshape(-1, GROUP, LANES), axis=0)
    return jnp.sum(jnp.sum(tiles, axis=1, keepdims=True), axis=0, keepdims=True)


def laplacian(x, plane):
    rows = x.shape[0]
    row = iota(x.shape, 0)
    lane = iota(x.shape, 1)
    per = plane // LANES
    inside = row % per * LANES + lane
    col = lane % SIDE
    total = jnp.where(col == 0, 0.0, pltpu.roll(x, 1, 1))
    total += jnp.where(col == SIDE - 1, 0.0, pltpu.roll(x, LANES - 1, 1))
    up = pltpu.roll(x, SIDE, 1)
    up = jnp.where(lane < SIDE, pltpu.roll(up, 1, 0), up)
    total += jnp.where(inside < SIDE, 0.0, up)
    down = pltpu.roll(x, LANES - SIDE, 1)
    down = jnp.where(lane >= LANES - SIDE, pltpu.roll(down, rows - 1, 0), down)
    total += jnp.where(inside >= plane - SIDE, 0.0, down)
    total += jnp.where(row < per, 0.0, pltpu.roll(x, per, 0))
    total += jnp.where(row >= rows - per, 0.0, pltpu.roll(x, rows - per, 0))
    return total - 6.0 * x


def finish_kernel(
    window, shells, out_hbm, pressure_out, out, walls_all, last, out_sems
):
    nodes, classes, cells = out.shape
    chunks = cells // LANES
    parts = nodes // GROUP
    width = GROUP * classes

    def piece(g):
        return pl.ds(g * GROUP, GROUP)

    plane = pressure_out.shape[1]
    blocks = window.shape[0]
    rows = blocks * chunks

    def field_of(f):
        return window[:, f].reshape(rows, LANES)

    field = field_of(2 * SUBSTEPS - 1)
    answer = field_of(SUBSTEPS)
    answer_total = total_of(answer)
    chamber = None
    walls = []
    for t in range(SUBSTEPS):
        gas = field_of(t)
        for s in range(1, t):
            gas = gas + field_of(SUBSTEPS + t - s) * walls[s]
        if t:
            gas = gas + answer * (0.5 * field)
        total = total_of(gas)
        if t:
            field = field + 0.2 * chamber
            gas = gas + answer * (0.1 * chamber)
            total = total + answer_total * (0.1 * chamber)
        walls.append(0.5 * field)
        walls_all[t] = walls[t]
        field = 0.8 * field + 0.15 * laplacian(field, plane) + 0.1 * gas
        chamber = 1.5 - 0.5 * total / (rows * LANES)
    last[...] = field + 0.2 * chamber
    cell = lax.axis_index("cell")
    first = cell * chunks
    tile = pressure_out.shape[0] * plane // LANES
    per = plane // LANES
    at = first + lax.axis_index("cls") * tile
    for i in range(tile):
        pressure_out[i // per : i // per + 1, (i % per) * LANES : (i % per + 1) * LANES] = last[
            pl.ds(at + i, 1), :
        ]
    right = []
    for r in range(chunks):
        wall = jnp.concatenate([walls_all[s, pl.ds(first + r, 1), :] for s in range(SUBSTEPS)], axis=0)
        high = wall.astype(jnp.bfloat16).astype(jnp.float32)
        right.append(jnp.concatenate([high, wall - high, high, jnp.zeros_like(high)], axis=0))
    right = jnp.concatenate(right, axis=1).astype(jnp.bfloat16)
    stores = [
        pltpu.make_async_copy(out.at[piece(g)], out_hbm.at[piece(g)], out_sems.at[g]) for g in range(parts)
    ]
    for g in range(parts):
        here = slice(g * width, (g + 1) * width)
        change = dot(shells[chunks, here, : 4 * SUBSTEPS].astype(jnp.bfloat16), right)
        for r in range(chunks):
            lanes = slice(r * LANES, (r + 1) * LANES)
            value = shells[r, here, :] + change[:, lanes]
            out[g * GROUP : (g + 1) * GROUP, :, lanes] = value.reshape(GROUP, classes, LANES)
        stores[g].start()
    for store in stores:
        store.wait()


HBM = pl.BlockSpec(memory_space=pltpu.HBM)
VMEM = pl.BlockSpec(memory_space=pltpu.VMEM)
DMA = pltpu.SemaphoreType.DMA


def exchange(copies, axis):
    return lax.all_to_all(copies, axis, split_axis=0, concat_axis=0, tiled=True)


def shards(melt, counts, pressure, propagator, coupling, flux_weights):
    nodes, classes, cells = melt.shape
    chunks = cells // LANES
    f32 = jnp.float32
    split = (chunks, nodes * classes, LANES)
    whole = pltpu.CompilerParams(vmem_limit_bytes=60 * 2**20)
    most = pltpu.CompilerParams(vmem_limit_bytes=48 * 2**20)
    little = pltpu.CompilerParams(vmem_limit_bytes=32 * 2**20)
    cls_count = lax.axis_size("cls")
    cell_count = lax.axis_size("cell")
    prop_v = pltpu.VMEM((classes, nodes, nodes), f32)
    small = pltpu.VMEM((classes, nodes), f32)
    parts = nodes // GROUP
    packed = pl.pallas_call(
        fields_kernel,
        out_shape=jax.ShapeDtypeStruct((cls_count, FIELDS, chunks, LANES), f32),
        in_specs=[HBM] * 6,
        out_specs=VMEM,
        scratch_shapes=[
            pltpu.VMEM(melt.shape, f32),
            pltpu.VMEM((nodes * classes, cells), jnp.bfloat16),
            pltpu.VMEM((nodes * classes, cells), jnp.bfloat16),
            pltpu.VMEM(counts.shape, counts.dtype),
            pltpu.VMEM(pressure.shape, f32),
            prop_v,
            small,
            small,
            DMA((parts,)),
            DMA((5,)),
        ],
        compiler_params=whole,
        name="fields",
    )(melt, counts, pressure, propagator, coupling, flux_weights)
    shells = pl.pallas_call(
        power_kernel,
        out_shape=jax.ShapeDtypeStruct((chunks + 1,) + split[1:], f32),
        in_specs=[HBM] * 3,
        out_specs=VMEM,
        scratch_shapes=[
            pltpu.VMEM(split, f32),
            prop_v,
            small,
            DMA((chunks,)),
            DMA((2,)),
        ],
        compiler_params=most,
        cost_estimate=pl.CostEstimate(flops=2 * 10**9, bytes_accessed=2 * melt.size * 4, transcendentals=0),
        name="power",
    )(melt.reshape(nodes * classes, cells), propagator, coupling)
    fields = pl.pallas_call(
        combine_kernel,
        out_shape=jax.ShapeDtypeStruct((FIELDS - 1, chunks, LANES), f32),
        in_specs=[VMEM, VMEM],
        out_specs=VMEM,
        compiler_params=little,
        name="combine",
    )(exchange(packed, "cls"), shells)
    window = lax.all_gather(fields, "cell", axis=0)
    rows = cell_count * chunks
    return pl.pallas_call(
        finish_kernel,
        out_shape=[jax.ShapeDtypeStruct(melt.shape, f32), jax.ShapeDtypeStruct(pressure.shape, f32)],
        in_specs=[VMEM, VMEM],
        out_specs=[HBM, VMEM],
        scratch_shapes=[
            pltpu.VMEM(melt.shape, f32),
            pltpu.VMEM((SUBSTEPS, rows, LANES), f32),
            pltpu.VMEM((rows, LANES), f32),
            DMA((parts,)),
        ],
        compiler_params=little,
        name="finish",
    )(window, shells)


def solution(mesh):
    placed = (P(None, "cls", "cell"), P("cls", "cell"), P(("cell", "cls"), None), P(), P(), P())
    return jax.shard_map(
        shards,
        mesh=mesh,
        in_specs=placed,
        out_specs=(P(None, "cls", "cell"), P(("cell", "cls"), None)),
        check_vma=False,
    )
```

```python
import functools

import jax
import jax.numpy as jnp
from jax import lax
from jax.experimental import pallas as pl
from jax.experimental.pallas import tpu as pltpu
from jax.sharding import PartitionSpec as P

CLASSES = 32
SIDE = 16
SUBSTEPS = 4
COUNT_SCALE = 400.0
LANES = 128
GROUP = 8
FIELDS = 2 * SUBSTEPS


def grow(value, factor, times):
    for _ in range(times):
        value = value * factor
    return value


def iota(shape, dim):
    return lax.broadcasted_iota(jnp.int32, shape, dim)


def split2(x):
    high = x.astype(jnp.bfloat16)
    return high, (x - high.astype(jnp.float32)).astype(jnp.bfloat16)


def dot(a, b):
    return jnp.dot(a, b, preferred_element_type=jnp.float32)


def left_of(x):
    high, low = split2(x)
    return jnp.concatenate([high, high, low], axis=1)


def right_of(x):
    high, low = split2(x)
    return jnp.concatenate([high, low, high], axis=0)


def class_scale(prop):
    rows = [jnp.max(jnp.abs(prop[k]), axis=0, keepdims=True) for k in range(prop.shape[0])]
    return jnp.maximum(1.0, jnp.max(jnp.concatenate(rows, axis=0), axis=1, keepdims=True))


def param_copies(pairs, sems):
    copies = []
    for n, (source, target) in enumerate(pairs):
        own = pl.ds(lax.axis_index("cls") * target.shape[0], target.shape[0])
        copies.append(pltpu.make_async_copy(source.at[own], target, sems.at[n]))
    return copies


def fields_kernel(
    melt_hbm, counts_hbm, pressure_hbm, prop_hbm, coup_hbm, flux_hbm, out, melt, highs, lows, counts, pressure, prop, coup, flux, sems, other_sems
):
    nodes, classes, cells = melt.shape
    first = param_copies([(prop_hbm, prop), (flux_hbm, flux), (coup_hbm, coup)], other_sems)
    for copy in first:
        copy.start()
    parts = nodes // GROUP
    pieces = [
        pltpu.make_async_copy(
            melt_hbm.at[pl.ds(g * GROUP, GROUP)], melt.at[pl.ds(g * GROUP, GROUP)], sems.at[g]
        )
        for g in range(parts)
    ]
    for piece in pieces:
        piece.start()
    rest = [
        pltpu.make_async_copy(counts_hbm, counts, other_sems.at[3]),
        pltpu.make_async_copy(pressure_hbm, pressure, other_sems.at[4]),
    ]
    for copy in rest:
        copy.start()
    for copy in first:
        copy.wait()
    scale = class_scale(prop)
    width = classes * nodes
    table = jnp.concatenate(split2(prop[...].reshape(width, nodes)), axis=1)
    inverse = 1.0 / scale
    mask = iota((classes, width), 1) // nodes == iota((classes, width), 0)
    rows = [flux[...]]
    tall = GROUP * classes
    each = parts // SUBSTEPS
    for t in range(SUBSTEPS):
        wide = jnp.where(mask, jnp.concatenate([rows[-1]] * classes, axis=1), 0.0)
        pairs = dot(jnp.concatenate(split2(wide), axis=0), table)
        row = pairs[:classes] + pairs[classes:]
        rows.append((row[:, :nodes] + row[:, nodes:]) * inverse)
        for g in range(t * each, parts if t == SUBSTEPS - 1 else (t + 1) * each):
            pieces[g].wait()
            here = slice(g * tall, (g + 1) * tall)
            highs[here, :], lows[here, :] = split2(
                melt[g * GROUP : (g + 1) * GROUP].reshape(tall, cells)
            )
    spread_out = (iota((nodes, width), 1) // classes == iota((nodes, width), 0)).astype(jnp.bfloat16)
    parts_of_rows = jnp.concatenate(split2(jnp.concatenate(rows[1:], axis=0)), axis=0)
    dense = dot(parts_of_rows, spread_out)
    same = iota(dense.shape, 0) % classes == iota(dense.shape, 1) % classes
    dense = jnp.where(same, dense, 0.0).astype(jnp.bfloat16)
    count = SUBSTEPS * classes
    fluxes = dot(dense, highs[...])
    fluxes = fluxes[:count] + fluxes[count:] + dot(dense[:count], lows[...])
    spread = [
        grow(jnp.sum(rows[d] * coup[...], axis=1, keepdims=True), scale, d) for d in range(SUBSTEPS)
    ]
    for copy in rest:
        copy.wait()
    counts_n = counts[...].astype(jnp.float32) / (COUNT_SCALE * CLASSES)
    chunks = cells // LANES
    targets = range(out.shape[0])
    per = pressure.shape[1] // LANES
    tile = pressure.shape[0] * per
    tail = out.shape[1] - 1
    total = jnp.zeros((1, LANES), jnp.float32)
    for n in targets:
        out[n, tail] = jnp.zeros((chunks, LANES), jnp.float32)
    for r in range(chunks):
        here = counts_n[:, r * LANES : (r + 1) * LANES]
        for t in range(SUBSTEPS):
            part = fluxes[t * classes : (t + 1) * classes, r * LANES : (r + 1) * LANES]
            row = jnp.sum(grow(here * part, scale, t + 1), axis=0, keepdims=True)
            if t < SUBSTEPS - 1:
                for n in targets:
                    out[n, t, r : r + 1, :] = row
            else:
                out[r // tile, tail, r % tile : r % tile + 1, :] = row
                total = total + row
        for d in range(SUBSTEPS):
            row = jnp.sum(here * spread[d], axis=0, keepdims=True)
            for n in targets:
                out[n, SUBSTEPS - 1 + d, r : r + 1, :] = row
    total = jnp.broadcast_to(jnp.sum(total, axis=1, keepdims=True), (1, LANES))
    for n in targets:
        for i in range(tile):
            out[n, tail, tile + i : tile + i + 1, :] = pressure[
                i // per : i // per + 1, (i % per) * LANES : (i % per + 1) * LANES
            ]
        out[n, tail, 2 * tile : 2 * tile + 1, :] = total


def power_kernel(melt_hbm, prop_hbm, coup_hbm, out, melt, prop, coup, sems, param_sems):
    chunks = melt.shape[0]
    classes, nodes = prop.shape[:2]
    params = param_copies([(prop_hbm, prop), (coup_hbm, coup)], param_sems)
    for copy in params:
        copy.start()
    loads = [
        pltpu.make_async_copy(melt_hbm.at[:, pl.ds(r * LANES, LANES)], melt.at[r], sems.at[r])
        for r in range(chunks)
    ]
    for load in loads:
        load.start()
    for copy in params:
        copy.wait()
    scale = class_scale(prop)
    inverse = 1.0 / scale
    every = range(classes)
    factors = [scale[k : k + 1, :] for k in every]
    unit = [prop[k] * inverse[k : k + 1, :] for k in every]
    first = [left_of(unit[k]) for k in every]
    square = [dot(first[k], right_of(unit[k])) for k in every]
    second = [left_of(square[k]) for k in every]
    lefts = [left_of(dot(second[k], right_of(square[k]))) for k in every]
    start = jnp.concatenate(
        [jnp.transpose(coup[...]), jnp.zeros((nodes, LANES - classes), jnp.float32)], axis=1
    )
    once = [dot(first[k], right_of(start)) for k in every]
    start = start[:, :classes]
    twice = [
        dot(second[k], right_of(jnp.concatenate([start, once[k][:, :classes]], axis=1))) for k in every
    ]
    lane = iota((nodes, LANES), 1)
    for k in every:
        powers = [
            start[:, k : k + 1],
            once[k][:, k : k + 1],
            twice[k][:, k : k + 1],
            twice[k][:, classes + k : classes + k + 1],
        ]
        value = jnp.zeros((nodes, LANES), jnp.float32)
        for d in range(SUBSTEPS):
            value = jnp.where(lane % SUBSTEPS == SUBSTEPS - 1 - d, grow(powers[d], factors[k], d), value)
        high = value.astype(jnp.bfloat16).astype(jnp.float32)
        value = jnp.where(lane < 2 * SUBSTEPS, high, jnp.where(lane < 3 * SUBSTEPS, value - high, 0.0))
        out[chunks, pl.ds(k, nodes, stride=classes), :] = value
    together = 2 if chunks % 2 == 0 else 1
    for r in range(0, chunks, together):
        for n in range(together):
            loads[r + n].wait()
        for k in every:
            own = pl.ds(k, nodes, stride=classes)
            x = jnp.concatenate([melt[r + n, own, :] for n in range(together)], axis=1)
            part = grow(dot(lefts[k], right_of(x)), factors[k], SUBSTEPS)
            for n in range(together):
                out[r + n, own, :] = part[:, n * LANES : (n + 1) * LANES]


def combine_kernel(parts, _, out, kept):
    senders, fields = parts.shape[:2]
    tail = fields - 1
    tile = out.shape[1] // senders
    total = parts[0]
    for n in range(1, senders):
        total = total + parts[n]
    pressure = jnp.concatenate([parts[n, tail, tile : 2 * tile, :] for n in range(senders)], axis=0)
    wall = 0.5 * pressure
    for t in range(SUBSTEPS - 1):
        out[t] = total[t] + total[SUBSTEPS - 1 + t] * wall
        out[SUBSTEPS - 1 + t] = total[SUBSTEPS - 1 + t]
    out[tail - 1] = pressure
    change = total[tail - 1] * wall
    kept[...] = change
    own = kept[pl.ds(lax.axis_index("cls") * tile, tile), :]
    out[tail] = jnp.zeros_like(pressure)
    out[tail, :tile, :] = total[tail, :tile, :] + own
    out[tail, tile : tile + 1, :] = total[tail, 2 * tile : 2 * tile + 1, :] + total_of(change)


def total_of(x):
    tiles = jnp.sum(x.reshape(-1, GROUP, LANES), axis=0)
    return jnp.sum(jnp.sum(tiles, axis=1, keepdims=True), axis=0, keepdims=True)


def laplacian(x, plane):
    rows = x.shape[0]
    row = iota(x.shape, 0)
    lane = iota(x.shape, 1)
    per = plane // LANES
    inside = row % per * LANES + lane
    col = lane % SIDE
    total = jnp.where(col == 0, 0.0, pltpu.roll(x, 1, 1))
    total += jnp.where(col == SIDE - 1, 0.0, pltpu.roll(x, LANES - 1, 1))
    up = pltpu.roll(x, SIDE, 1)
    up = jnp.where(lane < SIDE, pltpu.roll(up, 1, 0), up)
    total += jnp.where(inside < SIDE, 0.0, up)
    down = pltpu.roll(x, LANES - SIDE, 1)
    down = jnp.where(lane >= LANES - SIDE, pltpu.roll(down, rows - 1, 0), down)
    total += jnp.where(inside >= plane - SIDE, 0.0, down)
    total += jnp.where(row < per, 0.0, pltpu.roll(x, per, 0))
    total += jnp.where(row >= rows - per, 0.0, pltpu.roll(x, rows - per, 0))
    return total - 6.0 * x


def finish_kernel(
    window, shells, out_hbm, pressure_out, out, walls_all, last, out_sems
):
    nodes, classes, cells = out.shape
    chunks = cells // LANES
    parts = nodes // GROUP
    width = GROUP * classes

    def piece(g):
        return pl.ds(g * GROUP, GROUP)

    plane = pressure_out.shape[1]
    blocks = window.shape[0]
    rows = blocks * chunks
    per = plane // LANES
    tile = pressure_out.shape[0] * per

    def field_of(f):
        return window[:, f].reshape(rows, LANES)

    field = field_of(2 * SUBSTEPS - 2)
    answer = field_of(SUBSTEPS - 1)
    answer_total = total_of(answer)
    chamber = None
    walls = []
    for t in range(SUBSTEPS):
        gas = answer * (0.5 * field) if t else field_of(0)
        for s in range(1, t):
            gas = gas + field_of(SUBSTEPS - 1 + t - s) * walls[s]
        if 0 < t < SUBSTEPS - 1:
            gas = gas + field_of(t)
        total = total_of(gas)
        if t == SUBSTEPS - 1:
            total = total + jnp.sum(window[:, 2 * SUBSTEPS - 1], axis=0)[tile : tile + 1, :1]
        if t:
            field = field + 0.2 * chamber
            gas = gas + answer * (0.1 * chamber)
            total = total + answer_total * (0.1 * chamber)
        walls.append(0.5 * field)
        walls_all[t] = walls[t]
        field = 0.8 * field + 0.15 * laplacian(field, plane) + 0.1 * gas
        chamber = 1.5 - 0.5 * total / (rows * LANES)
    last[...] = field + 0.2 * chamber
    cell = lax.axis_index("cell")
    first = cell * chunks
    at = first + lax.axis_index("cls") * tile
    for i in range(tile):
        pressure_out[i // per : i // per + 1, (i % per) * LANES : (i % per + 1) * LANES] = (
            last[pl.ds(at + i, 1), :] + 0.1 * window[cell, 2 * SUBSTEPS - 1, i : i + 1, :]
        )
    right = []
    for r in range(chunks):
        wall = jnp.concatenate([walls_all[s, pl.ds(first + r, 1), :] for s in range(SUBSTEPS)], axis=0)
        high = wall.astype(jnp.bfloat16).astype(jnp.float32)
        right.append(jnp.concatenate([high, wall - high, high, jnp.zeros_like(high)], axis=0))
    right = jnp.concatenate(right, axis=1).astype(jnp.bfloat16)
    stores = [
        pltpu.make_async_copy(out.at[piece(g)], out_hbm.at[piece(g)], out_sems.at[g]) for g in range(parts)
    ]
    for g in range(parts):
        here = slice(g * width, (g + 1) * width)
        change = dot(shells[chunks, here, : 4 * SUBSTEPS].astype(jnp.bfloat16), right)
        for r in range(chunks):
            lanes = slice(r * LANES, (r + 1) * LANES)
            value = shells[r, here, :] + change[:, lanes]
            out[g * GROUP : (g + 1) * GROUP, :, lanes] = value.reshape(GROUP, classes, LANES)
        stores[g].start()
    for store in stores:
        store.wait()


HBM = pl.BlockSpec(memory_space=pltpu.HBM)
VMEM = pl.BlockSpec(memory_space=pltpu.VMEM)
DMA = pltpu.SemaphoreType.DMA


def exchange(copies, axis):
    return lax.all_to_all(copies, axis, split_axis=0, concat_axis=0, tiled=True)


def shards(melt, counts, pressure, propagator, coupling, flux_weights):
    nodes, classes, cells = melt.shape
    chunks = cells // LANES
    f32 = jnp.float32
    split = (chunks, nodes * classes, LANES)
    whole = pltpu.CompilerParams(vmem_limit_bytes=60 * 2**20)
    most = pltpu.CompilerParams(vmem_limit_bytes=48 * 2**20)
    little = pltpu.CompilerParams(vmem_limit_bytes=32 * 2**20)
    cls_count = lax.axis_size("cls")
    cell_count = lax.axis_size("cell")
    prop_v = pltpu.VMEM((classes, nodes, nodes), f32)
    small = pltpu.VMEM((classes, nodes), f32)
    parts = nodes // GROUP
    packed = pl.pallas_call(
        fields_kernel,
        out_shape=jax.ShapeDtypeStruct((cls_count, FIELDS, chunks, LANES), f32),
        in_specs=[HBM] * 6,
        out_specs=VMEM,
        scratch_shapes=[
            pltpu.VMEM(melt.shape, f32),
            pltpu.VMEM((nodes * classes, cells), jnp.bfloat16),
            pltpu.VMEM((nodes * classes, cells), jnp.bfloat16),
            pltpu.VMEM(counts.shape, counts.dtype),
            pltpu.VMEM(pressure.shape, f32),
            prop_v,
            small,
            small,
            DMA((parts,)),
            DMA((5,)),
        ],
        compiler_params=whole,
        name="fields",
    )(melt, counts, pressure, propagator, coupling, flux_weights)
    shells = pl.pallas_call(
        power_kernel,
        out_shape=jax.ShapeDtypeStruct((chunks + 1,) + split[1:], f32),
        in_specs=[HBM] * 3,
        out_specs=VMEM,
        scratch_shapes=[
            pltpu.VMEM(split, f32),
            prop_v,
            small,
            DMA((chunks,)),
            DMA((2,)),
        ],
        compiler_params=most,
        cost_estimate=pl.CostEstimate(flops=2 * 10**9, bytes_accessed=2 * melt.size * 4, transcendentals=0),
        name="power",
    )(melt.reshape(nodes * classes, cells), propagator, coupling)
    fields = pl.pallas_call(
        combine_kernel,
        out_shape=jax.ShapeDtypeStruct((FIELDS, chunks, LANES), f32),
        in_specs=[VMEM, VMEM],
        out_specs=VMEM,
        scratch_shapes=[pltpu.VMEM((chunks, LANES), f32)],
        compiler_params=little,
        name="combine",
    )(exchange(packed, "cls"), shells)
    window = lax.all_gather(fields, "cell", axis=0)
    rows = cell_count * chunks
    return pl.pallas_call(
        finish_kernel,
        out_shape=[jax.ShapeDtypeStruct(melt.shape, f32), jax.ShapeDtypeStruct(pressure.shape, f32)],
        in_specs=[VMEM, VMEM],
        out_specs=[HBM, VMEM],
        scratch_shapes=[
            pltpu.VMEM(melt.shape, f32),
            pltpu.VMEM((SUBSTEPS, rows, LANES), f32),
            pltpu.VMEM((rows, LANES), f32),
            DMA((parts,)),
        ],
        compiler_params=little,
        name="finish",
    )(window, shells)


def solution(mesh):
    placed = (P(None, "cls", "cell"), P("cls", "cell"), P(("cell", "cls"), None), P(), P(), P())
    return jax.shard_map(
        shards,
        mesh=mesh,
        in_specs=placed,
        out_specs=(P(None, "cls", "cell"), P(("cell", "cls"), None)),
        check_vma=False,
    )
```

```python
import functools

import jax
import jax.numpy as jnp
from jax import lax
from jax.experimental import pallas as pl
from jax.experimental.pallas import tpu as pltpu
from jax.sharding import PartitionSpec as P

CLASSES = 32
SIDE = 16
SUBSTEPS = 4
COUNT_SCALE = 400.0
LANES = 128
GROUP = 8
FIELDS = 2 * SUBSTEPS


def grow(value, factor, times):
    for _ in range(times):
        value = value * factor
    return value


def iota(shape, dim):
    return lax.broadcasted_iota(jnp.int32, shape, dim)


def split2(x):
    high = x.astype(jnp.bfloat16)
    return high, (x - high.astype(jnp.float32)).astype(jnp.bfloat16)


def dot(a, b):
    return jnp.dot(a, b, preferred_element_type=jnp.float32)


def left_of(x):
    high, low = split2(x)
    return jnp.concatenate([high, high, low], axis=1)


def right_of(x):
    high, low = split2(x)
    return jnp.concatenate([high, low, high], axis=0)


def class_scale(prop):
    rows = [jnp.max(jnp.abs(prop[k]), axis=0, keepdims=True) for k in range(prop.shape[0])]
    return jnp.maximum(1.0, jnp.max(jnp.concatenate(rows, axis=0), axis=1, keepdims=True))


def param_copies(pairs, sems):
    copies = []
    for n, (source, target) in enumerate(pairs):
        own = pl.ds(lax.axis_index("cls") * target.shape[0], target.shape[0])
        copies.append(pltpu.make_async_copy(source.at[own], target, sems.at[n]))
    return copies


def fields_kernel(
    melt_hbm, counts_hbm, pressure_hbm, prop_hbm, coup_hbm, flux_hbm, out, melt, highs, lows, counts, pressure, prop, coup, flux, sems, other_sems
):
    nodes, classes, cells = melt.shape
    first = param_copies([(prop_hbm, prop), (flux_hbm, flux), (coup_hbm, coup)], other_sems)
    for copy in first:
        copy.start()
    parts = nodes // GROUP
    pieces = [
        pltpu.make_async_copy(
            melt_hbm.at[pl.ds(g * GROUP, GROUP)], melt.at[pl.ds(g * GROUP, GROUP)], sems.at[g]
        )
        for g in range(parts)
    ]
    for piece in pieces:
        piece.start()
    rest = [
        pltpu.make_async_copy(counts_hbm, counts, other_sems.at[3]),
        pltpu.make_async_copy(pressure_hbm, pressure, other_sems.at[4]),
    ]
    for copy in rest:
        copy.start()
    for copy in first:
        copy.wait()
    scale = class_scale(prop)
    width = classes * nodes
    table = jnp.concatenate(split2(prop[...].reshape(width, nodes)), axis=1)
    inverse = 1.0 / scale
    mask = iota((classes, width), 1) // nodes == iota((classes, width), 0)
    rows = [flux[...]]
    tall = GROUP * classes
    each = parts // SUBSTEPS
    for t in range(SUBSTEPS):
        wide = jnp.where(mask, jnp.concatenate([rows[-1]] * classes, axis=1), 0.0)
        pairs = dot(jnp.concatenate(split2(wide), axis=0), table)
        row = pairs[:classes] + pairs[classes:]
        rows.append((row[:, :nodes] + row[:, nodes:]) * inverse)
        for g in range(t * each, parts if t == SUBSTEPS - 1 else (t + 1) * each):
            pieces[g].wait()
            here = slice(g * tall, (g + 1) * tall)
            highs[here, :], lows[here, :] = split2(
                melt[g * GROUP : (g + 1) * GROUP].reshape(tall, cells)
            )
    spread_out = (iota((nodes, width), 1) // classes == iota((nodes, width), 0)).astype(jnp.bfloat16)
    parts_of_rows = jnp.concatenate(split2(jnp.concatenate(rows[1:], axis=0)), axis=0)
    dense = dot(parts_of_rows, spread_out)
    same = iota(dense.shape, 0) % classes == iota(dense.shape, 1) % classes
    dense = jnp.where(same, dense, 0.0).astype(jnp.bfloat16)
    count = SUBSTEPS * classes
    fluxes = dot(dense, highs[...])
    fluxes = fluxes[:count] + fluxes[count:] + dot(dense[:count], lows[...])
    spread = [
        grow(jnp.sum(rows[d] * coup[...], axis=1, keepdims=True), scale, d) for d in range(SUBSTEPS)
    ]
    for copy in rest:
        copy.wait()
    counts_n = counts[...].astype(jnp.float32) / (COUNT_SCALE * CLASSES)
    chunks = cells // LANES
    for r in range(chunks):
        here = counts_n[:, r * LANES : (r + 1) * LANES]
        for t in range(SUBSTEPS):
            part = fluxes[t * classes : (t + 1) * classes, r * LANES : (r + 1) * LANES]
            out[t, r : r + 1, :] = jnp.sum(grow(here * part, scale, t + 1), axis=0, keepdims=True)
        for d in range(SUBSTEPS):
            out[SUBSTEPS + d, r : r + 1, :] = jnp.sum(here * spread[d], axis=0, keepdims=True)
    out[2 * SUBSTEPS] = jnp.zeros((chunks, LANES), jnp.float32)
    per = pressure.shape[1] // LANES
    tile = pressure.shape[0] * per
    at = lax.axis_index("cls") * tile
    for i in range(tile):
        out[2 * SUBSTEPS, pl.ds(at + i, 1), :] = pressure[
            i // per : i // per + 1, (i % per) * LANES : (i % per + 1) * LANES
        ]


def power_kernel(melt_hbm, prop_hbm, coup_hbm, _, out, melt, prop, coup, sems, param_sems):
    chunks = melt.shape[0]
    classes, nodes = prop.shape[:2]
    params = param_copies([(prop_hbm, prop), (coup_hbm, coup)], param_sems)
    for copy in params:
        copy.start()
    loads = [
        pltpu.make_async_copy(melt_hbm.at[:, pl.ds(r * LANES, LANES)], melt.at[r], sems.at[r])
        for r in range(chunks)
    ]
    for load in loads:
        load.start()
    for copy in params:
        copy.wait()
    scale = class_scale(prop)
    inverse = 1.0 / scale
    every = range(classes)
    factors = [scale[k : k + 1, :] for k in every]
    unit = [prop[k] * inverse[k : k + 1, :] for k in every]
    first = [left_of(unit[k]) for k in every]
    square = [dot(first[k], right_of(unit[k])) for k in every]
    second = [left_of(square[k]) for k in every]
    lefts = [left_of(dot(second[k], right_of(square[k]))) for k in every]
    start = jnp.concatenate(
        [jnp.transpose(coup[...]), jnp.zeros((nodes, LANES - classes), jnp.float32)], axis=1
    )
    once = [dot(first[k], right_of(start)) for k in every]
    start = start[:, :classes]
    twice = [
        dot(second[k], right_of(jnp.concatenate([start, once[k][:, :classes]], axis=1))) for k in every
    ]
    lane = iota((nodes, LANES), 1)
    for k in every:
        powers = [
            start[:, k : k + 1],
            once[k][:, k : k + 1],
            twice[k][:, k : k + 1],
            twice[k][:, classes + k : classes + k + 1],
        ]
        value = jnp.zeros((nodes, LANES), jnp.float32)
        for d in range(SUBSTEPS):
            value = jnp.where(lane % SUBSTEPS == SUBSTEPS - 1 - d, grow(powers[d], factors[k], d), value)
        high = value.astype(jnp.bfloat16).astype(jnp.float32)
        value = jnp.where(lane < 2 * SUBSTEPS, high, jnp.where(lane < 3 * SUBSTEPS, value - high, 0.0))
        out[chunks, pl.ds(k, nodes, stride=classes), :] = value
    together = 2 if chunks % 2 == 0 else 1
    for r in range(0, chunks, together):
        for n in range(together):
            loads[r + n].wait()
        for k in every:
            own = pl.ds(k, nodes, stride=classes)
            x = jnp.concatenate([melt[r + n, own, :] for n in range(together)], axis=1)
            part = grow(dot(lefts[k], right_of(x)), factors[k], SUBSTEPS)
            for n in range(together):
                out[r + n, own, :] = part[:, n * LANES : (n + 1) * LANES]


def combine_kernel(senders, mine, theirs, _, out, kept):
    total = mine[...] + theirs[...]
    tail = out.shape[0] - 1
    tile = out.shape[1] // senders
    pressure = total[2 * SUBSTEPS]
    wall = 0.5 * pressure
    for t in range(SUBSTEPS - 1):
        out[t] = total[t] + total[SUBSTEPS + t] * wall
        out[SUBSTEPS - 1 + t] = total[SUBSTEPS + t]
    out[tail - 1] = pressure
    gas = total[SUBSTEPS - 1] + total[2 * SUBSTEPS - 1] * wall
    kept[...] = gas
    out[tail] = jnp.broadcast_to(total_of(gas), gas.shape)
    out[tail, :tile, :] = kept[pl.ds(lax.axis_index("cls") * tile, tile), :]


def total_of(x):
    tiles = jnp.sum(x.reshape(-1, GROUP, LANES), axis=0)
    return jnp.sum(jnp.sum(tiles, axis=1, keepdims=True), axis=0, keepdims=True)


def laplacian(x, plane):
    rows = x.shape[0]
    row = iota(x.shape, 0)
    lane = iota(x.shape, 1)
    per = plane // LANES
    inside = row % per * LANES + lane
    col = lane % SIDE
    total = jnp.where(col == 0, 0.0, pltpu.roll(x, 1, 1))
    total += jnp.where(col == SIDE - 1, 0.0, pltpu.roll(x, LANES - 1, 1))
    up = pltpu.roll(x, SIDE, 1)
    up = jnp.where(lane < SIDE, pltpu.roll(up, 1, 0), up)
    total += jnp.where(inside < SIDE, 0.0, up)
    down = pltpu.roll(x, LANES - SIDE, 1)
    down = jnp.where(lane >= LANES - SIDE, pltpu.roll(down, rows - 1, 0), down)
    total += jnp.where(inside >= plane - SIDE, 0.0, down)
    total += jnp.where(row < per, 0.0, pltpu.roll(x, per, 0))
    total += jnp.where(row >= rows - per, 0.0, pltpu.roll(x, rows - per, 0))
    return total - 6.0 * x


def finish_kernel(
    window, shells, out_hbm, pressure_out, out, walls_all, last, out_sems
):
    nodes, classes, cells = out.shape
    chunks = cells // LANES
    parts = nodes // GROUP
    width = GROUP * classes

    def piece(g):
        return pl.ds(g * GROUP, GROUP)

    plane = pressure_out.shape[1]
    blocks = window.shape[0]
    rows = blocks * chunks
    per = plane // LANES
    tile = pressure_out.shape[0] * per

    def field_of(f):
        return window[:, f].reshape(rows, LANES)

    field = field_of(2 * SUBSTEPS - 2)
    answer = field_of(SUBSTEPS - 1)
    answer_total = total_of(answer)
    chamber = None
    walls = []
    for t in range(SUBSTEPS):
        gas = answer * (0.5 * field) if t else field_of(0)
        for s in range(1, t):
            gas = gas + field_of(SUBSTEPS - 1 + t - s) * walls[s]
        if 0 < t < SUBSTEPS - 1:
            gas = gas + field_of(t)
        total = total_of(gas)
        if t == SUBSTEPS - 1:
            total = total + jnp.sum(window[:, 2 * SUBSTEPS - 1], axis=0)[tile : tile + 1, :1]
        if t:
            field = field + 0.2 * chamber
            gas = gas + answer * (0.1 * chamber)
            total = total + answer_total * (0.1 * chamber)
        walls.append(0.5 * field)
        walls_all[t] = walls[t]
        field = 0.8 * field + 0.15 * laplacian(field, plane) + 0.1 * gas
        chamber = 1.5 - 0.5 * total / (rows * LANES)
    last[...] = field + 0.2 * chamber
    cell = lax.axis_index("cell")
    first = cell * chunks
    at = first + lax.axis_index("cls") * tile
    for i in range(tile):
        pressure_out[i // per : i // per + 1, (i % per) * LANES : (i % per + 1) * LANES] = (
            last[pl.ds(at + i, 1), :] + 0.1 * window[cell, 2 * SUBSTEPS - 1, i : i + 1, :]
        )
    right = []
    for r in range(chunks):
        wall = jnp.concatenate([walls_all[s, pl.ds(first + r, 1), :] for s in range(SUBSTEPS)], axis=0)
        high = wall.astype(jnp.bfloat16).astype(jnp.float32)
        right.append(jnp.concatenate([high, wall - high, high, jnp.zeros_like(high)], axis=0))
    right = jnp.concatenate(right, axis=1).astype(jnp.bfloat16)
    stores = [
        pltpu.make_async_copy(out.at[piece(g)], out_hbm.at[piece(g)], out_sems.at[g]) for g in range(parts)
    ]
    for g in range(parts):
        here = slice(g * width, (g + 1) * width)
        change = dot(shells[chunks, here, : 4 * SUBSTEPS].astype(jnp.bfloat16), right)
        for r in range(chunks):
            lanes = slice(r * LANES, (r + 1) * LANES)
            value = shells[r, here, :] + change[:, lanes]
            out[g * GROUP : (g + 1) * GROUP, :, lanes] = value.reshape(GROUP, classes, LANES)
        stores[g].start()
    for store in stores:
        store.wait()


HBM = pl.BlockSpec(memory_space=pltpu.HBM)
VMEM = pl.BlockSpec(memory_space=pltpu.VMEM)
DMA = pltpu.SemaphoreType.DMA


def partner(value, axis, distance):
    return lax.ppermute(value, axis, [(i, i ^ distance) for i in range(lax.axis_size(axis))])


def shards(melt, counts, pressure, propagator, coupling, flux_weights):
    nodes, classes, cells = melt.shape
    chunks = cells // LANES
    f32 = jnp.float32
    split = (chunks, nodes * classes, LANES)
    whole = pltpu.CompilerParams(vmem_limit_bytes=60 * 2**20)
    most = pltpu.CompilerParams(vmem_limit_bytes=48 * 2**20)
    little = pltpu.CompilerParams(vmem_limit_bytes=32 * 2**20)
    cls_count = lax.axis_size("cls")
    cell_count = lax.axis_size("cell")
    prop_v = pltpu.VMEM((classes, nodes, nodes), f32)
    small = pltpu.VMEM((classes, nodes), f32)
    parts = nodes // GROUP
    packed = pl.pallas_call(
        fields_kernel,
        out_shape=jax.ShapeDtypeStruct((FIELDS + 1, chunks, LANES), f32),
        in_specs=[HBM] * 6,
        out_specs=VMEM,
        scratch_shapes=[
            pltpu.VMEM(melt.shape, f32),
            pltpu.VMEM((nodes * classes, cells), jnp.bfloat16),
            pltpu.VMEM((nodes * classes, cells), jnp.bfloat16),
            pltpu.VMEM(counts.shape, counts.dtype),
            pltpu.VMEM(pressure.shape, f32),
            prop_v,
            small,
            small,
            DMA((parts,)),
            DMA((5,)),
        ],
        compiler_params=whole,
        name="fields",
    )(melt, counts, pressure, propagator, coupling, flux_weights)
    distance = 1
    theirs = partner(packed, "cls", distance)
    while 2 * distance < cls_count:
        distance *= 2
        packed = packed + theirs
        theirs = partner(packed, "cls", distance)
    shells = pl.pallas_call(
        power_kernel,
        out_shape=jax.ShapeDtypeStruct((chunks + 1,) + split[1:], f32),
        in_specs=[HBM] * 4,
        out_specs=VMEM,
        scratch_shapes=[
            pltpu.VMEM(split, f32),
            prop_v,
            small,
            DMA((chunks,)),
            DMA((2,)),
        ],
        compiler_params=most,
        cost_estimate=pl.CostEstimate(flops=2 * 10**9, bytes_accessed=2 * melt.size * 4, transcendentals=0),
        name="power",
    )(melt.reshape(nodes * classes, cells), propagator, coupling, packed)
    fields = pl.pallas_call(
        functools.partial(combine_kernel, cls_count),
        out_shape=jax.ShapeDtypeStruct((FIELDS, chunks, LANES), f32),
        in_specs=[VMEM, VMEM, VMEM],
        out_specs=VMEM,
        scratch_shapes=[pltpu.VMEM((chunks, LANES), f32)],
        compiler_params=little,
        name="combine",
    )(packed, theirs, shells)
    window = lax.all_gather(fields, "cell", axis=0)
    rows = cell_count * chunks
    return pl.pallas_call(
        finish_kernel,
        out_shape=[jax.ShapeDtypeStruct(melt.shape, f32), jax.ShapeDtypeStruct(pressure.shape, f32)],
        in_specs=[VMEM, VMEM],
        out_specs=[HBM, VMEM],
        scratch_shapes=[
            pltpu.VMEM(melt.shape, f32),
            pltpu.VMEM((SUBSTEPS, rows, LANES), f32),
            pltpu.VMEM((rows, LANES), f32),
            DMA((parts,)),
        ],
        compiler_params=little,
        name="finish",
    )(window, shells)


def solution(mesh):
    placed = (P(None, "cls", "cell"), P("cls", "cell"), P(("cell", "cls"), None), P(), P(), P())
    return jax.shard_map(
        shards,
        mesh=mesh,
        in_specs=placed,
        out_specs=(P(None, "cls", "cell"), P(("cell", "cls"), None)),
        check_vma=False,
    )
```

```python
import functools

import jax
import jax.numpy as jnp
from jax import lax
from jax.experimental import pallas as pl
from jax.experimental.pallas import tpu as pltpu
from jax.sharding import PartitionSpec as P

CLASSES = 32
SIDE = 16
SUBSTEPS = 4
COUNT_SCALE = 400.0
LANES = 128
GROUP = 8
FIELDS = 2 * SUBSTEPS


def grow(value, factor, times):
    for _ in range(times):
        value = value * factor
    return value


def iota(shape, dim):
    return lax.broadcasted_iota(jnp.int32, shape, dim)


def split2(x):
    high = x.astype(jnp.bfloat16)
    return high, (x - high.astype(jnp.float32)).astype(jnp.bfloat16)


def dot(a, b):
    return jnp.dot(a, b, preferred_element_type=jnp.float32)


def left_of(x):
    high, low = split2(x)
    return jnp.concatenate([high, high, low], axis=1)


def right_of(x):
    high, low = split2(x)
    return jnp.concatenate([high, low, high], axis=0)


def class_scale(prop):
    rows = [jnp.max(jnp.abs(prop[k]), axis=0, keepdims=True) for k in range(prop.shape[0])]
    return jnp.maximum(1.0, jnp.max(jnp.concatenate(rows, axis=0), axis=1, keepdims=True))


def param_copies(pairs, sems):
    copies = []
    for n, (source, target) in enumerate(pairs):
        own = pl.ds(lax.axis_index("cls") * target.shape[0], target.shape[0])
        copies.append(pltpu.make_async_copy(source.at[own], target, sems.at[n]))
    return copies


def fields_kernel(
    melt_hbm, counts_hbm, pressure_hbm, prop_hbm, coup_hbm, flux_hbm, out, melt, highs, lows, counts, pressure, prop, coup, flux, sems, other_sems
):
    nodes, classes, cells = melt.shape
    first = param_copies([(prop_hbm, prop), (flux_hbm, flux), (coup_hbm, coup)], other_sems)
    for copy in first:
        copy.start()
    parts = nodes // GROUP
    pieces = [
        pltpu.make_async_copy(
            melt_hbm.at[pl.ds(g * GROUP, GROUP)], melt.at[pl.ds(g * GROUP, GROUP)], sems.at[g]
        )
        for g in range(parts)
    ]
    for piece in pieces:
        piece.start()
    rest = [
        pltpu.make_async_copy(counts_hbm, counts, other_sems.at[3]),
        pltpu.make_async_copy(pressure_hbm, pressure, other_sems.at[4]),
    ]
    for copy in rest:
        copy.start()
    for copy in first:
        copy.wait()
    scale = class_scale(prop)
    width = classes * nodes
    table = jnp.concatenate(split2(prop[...].reshape(width, nodes)), axis=1)
    inverse = 1.0 / scale
    mask = iota((classes, width), 1) // nodes == iota((classes, width), 0)
    rows = [flux[...]]
    tall = GROUP * classes
    each = parts // SUBSTEPS
    for t in range(SUBSTEPS):
        wide = jnp.where(mask, jnp.concatenate([rows[-1]] * classes, axis=1), 0.0)
        pairs = dot(jnp.concatenate(split2(wide), axis=0), table)
        row = pairs[:classes] + pairs[classes:]
        rows.append((row[:, :nodes] + row[:, nodes:]) * inverse)
        for g in range(t * each, parts if t == SUBSTEPS - 1 else (t + 1) * each):
            pieces[g].wait()
            here = slice(g * tall, (g + 1) * tall)
            highs[here, :], lows[here, :] = split2(
                melt[g * GROUP : (g + 1) * GROUP].reshape(tall, cells)
            )
    spread_out = (iota((nodes, width), 1) // classes == iota((nodes, width), 0)).astype(jnp.bfloat16)
    parts_of_rows = jnp.concatenate(split2(jnp.concatenate(rows[1:], axis=0)), axis=0)
    dense = dot(parts_of_rows, spread_out)
    same = iota(dense.shape, 0) % classes == iota(dense.shape, 1) % classes
    dense = jnp.where(same, dense, 0.0).astype(jnp.bfloat16)
    count = SUBSTEPS * classes
    fluxes = dot(dense, highs[...])
    fluxes = fluxes[:count] + fluxes[count:] + dot(dense[:count], lows[...])
    spread = [
        grow(jnp.sum(rows[d] * coup[...], axis=1, keepdims=True), scale, d) for d in range(SUBSTEPS)
    ]
    for copy in rest:
        copy.wait()
    counts_n = counts[...].astype(jnp.float32) / (COUNT_SCALE * CLASSES)
    chunks = cells // LANES
    for r in range(chunks):
        here = counts_n[:, r * LANES : (r + 1) * LANES]
        for t in range(SUBSTEPS):
            part = fluxes[t * classes : (t + 1) * classes, r * LANES : (r + 1) * LANES]
            out[t, r : r + 1, :] = jnp.sum(grow(here * part, scale, t + 1), axis=0, keepdims=True)
        for d in range(SUBSTEPS):
            out[SUBSTEPS + d, r : r + 1, :] = jnp.sum(here * spread[d], axis=0, keepdims=True)
    out[2 * SUBSTEPS] = jnp.zeros((chunks, LANES), jnp.float32)
    per = pressure.shape[1] // LANES
    tile = pressure.shape[0] * per
    at = lax.axis_index("cls") * tile
    for i in range(tile):
        out[2 * SUBSTEPS, pl.ds(at + i, 1), :] = pressure[
            i // per : i // per + 1, (i % per) * LANES : (i % per + 1) * LANES
        ]


def powers_kernel(prop_hbm, coup_hbm, _, lefts, columns, factors, prop, coup, param_sems):
    classes, nodes = prop.shape[:2]
    params = param_copies([(prop_hbm, prop), (coup_hbm, coup)], param_sems)
    for copy in params:
        copy.start()
    for copy in params:
        copy.wait()
    scale = class_scale(prop)
    factors[...] = jnp.broadcast_to(scale, factors.shape)
    inverse = 1.0 / scale
    every = range(classes)
    unit = [prop[k] * inverse[k : k + 1, :] for k in every]
    first = [left_of(unit[k]) for k in every]
    square = [dot(first[k], right_of(unit[k])) for k in every]
    second = [left_of(square[k]) for k in every]
    for k in every:
        lefts[k] = left_of(dot(second[k], right_of(square[k])))
    start = jnp.concatenate(
        [jnp.transpose(coup[...]), jnp.zeros((nodes, LANES - classes), jnp.float32)], axis=1
    )
    once = [dot(first[k], right_of(start)) for k in every]
    start = start[:, :classes]
    twice = [
        dot(second[k], right_of(jnp.concatenate([start, once[k][:, :classes]], axis=1))) for k in every
    ]
    lane = iota((nodes, LANES), 1)
    for k in every:
        powers = [
            start[:, k : k + 1],
            once[k][:, k : k + 1],
            twice[k][:, k : k + 1],
            twice[k][:, classes + k : classes + k + 1],
        ]
        value = jnp.zeros((nodes, LANES), jnp.float32)
        for d in range(SUBSTEPS):
            grown = grow(powers[d], scale[k : k + 1, :], d)
            value = jnp.where(lane % SUBSTEPS == SUBSTEPS - 1 - d, grown, value)
        high = value.astype(jnp.bfloat16).astype(jnp.float32)
        value = jnp.where(lane < 2 * SUBSTEPS, high, jnp.where(lane < 3 * SUBSTEPS, value - high, 0.0))
        columns[pl.ds(k, nodes, stride=classes), :] = value


def apply_kernel(melt_hbm, lefts, factors, _, out, melt, sems):
    chunks = melt.shape[0]
    classes, nodes = lefts.shape[:2]
    loads = [
        pltpu.make_async_copy(melt_hbm.at[:, pl.ds(r * LANES, LANES)], melt.at[r], sems.at[r])
        for r in range(chunks)
    ]
    for load in loads:
        load.start()
    together = 2 if chunks % 2 == 0 else 1
    for r in range(0, chunks, together):
        for n in range(together):
            loads[r + n].wait()
        for k in range(classes):
            own = pl.ds(k, nodes, stride=classes)
            x = jnp.concatenate([melt[r + n, own, :] for n in range(together)], axis=1)
            part = grow(dot(lefts[k], right_of(x)), factors[k : k + 1, :1], SUBSTEPS)
            for n in range(together):
                out[r + n, own, :] = part[:, n * LANES : (n + 1) * LANES]


def add_kernel(mine, theirs, _, out):
    out[...] = mine[...] + theirs[...]


def combine_kernel(senders, mine, theirs, _, out, kept):
    total = mine[...] + theirs[...]
    tail = out.shape[0] - 1
    tile = out.shape[1] // senders
    pressure = total[2 * SUBSTEPS]
    wall = 0.5 * pressure
    for t in range(SUBSTEPS - 1):
        out[t] = total[t] + total[SUBSTEPS + t] * wall
        out[SUBSTEPS - 1 + t] = total[SUBSTEPS + t]
    out[tail - 1] = pressure
    gas = total[SUBSTEPS - 1] + total[2 * SUBSTEPS - 1] * wall
    kept[...] = gas
    out[tail] = jnp.broadcast_to(total_of(gas), gas.shape)
    out[tail, :tile, :] = kept[pl.ds(lax.axis_index("cls") * tile, tile), :]


def total_of(x):
    tiles = jnp.sum(x.reshape(-1, GROUP, LANES), axis=0)
    return jnp.sum(jnp.sum(tiles, axis=1, keepdims=True), axis=0, keepdims=True)


def laplacian(x, plane):
    rows = x.shape[0]
    row = iota(x.shape, 0)
    lane = iota(x.shape, 1)
    per = plane // LANES
    inside = row % per * LANES + lane
    col = lane % SIDE
    total = jnp.where(col == 0, 0.0, pltpu.roll(x, 1, 1))
    total += jnp.where(col == SIDE - 1, 0.0, pltpu.roll(x, LANES - 1, 1))
    up = pltpu.roll(x, SIDE, 1)
    up = jnp.where(lane < SIDE, pltpu.roll(up, 1, 0), up)
    total += jnp.where(inside < SIDE, 0.0, up)
    down = pltpu.roll(x, LANES - SIDE, 1)
    down = jnp.where(lane >= LANES - SIDE, pltpu.roll(down, rows - 1, 0), down)
    total += jnp.where(inside >= plane - SIDE, 0.0, down)
    total += jnp.where(row < per, 0.0, pltpu.roll(x, per, 0))
    total += jnp.where(row >= rows - per, 0.0, pltpu.roll(x, rows - per, 0))
    return total - 6.0 * x


def finish_kernel(
    window, shells, columns, out_hbm, pressure_out, out, walls_all, last, out_sems
):
    nodes, classes, cells = out.shape
    chunks = cells // LANES
    parts = nodes // GROUP
    width = GROUP * classes

    def piece(g):
        return pl.ds(g * GROUP, GROUP)

    plane = pressure_out.shape[1]
    blocks = window.shape[0]
    rows = blocks * chunks
    per = plane // LANES
    tile = pressure_out.shape[0] * per

    def field_of(f):
        return window[:, f].reshape(rows, LANES)

    field = field_of(2 * SUBSTEPS - 2)
    answer = field_of(SUBSTEPS - 1)
    answer_total = total_of(answer)
    chamber = None
    walls = []
    for t in range(SUBSTEPS):
        gas = answer * (0.5 * field) if t else field_of(0)
        for s in range(1, t):
            gas = gas + field_of(SUBSTEPS - 1 + t - s) * walls[s]
        if 0 < t < SUBSTEPS - 1:
            gas = gas + field_of(t)
        total = total_of(gas)
        if t == SUBSTEPS - 1:
            total = total + jnp.sum(window[:, 2 * SUBSTEPS - 1], axis=0)[tile : tile + 1, :1]
        if t:
            field = field + 0.2 * chamber
            gas = gas + answer * (0.1 * chamber)
            total = total + answer_total * (0.1 * chamber)
        walls.append(0.5 * field)
        walls_all[t] = walls[t]
        field = 0.8 * field + 0.15 * laplacian(field, plane) + 0.1 * gas
        chamber = 1.5 - 0.5 * total / (rows * LANES)
    last[...] = field + 0.2 * chamber
    cell = lax.axis_index("cell")
    first = cell * chunks
    at = first + lax.axis_index("cls") * tile
    for i in range(tile):
        pressure_out[i // per : i // per + 1, (i % per) * LANES : (i % per + 1) * LANES] = (
            last[pl.ds(at + i, 1), :] + 0.1 * window[cell, 2 * SUBSTEPS - 1, i : i + 1, :]
        )
    right = []
    for r in range(chunks):
        wall = jnp.concatenate([walls_all[s, pl.ds(first + r, 1), :] for s in range(SUBSTEPS)], axis=0)
        high = wall.astype(jnp.bfloat16).astype(jnp.float32)
        right.append(jnp.concatenate([high, wall - high, high, jnp.zeros_like(high)], axis=0))
    right = jnp.concatenate(right, axis=1).astype(jnp.bfloat16)
    stores = [
        pltpu.make_async_copy(out.at[piece(g)], out_hbm.at[piece(g)], out_sems.at[g]) for g in range(parts)
    ]
    for g in range(parts):
        here = slice(g * width, (g + 1) * width)
        change = dot(columns[here, : 4 * SUBSTEPS].astype(jnp.bfloat16), right)
        for r in range(chunks):
            lanes = slice(r * LANES, (r + 1) * LANES)
            value = shells[r, here, :] + change[:, lanes]
            out[g * GROUP : (g + 1) * GROUP, :, lanes] = value.reshape(GROUP, classes, LANES)
        stores[g].start()
    for store in stores:
        store.wait()


HBM = pl.BlockSpec(memory_space=pltpu.HBM)
VMEM = pl.BlockSpec(memory_space=pltpu.VMEM)
DMA = pltpu.SemaphoreType.DMA


def partner(value, axis, distance):
    return lax.ppermute(value, axis, [(i, i ^ distance) for i in range(lax.axis_size(axis))])


def shards(melt, counts, pressure, propagator, coupling, flux_weights):
    nodes, classes, cells = melt.shape
    chunks = cells // LANES
    f32 = jnp.float32
    split = (chunks, nodes * classes, LANES)
    whole = pltpu.CompilerParams(vmem_limit_bytes=60 * 2**20)
    most = pltpu.CompilerParams(vmem_limit_bytes=48 * 2**20)
    little = pltpu.CompilerParams(vmem_limit_bytes=32 * 2**20)
    cls_count = lax.axis_size("cls")
    cell_count = lax.axis_size("cell")
    prop_v = pltpu.VMEM((classes, nodes, nodes), f32)
    small = pltpu.VMEM((classes, nodes), f32)
    parts = nodes // GROUP
    packed = pl.pallas_call(
        fields_kernel,
        out_shape=jax.ShapeDtypeStruct((FIELDS + 1, chunks, LANES), f32),
        in_specs=[HBM] * 6,
        out_specs=VMEM,
        scratch_shapes=[
            pltpu.VMEM(melt.shape, f32),
            pltpu.VMEM((nodes * classes, cells), jnp.bfloat16),
            pltpu.VMEM((nodes * classes, cells), jnp.bfloat16),
            pltpu.VMEM(counts.shape, counts.dtype),
            pltpu.VMEM(pressure.shape, f32),
            prop_v,
            small,
            small,
            DMA((parts,)),
            DMA((5,)),
        ],
        compiler_params=whole,
        name="fields",
    )(melt, counts, pressure, propagator, coupling, flux_weights)
    lefts_shape = (classes, nodes, 3 * nodes)
    theirs = partner(packed, "cls", 1)
    lefts, columns, factors = pl.pallas_call(
        powers_kernel,
        out_shape=[
            jax.ShapeDtypeStruct(lefts_shape, jnp.bfloat16),
            jax.ShapeDtypeStruct(split[1:], f32),
            jax.ShapeDtypeStruct((classes, LANES), f32),
        ],
        in_specs=[HBM, HBM, VMEM],
        out_specs=[VMEM] * 3,
        scratch_shapes=[prop_v, small, DMA((2,))],
        compiler_params=most,
        cost_estimate=pl.CostEstimate(flops=10**9, bytes_accessed=10**6, transcendentals=0),
        name="powers",
    )(propagator, coupling, packed)
    distance = 1
    after = factors
    while 2 * distance < cls_count:
        distance *= 2
        packed = pl.pallas_call(
            add_kernel,
            out_shape=jax.ShapeDtypeStruct(packed.shape, f32),
            in_specs=[VMEM] * 3,
            out_specs=VMEM,
            compiler_params=little,
            name="add",
        )(packed, theirs, after)
        theirs = partner(packed, "cls", distance)
    shells = pl.pallas_call(
        apply_kernel,
        out_shape=jax.ShapeDtypeStruct(split, f32),
        in_specs=[HBM, VMEM, VMEM, VMEM],
        out_specs=VMEM,
        scratch_shapes=[pltpu.VMEM(split, f32), DMA((chunks,))],
        compiler_params=most,
        cost_estimate=pl.CostEstimate(flops=10**9, bytes_accessed=melt.size * 4, transcendentals=0),
        name="apply",
    )(melt.reshape(nodes * classes, cells), lefts, factors, packed)
    fields = pl.pallas_call(
        functools.partial(combine_kernel, cls_count),
        out_shape=jax.ShapeDtypeStruct((FIELDS, chunks, LANES), f32),
        in_specs=[VMEM, VMEM, VMEM],
        out_specs=VMEM,
        scratch_shapes=[pltpu.VMEM((chunks, LANES), f32)],
        compiler_params=little,
        name="combine",
    )(packed, theirs, shells)
    window = lax.all_gather(fields, "cell", axis=0)
    rows = cell_count * chunks
    return pl.pallas_call(
        finish_kernel,
        out_shape=[jax.ShapeDtypeStruct(melt.shape, f32), jax.ShapeDtypeStruct(pressure.shape, f32)],
        in_specs=[VMEM, VMEM, VMEM],
        out_specs=[HBM, VMEM],
        scratch_shapes=[
            pltpu.VMEM(melt.shape, f32),
            pltpu.VMEM((SUBSTEPS, rows, LANES), f32),
            pltpu.VMEM((rows, LANES), f32),
            DMA((parts,)),
        ],
        compiler_params=little,
        name="finish",
    )(window, shells, columns)


def solution(mesh):
    placed = (P(None, "cls", "cell"), P("cls", "cell"), P(("cell", "cls"), None), P(), P(), P())
    return jax.shard_map(
        shards,
        mesh=mesh,
        in_specs=placed,
        out_specs=(P(None, "cls", "cell"), P(("cell", "cls"), None)),
        check_vma=False,
    )
```

```python
import functools

import jax
import jax.numpy as jnp
from jax import lax
from jax.experimental import pallas as pl
from jax.experimental.pallas import tpu as pltpu
from jax.sharding import PartitionSpec as P

CLASSES = 32
SIDE = 16
SUBSTEPS = 4
COUNT_SCALE = 400.0
LANES = 128
GROUP = 8
FIELDS = 2 * SUBSTEPS


def grow(value, factor, times):
    for _ in range(times):
        value = value * factor
    return value


def iota(shape, dim):
    return lax.broadcasted_iota(jnp.int32, shape, dim)


def split2(x):
    high = x.astype(jnp.bfloat16)
    return high, (x - high.astype(jnp.float32)).astype(jnp.bfloat16)


def dot(a, b):
    return jnp.dot(a, b, preferred_element_type=jnp.float32)


def left_of(x):
    high, low = split2(x)
    return jnp.concatenate([high, high, low], axis=1)


def right_of(x):
    high, low = split2(x)
    return jnp.concatenate([high, low, high], axis=0)


def class_scale(prop):
    rows = [jnp.max(jnp.abs(prop[k]), axis=0, keepdims=True) for k in range(prop.shape[0])]
    return jnp.maximum(1.0, jnp.max(jnp.concatenate(rows, axis=0), axis=1, keepdims=True))


def param_copies(pairs, sems):
    copies = []
    for n, (source, target) in enumerate(pairs):
        own = pl.ds(lax.axis_index("cls") * target.shape[0], target.shape[0])
        copies.append(pltpu.make_async_copy(source.at[own], target, sems.at[n]))
    return copies


def fields_kernel(
    melt_hbm, counts_hbm, pressure_hbm, prop_hbm, coup_hbm, flux_hbm, out, melt, highs, lows, counts, pressure, prop, coup, flux, sems, other_sems
):
    nodes, classes, cells = melt.shape
    first = param_copies([(prop_hbm, prop), (flux_hbm, flux), (coup_hbm, coup)], other_sems)
    for copy in first:
        copy.start()
    parts = nodes // GROUP
    pieces = [
        pltpu.make_async_copy(
            melt_hbm.at[pl.ds(g * GROUP, GROUP)], melt.at[pl.ds(g * GROUP, GROUP)], sems.at[g]
        )
        for g in range(parts)
    ]
    for piece in pieces:
        piece.start()
    rest = [
        pltpu.make_async_copy(counts_hbm, counts, other_sems.at[3]),
        pltpu.make_async_copy(pressure_hbm, pressure, other_sems.at[4]),
    ]
    for copy in rest:
        copy.start()
    for copy in first:
        copy.wait()
    scale = class_scale(prop)
    width = classes * nodes
    table = jnp.concatenate(split2(prop[...].reshape(width, nodes)), axis=1)
    inverse = 1.0 / scale
    mask = iota((classes, width), 1) // nodes == iota((classes, width), 0)
    rows = [flux[...]]
    tall = GROUP * classes
    each = parts // SUBSTEPS
    for t in range(SUBSTEPS):
        wide = jnp.where(mask, jnp.concatenate([rows[-1]] * classes, axis=1), 0.0)
        pairs = dot(jnp.concatenate(split2(wide), axis=0), table)
        row = pairs[:classes] + pairs[classes:]
        rows.append((row[:, :nodes] + row[:, nodes:]) * inverse)
        for g in range(t * each, parts if t == SUBSTEPS - 1 else (t + 1) * each):
            pieces[g].wait()
            here = slice(g * tall, (g + 1) * tall)
            highs[here, :], lows[here, :] = split2(
                melt[g * GROUP : (g + 1) * GROUP].reshape(tall, cells)
            )
    spread_out = (iota((nodes, width), 1) // classes == iota((nodes, width), 0)).astype(jnp.bfloat16)
    parts_of_rows = jnp.concatenate(split2(jnp.concatenate(rows[1:], axis=0)), axis=0)
    dense = dot(parts_of_rows, spread_out)
    same = iota(dense.shape, 0) % classes == iota(dense.shape, 1) % classes
    dense = jnp.where(same, dense, 0.0).astype(jnp.bfloat16)
    count = SUBSTEPS * classes
    fluxes = dot(dense, highs[...])
    fluxes = fluxes[:count] + fluxes[count:] + dot(dense[:count], lows[...])
    spread = [
        grow(jnp.sum(rows[d] * coup[...], axis=1, keepdims=True), scale, d) for d in range(SUBSTEPS)
    ]
    for copy in rest:
        copy.wait()
    counts_n = counts[...].astype(jnp.float32) / (COUNT_SCALE * CLASSES)
    chunks = cells // LANES
    for r in range(chunks):
        here = counts_n[:, r * LANES : (r + 1) * LANES]
        for t in range(SUBSTEPS):
            part = fluxes[t * classes : (t + 1) * classes, r * LANES : (r + 1) * LANES]
            out[t, r : r + 1, :] = jnp.sum(grow(here * part, scale, t + 1), axis=0, keepdims=True)
        for d in range(SUBSTEPS):
            out[SUBSTEPS + d, r : r + 1, :] = jnp.sum(here * spread[d], axis=0, keepdims=True)
    out[2 * SUBSTEPS] = jnp.zeros((chunks, LANES), jnp.float32)
    per = pressure.shape[1] // LANES
    tile = pressure.shape[0] * per
    at = lax.axis_index("cls") * tile
    for i in range(tile):
        out[2 * SUBSTEPS, pl.ds(at + i, 1), :] = pressure[
            i // per : i // per + 1, (i % per) * LANES : (i % per + 1) * LANES
        ]


def powers_kernel(prop_hbm, coup_hbm, _, lefts, columns, factors, prop, coup, param_sems):
    classes, nodes = prop.shape[:2]
    params = param_copies([(prop_hbm, prop), (coup_hbm, coup)], param_sems)
    for copy in params:
        copy.start()
    for copy in params:
        copy.wait()
    scale = class_scale(prop)
    factors[...] = jnp.broadcast_to(scale, factors.shape)
    inverse = 1.0 / scale
    every = range(classes)
    unit = [prop[k] * inverse[k : k + 1, :] for k in every]
    first = [left_of(unit[k]) for k in every]
    square = [dot(first[k], right_of(unit[k])) for k in every]
    second = [left_of(square[k]) for k in every]
    for k in every:
        lefts[k] = left_of(dot(second[k], right_of(square[k])))
    start = jnp.concatenate(
        [jnp.transpose(coup[...]), jnp.zeros((nodes, LANES - classes), jnp.float32)], axis=1
    )
    once = [dot(first[k], right_of(start)) for k in every]
    start = start[:, :classes]
    twice = [
        dot(second[k], right_of(jnp.concatenate([start, once[k][:, :classes]], axis=1))) for k in every
    ]
    lane = iota((nodes, LANES), 1)
    for k in every:
        powers = [
            start[:, k : k + 1],
            once[k][:, k : k + 1],
            twice[k][:, k : k + 1],
            twice[k][:, classes + k : classes + k + 1],
        ]
        value = jnp.zeros((nodes, LANES), jnp.float32)
        for d in range(SUBSTEPS):
            grown = grow(powers[d], scale[k : k + 1, :], d)
            value = jnp.where(lane % SUBSTEPS == SUBSTEPS - 1 - d, grown, value)
        high = value.astype(jnp.bfloat16).astype(jnp.float32)
        value = jnp.where(lane < 2 * SUBSTEPS, high, jnp.where(lane < 3 * SUBSTEPS, value - high, 0.0))
        columns[pl.ds(k, nodes, stride=classes), :] = value


def apply_kernel(melt_hbm, lefts, factors, _, out, melt, sems):
    chunks = melt.shape[0]
    classes, nodes = lefts.shape[:2]
    loads = [
        pltpu.make_async_copy(melt_hbm.at[:, pl.ds(r * LANES, LANES)], melt.at[r], sems.at[r])
        for r in range(chunks)
    ]
    for load in loads:
        load.start()
    together = 2 if chunks % 2 == 0 else 1
    for r in range(0, chunks, together):
        for n in range(together):
            loads[r + n].wait()
        for k in range(classes):
            own = pl.ds(k, nodes, stride=classes)
            x = jnp.concatenate([melt[r + n, own, :] for n in range(together)], axis=1)
            part = grow(dot(lefts[k], right_of(x)), factors[k : k + 1, :1], SUBSTEPS)
            for n in range(together):
                out[r + n, own, :] = part[:, n * LANES : (n + 1) * LANES]


def add_kernel(mine, theirs, _, out):
    out[...] = mine[...] + theirs[...]


def combine_kernel(senders, mine, theirs, _, out, kept):
    total = mine[...] + theirs[...]
    tail = out.shape[0] - 1
    tile = out.shape[1] // senders
    pressure = total[2 * SUBSTEPS]
    wall = 0.5 * pressure
    for t in range(SUBSTEPS - 1):
        out[t] = total[t] + total[SUBSTEPS + t] * wall
        out[SUBSTEPS - 1 + t] = total[SUBSTEPS + t]
    out[tail - 1] = pressure
    gas = total[SUBSTEPS - 1] + total[2 * SUBSTEPS - 1] * wall
    kept[...] = gas
    out[tail] = jnp.broadcast_to(total_of(gas), gas.shape)
    out[tail, :tile, :] = kept[pl.ds(lax.axis_index("cls") * tile, tile), :]


def total_of(x):
    tiles = jnp.sum(x.reshape(-1, GROUP, LANES), axis=0)
    return jnp.sum(jnp.sum(tiles, axis=1, keepdims=True), axis=0, keepdims=True)


def laplacian(x, plane):
    rows = x.shape[0]
    row = iota(x.shape, 0)
    lane = iota(x.shape, 1)
    per = plane // LANES
    inside = row % per * LANES + lane
    col = lane % SIDE
    total = jnp.where(col == 0, 0.0, pltpu.roll(x, 1, 1))
    total += jnp.where(col == SIDE - 1, 0.0, pltpu.roll(x, LANES - 1, 1))
    up = pltpu.roll(x, SIDE, 1)
    up = jnp.where(lane < SIDE, pltpu.roll(up, 1, 0), up)
    total += jnp.where(inside < SIDE, 0.0, up)
    down = pltpu.roll(x, LANES - SIDE, 1)
    down = jnp.where(lane >= LANES - SIDE, pltpu.roll(down, rows - 1, 0), down)
    total += jnp.where(inside >= plane - SIDE, 0.0, down)
    total += jnp.where(row < per, 0.0, pltpu.roll(x, per, 0))
    total += jnp.where(row >= rows - per, 0.0, pltpu.roll(x, rows - per, 0))
    return total - 6.0 * x


def finish_kernel(
    mine, theirs, shells, columns, out_hbm, pressure_out, out, walls_all, last, out_sems
):
    nodes, classes, cells = out.shape
    chunks = cells // LANES
    parts = nodes // GROUP
    width = GROUP * classes

    def piece(g):
        return pl.ds(g * GROUP, GROUP)

    plane = pressure_out.shape[1]
    cell = lax.axis_index("cell")
    even = cell % 2 == 0
    blocks = 2 * mine.shape[0]
    rows = blocks * chunks
    per = plane // LANES
    tile = pressure_out.shape[0] * per

    def field_of(f):
        first, second = mine[:, f], theirs[:, f]
        low, high = jnp.where(even, first, second), jnp.where(even, second, first)
        return jnp.stack([low, high], axis=1).reshape(rows, LANES)

    field = field_of(2 * SUBSTEPS - 2)
    answer = field_of(SUBSTEPS - 1)
    answer_total = total_of(answer)
    chamber = None
    walls = []
    for t in range(SUBSTEPS):
        gas = answer * (0.5 * field) if t else field_of(0)
        for s in range(1, t):
            gas = gas + field_of(SUBSTEPS - 1 + t - s) * walls[s]
        if 0 < t < SUBSTEPS - 1:
            gas = gas + field_of(t)
        total = total_of(gas)
        if t == SUBSTEPS - 1:
            rest = jnp.sum(mine[:, 2 * SUBSTEPS - 1] + theirs[:, 2 * SUBSTEPS - 1], axis=0)
            total = total + rest[tile : tile + 1, :1]
        if t:
            field = field + 0.2 * chamber
            gas = gas + answer * (0.1 * chamber)
            total = total + answer_total * (0.1 * chamber)
        walls.append(0.5 * field)
        walls_all[t] = walls[t]
        field = 0.8 * field + 0.15 * laplacian(field, plane) + 0.1 * gas
        chamber = 1.5 - 0.5 * total / (rows * LANES)
    last[...] = field + 0.2 * chamber
    first = cell * chunks
    at = first + lax.axis_index("cls") * tile
    for i in range(tile):
        pressure_out[i // per : i // per + 1, (i % per) * LANES : (i % per + 1) * LANES] = (
            last[pl.ds(at + i, 1), :] + 0.1 * mine[cell // 2, 2 * SUBSTEPS - 1, i : i + 1, :]
        )
    right = []
    for r in range(chunks):
        wall = jnp.concatenate([walls_all[s, pl.ds(first + r, 1), :] for s in range(SUBSTEPS)], axis=0)
        high = wall.astype(jnp.bfloat16).astype(jnp.float32)
        right.append(jnp.concatenate([high, wall - high, high, jnp.zeros_like(high)], axis=0))
    right = jnp.concatenate(right, axis=1).astype(jnp.bfloat16)
    stores = [
        pltpu.make_async_copy(out.at[piece(g)], out_hbm.at[piece(g)], out_sems.at[g]) for g in range(parts)
    ]
    for g in range(parts):
        here = slice(g * width, (g + 1) * width)
        change = dot(columns[here, : 4 * SUBSTEPS].astype(jnp.bfloat16), right)
        for r in range(chunks):
            lanes = slice(r * LANES, (r + 1) * LANES)
            value = shells[r, here, :] + change[:, lanes]
            out[g * GROUP : (g + 1) * GROUP, :, lanes] = value.reshape(GROUP, classes, LANES)
        stores[g].start()
    for store in stores:
        store.wait()


HBM = pl.BlockSpec(memory_space=pltpu.HBM)
VMEM = pl.BlockSpec(memory_space=pltpu.VMEM)
DMA = pltpu.SemaphoreType.DMA


def partner(value, axis, distance):
    return lax.ppermute(value, axis, [(i, i ^ distance) for i in range(lax.axis_size(axis))])


def shards(melt, counts, pressure, propagator, coupling, flux_weights):
    nodes, classes, cells = melt.shape
    chunks = cells // LANES
    f32 = jnp.float32
    split = (chunks, nodes * classes, LANES)
    whole = pltpu.CompilerParams(vmem_limit_bytes=60 * 2**20)
    most = pltpu.CompilerParams(vmem_limit_bytes=48 * 2**20)
    little = pltpu.CompilerParams(vmem_limit_bytes=32 * 2**20)
    cls_count = lax.axis_size("cls")
    cell_count = lax.axis_size("cell")
    prop_v = pltpu.VMEM((classes, nodes, nodes), f32)
    small = pltpu.VMEM((classes, nodes), f32)
    parts = nodes // GROUP
    packed = pl.pallas_call(
        fields_kernel,
        out_shape=jax.ShapeDtypeStruct((FIELDS + 1, chunks, LANES), f32),
        in_specs=[HBM] * 6,
        out_specs=VMEM,
        scratch_shapes=[
            pltpu.VMEM(melt.shape, f32),
            pltpu.VMEM((nodes * classes, cells), jnp.bfloat16),
            pltpu.VMEM((nodes * classes, cells), jnp.bfloat16),
            pltpu.VMEM(counts.shape, counts.dtype),
            pltpu.VMEM(pressure.shape, f32),
            prop_v,
            small,
            small,
            DMA((parts,)),
            DMA((5,)),
        ],
        compiler_params=whole,
        name="fields",
    )(melt, counts, pressure, propagator, coupling, flux_weights)
    lefts_shape = (classes, nodes, 3 * nodes)
    theirs = partner(packed, "cls", 1)
    lefts, columns, factors = pl.pallas_call(
        powers_kernel,
        out_shape=[
            jax.ShapeDtypeStruct(lefts_shape, jnp.bfloat16),
            jax.ShapeDtypeStruct(split[1:], f32),
            jax.ShapeDtypeStruct((classes, LANES), f32),
        ],
        in_specs=[HBM, HBM, VMEM],
        out_specs=[VMEM] * 3,
        scratch_shapes=[prop_v, small, DMA((2,))],
        compiler_params=most,
        cost_estimate=pl.CostEstimate(flops=10**9, bytes_accessed=10**6, transcendentals=0),
        name="powers",
    )(propagator, coupling, packed)
    distance = 1
    after = factors
    while 2 * distance < cls_count:
        distance *= 2
        packed = pl.pallas_call(
            add_kernel,
            out_shape=jax.ShapeDtypeStruct(packed.shape, f32),
            in_specs=[VMEM] * 3,
            out_specs=VMEM,
            compiler_params=little,
            name="add",
        )(packed, theirs, after)
        theirs = partner(packed, "cls", distance)
    shells = pl.pallas_call(
        apply_kernel,
        out_shape=jax.ShapeDtypeStruct(split, f32),
        in_specs=[HBM, VMEM, VMEM, VMEM],
        out_specs=VMEM,
        scratch_shapes=[pltpu.VMEM(split, f32), DMA((chunks,))],
        compiler_params=most,
        cost_estimate=pl.CostEstimate(flops=10**9, bytes_accessed=melt.size * 4, transcendentals=0),
        name="apply",
    )(melt.reshape(nodes * classes, cells), lefts, factors, packed)
    fields = pl.pallas_call(
        functools.partial(combine_kernel, cls_count),
        out_shape=jax.ShapeDtypeStruct((FIELDS, chunks, LANES), f32),
        in_specs=[VMEM, VMEM, VMEM],
        out_specs=VMEM,
        scratch_shapes=[pltpu.VMEM((chunks, LANES), f32)],
        compiler_params=little,
        name="combine",
    )(packed, theirs, shells)
    groups = [list(range(core, cell_count, 2)) for core in range(2)]
    own = lax.all_gather(fields, "cell", axis=0, axis_index_groups=groups)
    other = partner(own, "cell", 1)
    rows = cell_count * chunks
    return pl.pallas_call(
        finish_kernel,
        out_shape=[jax.ShapeDtypeStruct(melt.shape, f32), jax.ShapeDtypeStruct(pressure.shape, f32)],
        in_specs=[VMEM] * 4,
        out_specs=[HBM, VMEM],
        scratch_shapes=[
            pltpu.VMEM(melt.shape, f32),
            pltpu.VMEM((SUBSTEPS, rows, LANES), f32),
            pltpu.VMEM((rows, LANES), f32),
            DMA((parts,)),
        ],
        compiler_params=little,
        name="finish",
    )(own, other, shells, columns)


def solution(mesh):
    placed = (P(None, "cls", "cell"), P("cls", "cell"), P(("cell", "cls"), None), P(), P(), P())
    return jax.shard_map(
        shards,
        mesh=mesh,
        in_specs=placed,
        out_specs=(P(None, "cls", "cell"), P(("cell", "cls"), None)),
        check_vma=False,
    )
```

```python
import functools

import jax
import jax.numpy as jnp
from jax import lax
from jax.experimental import pallas as pl
from jax.experimental.pallas import tpu as pltpu
from jax.sharding import PartitionSpec as P

CLASSES = 32
SIDE = 16
SUBSTEPS = 4
COUNT_SCALE = 400.0
LANES = 128
GROUP = 8
FIELDS = 2 * SUBSTEPS


def grow(value, factor, times):
    for _ in range(times):
        value = value * factor
    return value


def iota(shape, dim):
    return lax.broadcasted_iota(jnp.int32, shape, dim)


def split2(x):
    high = x.astype(jnp.bfloat16)
    return high, (x - high.astype(jnp.float32)).astype(jnp.bfloat16)


def dot(a, b):
    return jnp.dot(a, b, preferred_element_type=jnp.float32)


def left_of(x):
    high, low = split2(x)
    return jnp.concatenate([high, high, low], axis=1)


def right_of(x):
    high, low = split2(x)
    return jnp.concatenate([high, low, high], axis=0)


def class_scale(prop):
    rows = [jnp.max(jnp.abs(prop[k]), axis=0, keepdims=True) for k in range(prop.shape[0])]
    return jnp.maximum(1.0, jnp.max(jnp.concatenate(rows, axis=0), axis=1, keepdims=True))


def param_copies(pairs, sems):
    copies = []
    for n, (source, target) in enumerate(pairs):
        own = pl.ds(lax.axis_index("cls") * target.shape[0], target.shape[0])
        copies.append(pltpu.make_async_copy(source.at[own], target, sems.at[n]))
    return copies


def fields_kernel(
    melt_hbm, counts_hbm, pressure_hbm, prop_hbm, coup_hbm, flux_hbm, out, melt, highs, lows, counts, pressure, prop, coup, flux, sems, other_sems
):
    nodes, classes, cells = melt.shape
    first = param_copies([(prop_hbm, prop), (flux_hbm, flux), (coup_hbm, coup)], other_sems)
    for copy in first:
        copy.start()
    parts = nodes // GROUP
    pieces = [
        pltpu.make_async_copy(
            melt_hbm.at[pl.ds(g * GROUP, GROUP)], melt.at[pl.ds(g * GROUP, GROUP)], sems.at[g]
        )
        for g in range(parts)
    ]
    for piece in pieces:
        piece.start()
    rest = [
        pltpu.make_async_copy(counts_hbm, counts, other_sems.at[3]),
        pltpu.make_async_copy(pressure_hbm, pressure, other_sems.at[4]),
    ]
    for copy in rest:
        copy.start()
    for copy in first:
        copy.wait()
    scale = class_scale(prop)
    width = classes * nodes
    table = jnp.concatenate(split2(prop[...].reshape(width, nodes)), axis=1)
    inverse = 1.0 / scale
    mask = iota((classes, width), 1) // nodes == iota((classes, width), 0)
    rows = [flux[...]]
    tall = GROUP * classes
    each = parts // SUBSTEPS
    for t in range(SUBSTEPS):
        wide = jnp.where(mask, jnp.concatenate([rows[-1]] * classes, axis=1), 0.0)
        pairs = dot(jnp.concatenate(split2(wide), axis=0), table)
        row = pairs[:classes] + pairs[classes:]
        rows.append((row[:, :nodes] + row[:, nodes:]) * inverse)
        for g in range(t * each, parts if t == SUBSTEPS - 1 else (t + 1) * each):
            pieces[g].wait()
            here = slice(g * tall, (g + 1) * tall)
            highs[here, :], lows[here, :] = split2(
                melt[g * GROUP : (g + 1) * GROUP].reshape(tall, cells)
            )
    spread_out = (iota((nodes, width), 1) // classes == iota((nodes, width), 0)).astype(jnp.bfloat16)
    parts_of_rows = jnp.concatenate(split2(jnp.concatenate(rows[1:], axis=0)), axis=0)
    dense = dot(parts_of_rows, spread_out)
    same = iota(dense.shape, 0) % classes == iota(dense.shape, 1) % classes
    dense = jnp.where(same, dense, 0.0).astype(jnp.bfloat16)
    count = SUBSTEPS * classes
    fluxes = dot(dense, highs[...])
    fluxes = fluxes[:count] + fluxes[count:] + dot(dense[:count], lows[...])
    spread = [
        grow(jnp.sum(rows[d] * coup[...], axis=1, keepdims=True), scale, d) for d in range(SUBSTEPS)
    ]
    for copy in rest:
        copy.wait()
    counts_n = counts[...].astype(jnp.float32) / (COUNT_SCALE * CLASSES)
    chunks = cells // LANES
    for r in range(chunks):
        here = counts_n[:, r * LANES : (r + 1) * LANES]
        for t in range(SUBSTEPS):
            part = fluxes[t * classes : (t + 1) * classes, r * LANES : (r + 1) * LANES]
            out[t, r : r + 1, :] = jnp.sum(grow(here * part, scale, t + 1), axis=0, keepdims=True)
        for d in range(SUBSTEPS):
            out[SUBSTEPS + d, r : r + 1, :] = jnp.sum(here * spread[d], axis=0, keepdims=True)
    out[2 * SUBSTEPS] = jnp.zeros((chunks, LANES), jnp.float32)
    per = pressure.shape[1] // LANES
    tile = pressure.shape[0] * per
    at = lax.axis_index("cls") * tile
    for i in range(tile):
        out[2 * SUBSTEPS, pl.ds(at + i, 1), :] = pressure[
            i // per : i // per + 1, (i % per) * LANES : (i % per + 1) * LANES
        ]


def powers_kernel(prop_hbm, coup_hbm, _, lefts, columns, factors, prop, coup, param_sems):
    classes, nodes = prop.shape[:2]
    params = param_copies([(prop_hbm, prop), (coup_hbm, coup)], param_sems)
    for copy in params:
        copy.start()
    for copy in params:
        copy.wait()
    scale = class_scale(prop)
    factors[...] = jnp.broadcast_to(scale, factors.shape)
    inverse = 1.0 / scale
    every = range(classes)
    unit = [prop[k] * inverse[k : k + 1, :] for k in every]
    first = [left_of(unit[k]) for k in every]
    square = [dot(first[k], right_of(unit[k])) for k in every]
    second = [left_of(square[k]) for k in every]
    for k in every:
        lefts[k] = left_of(dot(second[k], right_of(square[k])))
    start = jnp.concatenate(
        [jnp.transpose(coup[...]), jnp.zeros((nodes, LANES - classes), jnp.float32)], axis=1
    )
    once = [dot(first[k], right_of(start)) for k in every]
    start = start[:, :classes]
    twice = [
        dot(second[k], right_of(jnp.concatenate([start, once[k][:, :classes]], axis=1))) for k in every
    ]
    lane = iota((nodes, LANES), 1)
    for k in every:
        powers = [
            start[:, k : k + 1],
            once[k][:, k : k + 1],
            twice[k][:, k : k + 1],
            twice[k][:, classes + k : classes + k + 1],
        ]
        value = jnp.zeros((nodes, LANES), jnp.float32)
        for d in range(SUBSTEPS):
            grown = grow(powers[d], scale[k : k + 1, :], d)
            value = jnp.where(lane % SUBSTEPS == SUBSTEPS - 1 - d, grown, value)
        high = value.astype(jnp.bfloat16).astype(jnp.float32)
        value = jnp.where(lane < 2 * SUBSTEPS, high, jnp.where(lane < 3 * SUBSTEPS, value - high, 0.0))
        columns[pl.ds(k, nodes, stride=classes), :] = value


def apply_kernel(melt_hbm, lefts, factors, _, out, melt, sems):
    chunks = melt.shape[0]
    classes, nodes = lefts.shape[:2]
    loads = [
        pltpu.make_async_copy(melt_hbm.at[:, pl.ds(r * LANES, LANES)], melt.at[r], sems.at[r])
        for r in range(chunks)
    ]
    for load in loads:
        load.start()
    together = 2 if chunks % 2 == 0 else 1
    for r in range(0, chunks, together):
        for n in range(together):
            loads[r + n].wait()
        for k in range(classes):
            own = pl.ds(k, nodes, stride=classes)
            x = jnp.concatenate([melt[r + n, own, :] for n in range(together)], axis=1)
            part = grow(dot(lefts[k], right_of(x)), factors[k : k + 1, :1], SUBSTEPS)
            for n in range(together):
                out[r + n, own, :] = part[:, n * LANES : (n + 1) * LANES]


def add_kernel(mine, theirs, _, out):
    out[...] = mine[...] + theirs[...]


def combine_kernel(senders, mine, theirs, _, out_ref, kept):
    out = out_ref.at[0]
    total = mine[...] + theirs[...]
    tail = out.shape[0] - 1
    tile = out.shape[1] // senders
    pressure = total[2 * SUBSTEPS]
    wall = 0.5 * pressure
    for t in range(SUBSTEPS - 1):
        out[t] = total[t] + total[SUBSTEPS + t] * wall
        out[SUBSTEPS - 1 + t] = total[SUBSTEPS + t]
    out[tail - 1] = pressure
    gas = total[SUBSTEPS - 1] + total[2 * SUBSTEPS - 1] * wall
    kept[...] = gas
    out[tail] = jnp.broadcast_to(total_of(gas), gas.shape)
    out[tail, :tile, :] = kept[pl.ds(lax.axis_index("cls") * tile, tile), :]


def total_of(x):
    tiles = jnp.sum(x.reshape(-1, GROUP, LANES), axis=0)
    return jnp.sum(jnp.sum(tiles, axis=1, keepdims=True), axis=0, keepdims=True)


def laplacian(x, plane):
    rows = x.shape[0]
    row = iota(x.shape, 0)
    lane = iota(x.shape, 1)
    per = plane // LANES
    inside = row % per * LANES + lane
    col = lane % SIDE
    total = jnp.where(col == 0, 0.0, pltpu.roll(x, 1, 1))
    total += jnp.where(col == SIDE - 1, 0.0, pltpu.roll(x, LANES - 1, 1))
    up = pltpu.roll(x, SIDE, 1)
    up = jnp.where(lane < SIDE, pltpu.roll(up, 1, 0), up)
    total += jnp.where(inside < SIDE, 0.0, up)
    down = pltpu.roll(x, LANES - SIDE, 1)
    down = jnp.where(lane >= LANES - SIDE, pltpu.roll(down, rows - 1, 0), down)
    total += jnp.where(inside >= plane - SIDE, 0.0, down)
    total += jnp.where(row < per, 0.0, pltpu.roll(x, per, 0))
    total += jnp.where(row >= rows - per, 0.0, pltpu.roll(x, rows - per, 0))
    return total - 6.0 * x


def finish_kernel(
    mine, theirs, shells, columns, out_hbm, pressure_out, out, window, walls_all, last, out_sems
):
    nodes, classes, cells = out.shape
    chunks = cells // LANES
    parts = nodes // GROUP
    width = GROUP * classes

    def piece(g):
        return pl.ds(g * GROUP, GROUP)

    plane = pressure_out.shape[1]
    cell = lax.axis_index("cell")
    even = cell % 2 == 0
    blocks = window.shape[0]
    bits = chip_bits(blocks)
    for n, (first, second) in enumerate(zip(offsets(bits), offsets(bits[::-1]))):
        window[cell ^ jnp.where(even, first, second)] = mine[n]
        window[cell ^ 1 ^ jnp.where(even, second, first)] = theirs[n]
    rows = blocks * chunks
    per = plane // LANES
    tile = pressure_out.shape[0] * per

    def field_of(f):
        return window[:, f].reshape(rows, LANES)

    field = field_of(2 * SUBSTEPS - 2)
    answer = field_of(SUBSTEPS - 1)
    answer_total = total_of(answer)
    chamber = None
    walls = []
    for t in range(SUBSTEPS):
        gas = answer * (0.5 * field) if t else field_of(0)
        for s in range(1, t):
            gas = gas + field_of(SUBSTEPS - 1 + t - s) * walls[s]
        if 0 < t < SUBSTEPS - 1:
            gas = gas + field_of(t)
        total = total_of(gas)
        if t == SUBSTEPS - 1:
            rest = jnp.sum(window[:, 2 * SUBSTEPS - 1], axis=0)
            total = total + rest[tile : tile + 1, :1]
        if t:
            field = field + 0.2 * chamber
            gas = gas + answer * (0.1 * chamber)
            total = total + answer_total * (0.1 * chamber)
        walls.append(0.5 * field)
        walls_all[t] = walls[t]
        field = 0.8 * field + 0.15 * laplacian(field, plane) + 0.1 * gas
        chamber = 1.5 - 0.5 * total / (rows * LANES)
    last[...] = field + 0.2 * chamber
    first = cell * chunks
    at = first + lax.axis_index("cls") * tile
    for i in range(tile):
        pressure_out[i // per : i // per + 1, (i % per) * LANES : (i % per + 1) * LANES] = (
            last[pl.ds(at + i, 1), :] + 0.1 * mine[0, 2 * SUBSTEPS - 1, i : i + 1, :]
        )
    right = []
    for r in range(chunks):
        wall = jnp.concatenate([walls_all[s, pl.ds(first + r, 1), :] for s in range(SUBSTEPS)], axis=0)
        high = wall.astype(jnp.bfloat16).astype(jnp.float32)
        right.append(jnp.concatenate([high, wall - high, high, jnp.zeros_like(high)], axis=0))
    right = jnp.concatenate(right, axis=1).astype(jnp.bfloat16)
    stores = [
        pltpu.make_async_copy(out.at[piece(g)], out_hbm.at[piece(g)], out_sems.at[g]) for g in range(parts)
    ]
    for g in range(parts):
        here = slice(g * width, (g + 1) * width)
        change = dot(columns[here, : 4 * SUBSTEPS].astype(jnp.bfloat16), right)
        for r in range(chunks):
            lanes = slice(r * LANES, (r + 1) * LANES)
            value = shells[r, here, :] + change[:, lanes]
            out[g * GROUP : (g + 1) * GROUP, :, lanes] = value.reshape(GROUP, classes, LANES)
        stores[g].start()
    for store in stores:
        store.wait()


HBM = pl.BlockSpec(memory_space=pltpu.HBM)
VMEM = pl.BlockSpec(memory_space=pltpu.VMEM)
DMA = pltpu.SemaphoreType.DMA


def chip_bits(count):
    return [1 << b for b in reversed(range(1, count.bit_length() - 1))]


def offsets(bits):
    found = [0]
    for bit in bits:
        found = found + [m ^ bit for m in found]
    return found


def partner(value, axis, distance):
    return lax.ppermute(value, axis, [(i, i ^ distance) for i in range(lax.axis_size(axis))])


def shards(melt, counts, pressure, propagator, coupling, flux_weights):
    nodes, classes, cells = melt.shape
    chunks = cells // LANES
    f32 = jnp.float32
    split = (chunks, nodes * classes, LANES)
    whole = pltpu.CompilerParams(vmem_limit_bytes=60 * 2**20)
    most = pltpu.CompilerParams(vmem_limit_bytes=48 * 2**20)
    little = pltpu.CompilerParams(vmem_limit_bytes=32 * 2**20)
    cls_count = lax.axis_size("cls")
    cell_count = lax.axis_size("cell")
    prop_v = pltpu.VMEM((classes, nodes, nodes), f32)
    small = pltpu.VMEM((classes, nodes), f32)
    parts = nodes // GROUP
    packed = pl.pallas_call(
        fields_kernel,
        out_shape=jax.ShapeDtypeStruct((FIELDS + 1, chunks, LANES), f32),
        in_specs=[HBM] * 6,
        out_specs=VMEM,
        scratch_shapes=[
            pltpu.VMEM(melt.shape, f32),
            pltpu.VMEM((nodes * classes, cells), jnp.bfloat16),
            pltpu.VMEM((nodes * classes, cells), jnp.bfloat16),
            pltpu.VMEM(counts.shape, counts.dtype),
            pltpu.VMEM(pressure.shape, f32),
            prop_v,
            small,
            small,
            DMA((parts,)),
            DMA((5,)),
        ],
        compiler_params=whole,
        name="fields",
    )(melt, counts, pressure, propagator, coupling, flux_weights)
    lefts_shape = (classes, nodes, 3 * nodes)
    theirs = partner(packed, "cls", 1)
    lefts, columns, factors = pl.pallas_call(
        powers_kernel,
        out_shape=[
            jax.ShapeDtypeStruct(lefts_shape, jnp.bfloat16),
            jax.ShapeDtypeStruct(split[1:], f32),
            jax.ShapeDtypeStruct((classes, LANES), f32),
        ],
        in_specs=[HBM, HBM, VMEM],
        out_specs=[VMEM] * 3,
        scratch_shapes=[prop_v, small, DMA((2,))],
        compiler_params=most,
        cost_estimate=pl.CostEstimate(flops=10**9, bytes_accessed=10**6, transcendentals=0),
        name="powers",
    )(propagator, coupling, packed)
    distance = 1
    after = factors
    while 2 * distance < cls_count:
        distance *= 2
        packed = pl.pallas_call(
            add_kernel,
            out_shape=jax.ShapeDtypeStruct(packed.shape, f32),
            in_specs=[VMEM] * 3,
            out_specs=VMEM,
            compiler_params=little,
            name="add",
        )(packed, theirs, after)
        theirs = partner(packed, "cls", distance)
    shells = pl.pallas_call(
        apply_kernel,
        out_shape=jax.ShapeDtypeStruct(split, f32),
        in_specs=[HBM, VMEM, VMEM, VMEM],
        out_specs=VMEM,
        scratch_shapes=[pltpu.VMEM(split, f32), DMA((chunks,))],
        compiler_params=most,
        cost_estimate=pl.CostEstimate(flops=10**9, bytes_accessed=melt.size * 4, transcendentals=0),
        name="apply",
    )(melt.reshape(nodes * classes, cells), lefts, factors, packed)
    fields = pl.pallas_call(
        functools.partial(combine_kernel, cls_count),
        out_shape=jax.ShapeDtypeStruct((1, FIELDS, chunks, LANES), f32),
        in_specs=[VMEM, VMEM, VMEM],
        out_specs=VMEM,
        scratch_shapes=[pltpu.VMEM((chunks, LANES), f32)],
        compiler_params=little,
        name="combine",
    )(packed, theirs, shells)
    bits = chip_bits(cell_count)
    held = fields
    for even, odd in zip(bits, reversed(bits)):
        pairs = [(i, i ^ (odd if i % 2 else even)) for i in range(cell_count)]
        held = jnp.concatenate([held, lax.ppermute(held, "cell", pairs)], axis=0)
    other = partner(held, "cell", 1)
    rows = cell_count * chunks
    return pl.pallas_call(
        finish_kernel,
        out_shape=[jax.ShapeDtypeStruct(melt.shape, f32), jax.ShapeDtypeStruct(pressure.shape, f32)],
        in_specs=[VMEM] * 4,
        out_specs=[HBM, VMEM],
        scratch_shapes=[
            pltpu.VMEM(melt.shape, f32),
            pltpu.VMEM((cell_count, FIELDS, chunks, LANES), f32),
            pltpu.VMEM((SUBSTEPS, rows, LANES), f32),
            pltpu.VMEM((rows, LANES), f32),
            DMA((parts,)),
        ],
        compiler_params=little,
        name="finish",
    )(held, other, shells, columns)


def solution(mesh):
    placed = (P(None, "cls", "cell"), P("cls", "cell"), P(("cell", "cls"), None), P(), P(), P())
    return jax.shard_map(
        shards,
        mesh=mesh,
        in_specs=placed,
        out_specs=(P(None, "cls", "cell"), P(("cell", "cls"), None)),
        check_vma=False,
    )
```

```python
import functools

import jax
import jax.numpy as jnp
from jax import lax
from jax.experimental import pallas as pl
from jax.experimental.pallas import tpu as pltpu
from jax.sharding import PartitionSpec as P

CLASSES = 32
SIDE = 16
SUBSTEPS = 4
COUNT_SCALE = 400.0
LANES = 128
GROUP = 8
FIELDS = 2 * SUBSTEPS


def grow(value, factor, times):
    for _ in range(times):
        value = value * factor
    return value


def iota(shape, dim):
    return lax.broadcasted_iota(jnp.int32, shape, dim)


def split2(x):
    high = x.astype(jnp.bfloat16)
    return high, (x - high.astype(jnp.float32)).astype(jnp.bfloat16)


def dot(a, b):
    return jnp.dot(a, b, preferred_element_type=jnp.float32)


def left_of(x):
    high, low = split2(x)
    return jnp.concatenate([high, high, low], axis=1)


def right_of(x):
    high, low = split2(x)
    return jnp.concatenate([high, low, high], axis=0)


def class_scale(prop):
    rows = [jnp.max(jnp.abs(prop[k]), axis=0, keepdims=True) for k in range(prop.shape[0])]
    return jnp.maximum(1.0, jnp.max(jnp.concatenate(rows, axis=0), axis=1, keepdims=True))


def param_copies(pairs, sems):
    copies = []
    for n, (source, target) in enumerate(pairs):
        own = pl.ds(lax.axis_index("cls") * target.shape[0], target.shape[0])
        copies.append(pltpu.make_async_copy(source.at[own], target, sems.at[n]))
    return copies


def fields_kernel(
    melt_hbm, counts_hbm, pressure_hbm, prop_hbm, coup_hbm, flux_hbm, out, melt, highs, lows, counts, pressure, prop, coup, flux, sems, other_sems
):
    nodes, classes, cells = melt.shape
    first = param_copies([(prop_hbm, prop), (flux_hbm, flux), (coup_hbm, coup)], other_sems)
    for copy in first:
        copy.start()
    parts = nodes // GROUP
    pieces = [
        pltpu.make_async_copy(
            melt_hbm.at[pl.ds(g * GROUP, GROUP)], melt.at[pl.ds(g * GROUP, GROUP)], sems.at[g]
        )
        for g in range(parts)
    ]
    for piece in pieces:
        piece.start()
    rest = [
        pltpu.make_async_copy(counts_hbm, counts, other_sems.at[3]),
        pltpu.make_async_copy(pressure_hbm, pressure, other_sems.at[4]),
    ]
    for copy in rest:
        copy.start()
    for copy in first:
        copy.wait()
    scale = class_scale(prop)
    width = classes * nodes
    table = jnp.concatenate(split2(prop[...].reshape(width, nodes)), axis=1)
    inverse = 1.0 / scale
    mask = iota((classes, width), 1) // nodes == iota((classes, width), 0)
    rows = [flux[...]]
    tall = GROUP * classes
    each = parts // SUBSTEPS
    for t in range(SUBSTEPS):
        wide = jnp.where(mask, jnp.concatenate([rows[-1]] * classes, axis=1), 0.0)
        pairs = dot(jnp.concatenate(split2(wide), axis=0), table)
        row = pairs[:classes] + pairs[classes:]
        rows.append((row[:, :nodes] + row[:, nodes:]) * inverse)
        for g in range(t * each, parts if t == SUBSTEPS - 1 else (t + 1) * each):
            pieces[g].wait()
            here = slice(g * tall, (g + 1) * tall)
            highs[here, :], lows[here, :] = split2(
                melt[g * GROUP : (g + 1) * GROUP].reshape(tall, cells)
            )
    spread_out = (iota((nodes, width), 1) // classes == iota((nodes, width), 0)).astype(jnp.bfloat16)
    parts_of_rows = jnp.concatenate(split2(jnp.concatenate(rows[1:], axis=0)), axis=0)
    dense = dot(parts_of_rows, spread_out)
    same = iota(dense.shape, 0) % classes == iota(dense.shape, 1) % classes
    dense = jnp.where(same, dense, 0.0).astype(jnp.bfloat16)
    count = SUBSTEPS * classes
    fluxes = dot(dense, highs[...])
    fluxes = fluxes[:count] + fluxes[count:] + dot(dense[:count], lows[...])
    spread = [
        grow(jnp.sum(rows[d] * coup[...], axis=1, keepdims=True), scale, d) for d in range(SUBSTEPS)
    ]
    for copy in rest:
        copy.wait()
    counts_n = counts[...].astype(jnp.float32) / (COUNT_SCALE * CLASSES)
    chunks = cells // LANES
    for r in range(chunks):
        here = counts_n[:, r * LANES : (r + 1) * LANES]
        for t in range(SUBSTEPS):
            part = fluxes[t * classes : (t + 1) * classes, r * LANES : (r + 1) * LANES]
            out[t, r : r + 1, :] = jnp.sum(grow(here * part, scale, t + 1), axis=0, keepdims=True)
        for d in range(SUBSTEPS):
            out[SUBSTEPS + d, r : r + 1, :] = jnp.sum(here * spread[d], axis=0, keepdims=True)
    out[2 * SUBSTEPS] = jnp.zeros((chunks, LANES), jnp.float32)
    per = pressure.shape[1] // LANES
    tile = pressure.shape[0] * per
    at = lax.axis_index("cls") * tile
    for i in range(tile):
        out[2 * SUBSTEPS, pl.ds(at + i, 1), :] = pressure[
            i // per : i // per + 1, (i % per) * LANES : (i % per + 1) * LANES
        ]


def powers_kernel(prop_hbm, coup_hbm, _, lefts, columns, factors, prop, coup, param_sems):
    classes, nodes = prop.shape[:2]
    params = param_copies([(prop_hbm, prop), (coup_hbm, coup)], param_sems)
    for copy in params:
        copy.start()
    for copy in params:
        copy.wait()
    scale = class_scale(prop)
    factors[...] = jnp.broadcast_to(scale, factors.shape)
    inverse = 1.0 / scale
    every = range(classes)
    unit = [prop[k] * inverse[k : k + 1, :] for k in every]
    first = [left_of(unit[k]) for k in every]
    square = [dot(first[k], right_of(unit[k])) for k in every]
    second = [left_of(square[k]) for k in every]
    for k in every:
        lefts[k] = left_of(dot(second[k], right_of(square[k])))
    start = jnp.concatenate(
        [jnp.transpose(coup[...]), jnp.zeros((nodes, LANES - classes), jnp.float32)], axis=1
    )
    once = [dot(first[k], right_of(start)) for k in every]
    start = start[:, :classes]
    twice = [
        dot(second[k], right_of(jnp.concatenate([start, once[k][:, :classes]], axis=1))) for k in every
    ]
    lane = iota((nodes, LANES), 1)
    for k in every:
        powers = [
            start[:, k : k + 1],
            once[k][:, k : k + 1],
            twice[k][:, k : k + 1],
            twice[k][:, classes + k : classes + k + 1],
        ]
        value = jnp.zeros((nodes, LANES), jnp.float32)
        for d in range(SUBSTEPS):
            grown = grow(powers[d], scale[k : k + 1, :], d)
            value = jnp.where(lane % SUBSTEPS == SUBSTEPS - 1 - d, grown, value)
        high = value.astype(jnp.bfloat16).astype(jnp.float32)
        value = jnp.where(lane < 2 * SUBSTEPS, high, jnp.where(lane < 3 * SUBSTEPS, value - high, 0.0))
        columns[pl.ds(k, nodes, stride=classes), :] = value


def apply_kernel(melt_hbm, lefts, factors, _, out, melt, sems):
    chunks = melt.shape[0]
    classes, nodes = lefts.shape[:2]
    loads = [
        pltpu.make_async_copy(melt_hbm.at[:, pl.ds(r * LANES, LANES)], melt.at[r], sems.at[r])
        for r in range(chunks)
    ]
    for load in loads:
        load.start()
    together = 2 if chunks % 2 == 0 else 1
    for r in range(0, chunks, together):
        for n in range(together):
            loads[r + n].wait()
        for k in range(classes):
            own = pl.ds(k, nodes, stride=classes)
            x = jnp.concatenate([melt[r + n, own, :] for n in range(together)], axis=1)
            part = grow(dot(lefts[k], right_of(x)), factors[k : k + 1, :1], SUBSTEPS)
            for n in range(together):
                out[r + n, own, :] = part[:, n * LANES : (n + 1) * LANES]


def add_kernel(mine, theirs, _, out):
    out[...] = mine[...] + theirs[...]


def lift_kernel(value, out):
    out[...] = value[...]


def join_kernel(mine, theirs, out):
    out[0] = mine[...]
    out[1] = theirs[...]


def combine_kernel(senders, mine, theirs, _, out, kept):
    tail = out.shape[1] - 1
    tile = out.shape[2] // senders
    for n in range(out.shape[0]):
        total = mine[n] + theirs[n]
        pressure = total[2 * SUBSTEPS]
        wall = 0.5 * pressure
        for t in range(SUBSTEPS - 1):
            out[n, t] = total[t] + total[SUBSTEPS + t] * wall
            out[n, SUBSTEPS - 1 + t] = total[SUBSTEPS + t]
        out[n, tail - 1] = pressure
        gas = total[SUBSTEPS - 1] + total[2 * SUBSTEPS - 1] * wall
        kept[n] = gas
        out[n, tail] = jnp.broadcast_to(total_of(gas), gas.shape)
        out[n, tail, :tile, :] = kept[n, pl.ds(lax.axis_index("cls") * tile, tile), :]


def total_of(x):
    tiles = jnp.sum(x.reshape(-1, GROUP, LANES), axis=0)
    return jnp.sum(jnp.sum(tiles, axis=1, keepdims=True), axis=0, keepdims=True)


def laplacian(x, plane):
    rows = x.shape[0]
    row = iota(x.shape, 0)
    lane = iota(x.shape, 1)
    per = plane // LANES
    inside = row % per * LANES + lane
    col = lane % SIDE
    total = jnp.where(col == 0, 0.0, pltpu.roll(x, 1, 1))
    total += jnp.where(col == SIDE - 1, 0.0, pltpu.roll(x, LANES - 1, 1))
    up = pltpu.roll(x, SIDE, 1)
    up = jnp.where(lane < SIDE, pltpu.roll(up, 1, 0), up)
    total += jnp.where(inside < SIDE, 0.0, up)
    down = pltpu.roll(x, LANES - SIDE, 1)
    down = jnp.where(lane >= LANES - SIDE, pltpu.roll(down, rows - 1, 0), down)
    total += jnp.where(inside >= plane - SIDE, 0.0, down)
    total += jnp.where(row < per, 0.0, pltpu.roll(x, per, 0))
    total += jnp.where(row >= rows - per, 0.0, pltpu.roll(x, rows - per, 0))
    return total - 6.0 * x


def finish_kernel(
    mine, theirs, shells, columns, out_hbm, pressure_out, out, window, walls_all, last, out_sems
):
    nodes, classes, cells = out.shape
    chunks = cells // LANES
    parts = nodes // GROUP
    width = GROUP * classes

    def piece(g):
        return pl.ds(g * GROUP, GROUP)

    plane = pressure_out.shape[1]
    cell = lax.axis_index("cell")
    even = cell % 2 == 0
    blocks = window.shape[0]
    for n, offset in enumerate(offsets(chip_bits(blocks))):
        for core in range(2):
            at = (cell | 1) ^ (offset + core)
            window[at] = jnp.where(even, theirs[2 * n + core], mine[2 * n + core])
    rows = blocks * chunks
    per = plane // LANES
    tile = pressure_out.shape[0] * per

    def field_of(f):
        return window[:, f].reshape(rows, LANES)

    field = field_of(2 * SUBSTEPS - 2)
    answer = field_of(SUBSTEPS - 1)
    answer_total = total_of(answer)
    chamber = None
    walls = []
    for t in range(SUBSTEPS):
        gas = answer * (0.5 * field) if t else field_of(0)
        for s in range(1, t):
            gas = gas + field_of(SUBSTEPS - 1 + t - s) * walls[s]
        if 0 < t < SUBSTEPS - 1:
            gas = gas + field_of(t)
        total = total_of(gas)
        if t == SUBSTEPS - 1:
            rest = jnp.sum(window[:, 2 * SUBSTEPS - 1], axis=0)
            total = total + rest[tile : tile + 1, :1]
        if t:
            field = field + 0.2 * chamber
            gas = gas + answer * (0.1 * chamber)
            total = total + answer_total * (0.1 * chamber)
        walls.append(0.5 * field)
        walls_all[t] = walls[t]
        field = 0.8 * field + 0.15 * laplacian(field, plane) + 0.1 * gas
        chamber = 1.5 - 0.5 * total / (rows * LANES)
    last[...] = field + 0.2 * chamber
    first = cell * chunks
    at = first + lax.axis_index("cls") * tile
    for i in range(tile):
        pressure_out[i // per : i // per + 1, (i % per) * LANES : (i % per + 1) * LANES] = (
            last[pl.ds(at + i, 1), :] + 0.1 * window[cell, 2 * SUBSTEPS - 1, i : i + 1, :]
        )
    right = []
    for r in range(chunks):
        wall = jnp.concatenate([walls_all[s, pl.ds(first + r, 1), :] for s in range(SUBSTEPS)], axis=0)
        high = wall.astype(jnp.bfloat16).astype(jnp.float32)
        right.append(jnp.concatenate([high, wall - high, high, jnp.zeros_like(high)], axis=0))
    right = jnp.concatenate(right, axis=1).astype(jnp.bfloat16)
    stores = [
        pltpu.make_async_copy(out.at[piece(g)], out_hbm.at[piece(g)], out_sems.at[g]) for g in range(parts)
    ]
    for g in range(parts):
        here = slice(g * width, (g + 1) * width)
        change = dot(columns[here, : 4 * SUBSTEPS].astype(jnp.bfloat16), right)
        for r in range(chunks):
            lanes = slice(r * LANES, (r + 1) * LANES)
            value = shells[r, here, :] + change[:, lanes]
            out[g * GROUP : (g + 1) * GROUP, :, lanes] = value.reshape(GROUP, classes, LANES)
        stores[g].start()
    for store in stores:
        store.wait()


HBM = pl.BlockSpec(memory_space=pltpu.HBM)
VMEM = pl.BlockSpec(memory_space=pltpu.VMEM)
DMA = pltpu.SemaphoreType.DMA


def chip_bits(count):
    return [1 << b for b in reversed(range(1, count.bit_length() - 1))]


def offsets(bits):
    found = [0]
    for bit in bits:
        found = found + [m ^ bit for m in found]
    return found


def hand(value, odd):
    count = lax.axis_size("cell")
    return lax.ppermute(value, "cell", [(i, i ^ 1) for i in range(count) if i % 2 == odd])


def swap(value, cell_bit, cls_bit):
    cells, classes = lax.axis_size("cell"), lax.axis_size("cls")
    pairs = [
        (i * classes + k, (i ^ cell_bit) * classes + (k ^ cls_bit))
        for i in range(1, cells, 2)
        for k in range(classes)
    ]
    return lax.ppermute(value, ("cell", "cls"), pairs)


def shards(melt, counts, pressure, propagator, coupling, flux_weights):
    nodes, classes, cells = melt.shape
    chunks = cells // LANES
    f32 = jnp.float32
    split = (chunks, nodes * classes, LANES)
    whole = pltpu.CompilerParams(vmem_limit_bytes=60 * 2**20)
    most = pltpu.CompilerParams(vmem_limit_bytes=48 * 2**20)
    little = pltpu.CompilerParams(vmem_limit_bytes=32 * 2**20)
    cls_count = lax.axis_size("cls")
    cell_count = lax.axis_size("cell")
    prop_v = pltpu.VMEM((classes, nodes, nodes), f32)
    small = pltpu.VMEM((classes, nodes), f32)
    parts = nodes // GROUP
    packed = pl.pallas_call(
        fields_kernel,
        out_shape=jax.ShapeDtypeStruct((FIELDS + 1, chunks, LANES), f32),
        in_specs=[HBM] * 6,
        out_specs=VMEM,
        scratch_shapes=[
            pltpu.VMEM(melt.shape, f32),
            pltpu.VMEM((nodes * classes, cells), jnp.bfloat16),
            pltpu.VMEM((nodes * classes, cells), jnp.bfloat16),
            pltpu.VMEM(counts.shape, counts.dtype),
            pltpu.VMEM(pressure.shape, f32),
            prop_v,
            small,
            small,
            DMA((parts,)),
            DMA((5,)),
        ],
        compiler_params=whole,
        name="fields",
    )(melt, counts, pressure, propagator, coupling, flux_weights)
    lefts_shape = (classes, nodes, 3 * nodes)
    handed = hand(packed, 0)
    packed = pl.pallas_call(
        lift_kernel,
        out_shape=jax.ShapeDtypeStruct(packed.shape, f32),
        in_specs=[VMEM],
        out_specs=VMEM,
        compiler_params=little,
        cost_estimate=pl.CostEstimate(flops=10**8, bytes_accessed=10**6, transcendentals=0),
        name="lift",
    )(packed)
    packed = pl.pallas_call(
        join_kernel,
        out_shape=jax.ShapeDtypeStruct((2,) + packed.shape, f32),
        in_specs=[VMEM] * 2,
        out_specs=VMEM,
        compiler_params=little,
        name="join",
    )(packed, handed)
    theirs = swap(packed, 0, 1)
    lefts, columns, factors = pl.pallas_call(
        powers_kernel,
        out_shape=[
            jax.ShapeDtypeStruct(lefts_shape, jnp.bfloat16),
            jax.ShapeDtypeStruct(split[1:], f32),
            jax.ShapeDtypeStruct((classes, LANES), f32),
        ],
        in_specs=[HBM, HBM, VMEM],
        out_specs=[VMEM] * 3,
        scratch_shapes=[prop_v, small, DMA((2,))],
        compiler_params=most,
        cost_estimate=pl.CostEstimate(flops=10**9, bytes_accessed=10**6, transcendentals=0),
        name="powers",
    )(propagator, coupling, packed)
    distance = 1
    after = factors
    while 2 * distance < cls_count:
        distance *= 2
        packed = pl.pallas_call(
            add_kernel,
            out_shape=jax.ShapeDtypeStruct(packed.shape, f32),
            in_specs=[VMEM] * 3,
            out_specs=VMEM,
            compiler_params=little,
            name="add",
        )(packed, theirs, after)
        theirs = swap(packed, 0, distance)
    shells = pl.pallas_call(
        apply_kernel,
        out_shape=jax.ShapeDtypeStruct(split, f32),
        in_specs=[HBM, VMEM, VMEM, VMEM],
        out_specs=VMEM,
        scratch_shapes=[pltpu.VMEM(split, f32), DMA((chunks,))],
        compiler_params=most,
        cost_estimate=pl.CostEstimate(flops=10**9, bytes_accessed=melt.size * 4, transcendentals=0),
        name="apply",
    )(melt.reshape(nodes * classes, cells), lefts, factors, packed)
    fields = pl.pallas_call(
        functools.partial(combine_kernel, cls_count),
        out_shape=jax.ShapeDtypeStruct((2, FIELDS, chunks, LANES), f32),
        in_specs=[VMEM, VMEM, VMEM],
        out_specs=VMEM,
        scratch_shapes=[pltpu.VMEM((2, chunks, LANES), f32)],
        compiler_params=little,
        name="combine",
    )(packed, theirs, shells)
    held = fields
    for bit in chip_bits(cell_count):
        held = jnp.concatenate([held, swap(held, bit, 0)], axis=0)
    other = hand(held, 1)
    rows = cell_count * chunks
    return pl.pallas_call(
        finish_kernel,
        out_shape=[jax.ShapeDtypeStruct(melt.shape, f32), jax.ShapeDtypeStruct(pressure.shape, f32)],
        in_specs=[VMEM] * 4,
        out_specs=[HBM, VMEM],
        scratch_shapes=[
            pltpu.VMEM(melt.shape, f32),
            pltpu.VMEM((cell_count, FIELDS, chunks, LANES), f32),
            pltpu.VMEM((SUBSTEPS, rows, LANES), f32),
            pltpu.VMEM((rows, LANES), f32),
            DMA((parts,)),
        ],
        compiler_params=little,
        name="finish",
    )(held, other, shells, columns)


def solution(mesh):
    placed = (P(None, "cls", "cell"), P("cls", "cell"), P(("cell", "cls"), None), P(), P(), P())
    return jax.shard_map(
        shards,
        mesh=mesh,
        in_specs=placed,
        out_specs=(P(None, "cls", "cell"), P(("cell", "cls"), None)),
        check_vma=False,
    )
```

```python
import functools

import jax
import jax.numpy as jnp
from jax import lax
from jax.experimental import pallas as pl
from jax.experimental.pallas import tpu as pltpu
from jax.sharding import PartitionSpec as P

CLASSES = 32
SIDE = 16
SUBSTEPS = 4
COUNT_SCALE = 400.0
LANES = 128
GROUP = 8
FIELDS = 2 * SUBSTEPS


def grow(value, factor, times):
    for _ in range(times):
        value = value * factor
    return value


def iota(shape, dim):
    return lax.broadcasted_iota(jnp.int32, shape, dim)


def split2(x):
    high = x.astype(jnp.bfloat16)
    return high, (x - high.astype(jnp.float32)).astype(jnp.bfloat16)


def dot(a, b):
    return jnp.dot(a, b, preferred_element_type=jnp.float32)


def left_of(x):
    high, low = split2(x)
    return jnp.concatenate([high, high, low], axis=1)


def right_of(x):
    high, low = split2(x)
    return jnp.concatenate([high, low, high], axis=0)


def class_scale(prop):
    rows = [jnp.max(jnp.abs(prop[k]), axis=0, keepdims=True) for k in range(prop.shape[0])]
    return jnp.maximum(1.0, jnp.max(jnp.concatenate(rows, axis=0), axis=1, keepdims=True))


def param_copies(pairs, sems):
    copies = []
    for n, (source, target) in enumerate(pairs):
        own = pl.ds(lax.axis_index("cls") * target.shape[0], target.shape[0])
        copies.append(pltpu.make_async_copy(source.at[own], target, sems.at[n]))
    return copies


def fields_kernel(
    melt_hbm, counts_hbm, pressure_hbm, prop_hbm, coup_hbm, flux_hbm, out, melt, highs, lows, counts, pressure, prop, coup, flux, sems, other_sems
):
    nodes, classes, cells = melt.shape
    first = param_copies([(prop_hbm, prop), (flux_hbm, flux), (coup_hbm, coup)], other_sems)
    for copy in first:
        copy.start()
    parts = nodes // GROUP
    pieces = [
        pltpu.make_async_copy(
            melt_hbm.at[pl.ds(g * GROUP, GROUP)], melt.at[pl.ds(g * GROUP, GROUP)], sems.at[g]
        )
        for g in range(parts)
    ]
    for piece in pieces:
        piece.start()
    rest = [
        pltpu.make_async_copy(counts_hbm, counts, other_sems.at[3]),
        pltpu.make_async_copy(pressure_hbm, pressure, other_sems.at[4]),
    ]
    for copy in rest:
        copy.start()
    for copy in first:
        copy.wait()
    scale = class_scale(prop)
    width = classes * nodes
    table = jnp.concatenate(split2(prop[...].reshape(width, nodes)), axis=1)
    inverse = 1.0 / scale
    mask = iota((classes, width), 1) // nodes == iota((classes, width), 0)
    rows = [flux[...]]
    tall = GROUP * classes
    each = parts // SUBSTEPS
    for t in range(SUBSTEPS):
        wide = jnp.where(mask, jnp.concatenate([rows[-1]] * classes, axis=1), 0.0)
        pairs = dot(jnp.concatenate(split2(wide), axis=0), table)
        row = pairs[:classes] + pairs[classes:]
        rows.append((row[:, :nodes] + row[:, nodes:]) * inverse)
        for g in range(t * each, parts if t == SUBSTEPS - 1 else (t + 1) * each):
            pieces[g].wait()
            here = slice(g * tall, (g + 1) * tall)
            highs[here, :], lows[here, :] = split2(
                melt[g * GROUP : (g + 1) * GROUP].reshape(tall, cells)
            )
    spread_out = (iota((nodes, width), 1) // classes == iota((nodes, width), 0)).astype(jnp.bfloat16)
    parts_of_rows = jnp.concatenate(split2(jnp.concatenate(rows[1:], axis=0)), axis=0)
    dense = dot(parts_of_rows, spread_out)
    same = iota(dense.shape, 0) % classes == iota(dense.shape, 1) % classes
    dense = jnp.where(same, dense, 0.0).astype(jnp.bfloat16)
    count = SUBSTEPS * classes
    fluxes = dot(dense, highs[...])
    fluxes = fluxes[:count] + fluxes[count:] + dot(dense[:count], lows[...])
    spread = [
        grow(jnp.sum(rows[d] * coup[...], axis=1, keepdims=True), scale, d) for d in range(SUBSTEPS)
    ]
    for copy in rest:
        copy.wait()
    counts_n = counts[...].astype(jnp.float32) / (COUNT_SCALE * CLASSES)
    chunks = cells // LANES
    for r in range(chunks):
        here = counts_n[:, r * LANES : (r + 1) * LANES]
        for t in range(SUBSTEPS):
            part = fluxes[t * classes : (t + 1) * classes, r * LANES : (r + 1) * LANES]
            out[t, r : r + 1, :] = jnp.sum(grow(here * part, scale, t + 1), axis=0, keepdims=True)
        for d in range(SUBSTEPS):
            out[SUBSTEPS + d, r : r + 1, :] = jnp.sum(here * spread[d], axis=0, keepdims=True)
    out[2 * SUBSTEPS] = jnp.zeros((chunks, LANES), jnp.float32)
    per = pressure.shape[1] // LANES
    tile = pressure.shape[0] * per
    at = lax.axis_index("cls") * tile
    for i in range(tile):
        out[2 * SUBSTEPS, pl.ds(at + i, 1), :] = pressure[
            i // per : i // per + 1, (i % per) * LANES : (i % per + 1) * LANES
        ]


def powers_kernel(prop_hbm, coup_hbm, _, lefts, columns, factors, prop, coup, param_sems):
    classes, nodes = prop.shape[:2]
    params = param_copies([(prop_hbm, prop), (coup_hbm, coup)], param_sems)
    for copy in params:
        copy.start()
    for copy in params:
        copy.wait()
    scale = class_scale(prop)
    factors[...] = jnp.broadcast_to(scale, factors.shape)
    inverse = 1.0 / scale
    every = range(classes)
    unit = [prop[k] * inverse[k : k + 1, :] for k in every]
    first = [left_of(unit[k]) for k in every]
    square = [dot(first[k], right_of(unit[k])) for k in every]
    second = [left_of(square[k]) for k in every]
    for k in every:
        lefts[k] = left_of(dot(second[k], right_of(square[k])))
    start = jnp.concatenate(
        [jnp.transpose(coup[...]), jnp.zeros((nodes, LANES - classes), jnp.float32)], axis=1
    )
    once = [dot(first[k], right_of(start)) for k in every]
    start = start[:, :classes]
    twice = [
        dot(second[k], right_of(jnp.concatenate([start, once[k][:, :classes]], axis=1))) for k in every
    ]
    lane = iota((nodes, LANES), 1)
    for k in every:
        powers = [
            start[:, k : k + 1],
            once[k][:, k : k + 1],
            twice[k][:, k : k + 1],
            twice[k][:, classes + k : classes + k + 1],
        ]
        value = jnp.zeros((nodes, LANES), jnp.float32)
        for d in range(SUBSTEPS):
            grown = grow(powers[d], scale[k : k + 1, :], d)
            value = jnp.where(lane % SUBSTEPS == SUBSTEPS - 1 - d, grown, value)
        high = value.astype(jnp.bfloat16).astype(jnp.float32)
        value = jnp.where(lane < 2 * SUBSTEPS, high, jnp.where(lane < 3 * SUBSTEPS, value - high, 0.0))
        columns[pl.ds(k, nodes, stride=classes), :] = value


def apply_kernel(melt_hbm, lefts, factors, _, out, melt, sems):
    chunks = melt.shape[0]
    classes, nodes = lefts.shape[:2]
    loads = [
        pltpu.make_async_copy(melt_hbm.at[:, pl.ds(r * LANES, LANES)], melt.at[r], sems.at[r])
        for r in range(chunks)
    ]
    for load in loads:
        load.start()
    together = 2 if chunks % 2 == 0 else 1
    for r in range(0, chunks, together):
        for n in range(together):
            loads[r + n].wait()
        for k in range(classes):
            own = pl.ds(k, nodes, stride=classes)
            x = jnp.concatenate([melt[r + n, own, :] for n in range(together)], axis=1)
            part = grow(dot(lefts[k], right_of(x)), factors[k : k + 1, :1], SUBSTEPS)
            for n in range(together):
                out[r + n, own, :] = part[:, n * LANES : (n + 1) * LANES]


def add_kernel(mine, theirs, _, out):
    out[...] = mine[...] + theirs[...]


def lift_kernel(value, out):
    out[...] = value[...]


def join_kernel(mine, theirs, out):
    out[0] = mine[...]
    out[1] = theirs[...]


def combine_kernel(senders, mine, theirs, _, out, kept):
    tail = out.shape[1] - 1
    tile = out.shape[2] // senders
    for n in range(out.shape[0]):
        total = mine[n] + theirs[n]
        pressure = total[2 * SUBSTEPS]
        wall = 0.5 * pressure
        for t in range(SUBSTEPS - 1):
            out[n, t] = total[t] + total[SUBSTEPS + t] * wall
            out[n, SUBSTEPS - 1 + t] = total[SUBSTEPS + t]
        out[n, tail - 1] = pressure
        gas = total[SUBSTEPS - 1] + total[2 * SUBSTEPS - 1] * wall
        kept[n] = gas
        out[n, tail] = jnp.broadcast_to(total_of(gas), gas.shape)
        out[n, tail, :tile, :] = kept[n, pl.ds(lax.axis_index("cls") * tile, tile), :]


def total_of(x):
    tiles = jnp.sum(x.reshape(-1, GROUP, LANES), axis=0)
    return jnp.sum(jnp.sum(tiles, axis=1, keepdims=True), axis=0, keepdims=True)


def laplacian(x, plane):
    rows = x.shape[0]
    row = iota(x.shape, 0)
    lane = iota(x.shape, 1)
    per = plane // LANES
    inside = row % per * LANES + lane
    col = lane % SIDE
    total = jnp.where(col == 0, 0.0, pltpu.roll(x, 1, 1))
    total += jnp.where(col == SIDE - 1, 0.0, pltpu.roll(x, LANES - 1, 1))
    up = pltpu.roll(x, SIDE, 1)
    up = jnp.where(lane < SIDE, pltpu.roll(up, 1, 0), up)
    total += jnp.where(inside < SIDE, 0.0, up)
    down = pltpu.roll(x, LANES - SIDE, 1)
    down = jnp.where(lane >= LANES - SIDE, pltpu.roll(down, rows - 1, 0), down)
    total += jnp.where(inside >= plane - SIDE, 0.0, down)
    total += jnp.where(row < per, 0.0, pltpu.roll(x, per, 0))
    total += jnp.where(row >= rows - per, 0.0, pltpu.roll(x, rows - per, 0))
    return total - 6.0 * x


def finish_kernel(
    mine, theirs, shells, columns, out_hbm, pressure_out, out, window, walls_all, last, out_sems
):
    nodes, classes, cells = out.shape
    chunks = cells // LANES
    parts = nodes // GROUP
    width = GROUP * classes

    def piece(g):
        return pl.ds(g * GROUP, GROUP)

    plane = pressure_out.shape[1]
    cell = lax.axis_index("cell")
    even = cell % 2 == 0
    blocks = window.shape[0]
    for n, offset in enumerate(offsets(chip_bits(blocks))):
        for core in range(2):
            at = (cell | 1) ^ (offset + core)
            window[at] = jnp.where(even, theirs[2 * n + core], mine[2 * n + core])
    rows = blocks * chunks
    per = plane // LANES
    tile = pressure_out.shape[0] * per

    def field_of(f):
        return window[:, f].reshape(rows, LANES)

    field = field_of(2 * SUBSTEPS - 2)
    answer = field_of(SUBSTEPS - 1)
    answer_total = total_of(answer)
    chamber = None
    walls = []
    for t in range(SUBSTEPS):
        gas = answer * (0.5 * field) if t else field_of(0)
        for s in range(1, t):
            gas = gas + field_of(SUBSTEPS - 1 + t - s) * walls[s]
        if 0 < t < SUBSTEPS - 1:
            gas = gas + field_of(t)
        total = total_of(gas)
        if t == SUBSTEPS - 1:
            rest = jnp.sum(window[:, 2 * SUBSTEPS - 1], axis=0)
            total = total + rest[tile : tile + 1, :1]
        if t:
            field = field + 0.2 * chamber
            gas = gas + answer * (0.1 * chamber)
            total = total + answer_total * (0.1 * chamber)
        walls.append(0.5 * field)
        walls_all[t] = walls[t]
        field = 0.8 * field + 0.15 * laplacian(field, plane) + 0.1 * gas
        chamber = 1.5 - 0.5 * total / (rows * LANES)
    last[...] = field + 0.2 * chamber
    first = cell * chunks
    at = first + lax.axis_index("cls") * tile
    for i in range(tile):
        pressure_out[i // per : i // per + 1, (i % per) * LANES : (i % per + 1) * LANES] = (
            last[pl.ds(at + i, 1), :] + 0.1 * window[cell, 2 * SUBSTEPS - 1, i : i + 1, :]
        )
    right = []
    for r in range(chunks):
        wall = jnp.concatenate([walls_all[s, pl.ds(first + r, 1), :] for s in range(SUBSTEPS)], axis=0)
        high = wall.astype(jnp.bfloat16).astype(jnp.float32)
        right.append(jnp.concatenate([high, wall - high, high, jnp.zeros_like(high)], axis=0))
    right = jnp.concatenate(right, axis=1).astype(jnp.bfloat16)
    stores = [
        pltpu.make_async_copy(out.at[piece(g)], out_hbm.at[piece(g)], out_sems.at[g]) for g in range(parts)
    ]
    for g in range(parts):
        here = slice(g * width, (g + 1) * width)
        change = dot(columns[here, : 4 * SUBSTEPS].astype(jnp.bfloat16), right)
        for r in range(chunks):
            lanes = slice(r * LANES, (r + 1) * LANES)
            value = shells[r, here, :] + change[:, lanes]
            out[g * GROUP : (g + 1) * GROUP, :, lanes] = value.reshape(GROUP, classes, LANES)
        stores[g].start()
    for store in stores:
        store.wait()


HBM = pl.BlockSpec(memory_space=pltpu.HBM)
VMEM = pl.BlockSpec(memory_space=pltpu.VMEM)
DMA = pltpu.SemaphoreType.DMA


def chip_bits(count):
    return [1 << b for b in reversed(range(1, count.bit_length() - 1))]


def offsets(bits):
    found = [0]
    for bit in bits:
        found = found + [m ^ bit for m in found]
    return found


def swap_cores(value):
    return lax.ppermute(value, "cell", [(i, i ^ 1) for i in range(lax.axis_size("cell"))])


def swap(value, cell_bit, cls_bit):
    cells, classes = lax.axis_size("cell"), lax.axis_size("cls")
    pairs = [
        (i * classes + k, (i ^ cell_bit if i % 2 else i) * classes + (k ^ cls_bit if i % 2 else k))
        for i in range(cells)
        for k in range(classes)
    ]
    return lax.ppermute(value, ("cell", "cls"), pairs)


def shards(melt, counts, pressure, propagator, coupling, flux_weights):
    nodes, classes, cells = melt.shape
    chunks = cells // LANES
    f32 = jnp.float32
    split = (chunks, nodes * classes, LANES)
    whole = pltpu.CompilerParams(vmem_limit_bytes=60 * 2**20)
    most = pltpu.CompilerParams(vmem_limit_bytes=48 * 2**20)
    little = pltpu.CompilerParams(vmem_limit_bytes=32 * 2**20)
    cls_count = lax.axis_size("cls")
    cell_count = lax.axis_size("cell")
    prop_v = pltpu.VMEM((classes, nodes, nodes), f32)
    small = pltpu.VMEM((classes, nodes), f32)
    parts = nodes // GROUP
    packed = pl.pallas_call(
        fields_kernel,
        out_shape=jax.ShapeDtypeStruct((FIELDS + 1, chunks, LANES), f32),
        in_specs=[HBM] * 6,
        out_specs=VMEM,
        scratch_shapes=[
            pltpu.VMEM(melt.shape, f32),
            pltpu.VMEM((nodes * classes, cells), jnp.bfloat16),
            pltpu.VMEM((nodes * classes, cells), jnp.bfloat16),
            pltpu.VMEM(counts.shape, counts.dtype),
            pltpu.VMEM(pressure.shape, f32),
            prop_v,
            small,
            small,
            DMA((parts,)),
            DMA((5,)),
        ],
        compiler_params=whole,
        name="fields",
    )(melt, counts, pressure, propagator, coupling, flux_weights)
    lefts_shape = (classes, nodes, 3 * nodes)
    handed = swap_cores(packed)
    packed = pl.pallas_call(
        lift_kernel,
        out_shape=jax.ShapeDtypeStruct(packed.shape, f32),
        in_specs=[VMEM],
        out_specs=VMEM,
        compiler_params=little,
        cost_estimate=pl.CostEstimate(flops=10**8, bytes_accessed=10**6, transcendentals=0),
        name="lift",
    )(packed)
    packed = pl.pallas_call(
        join_kernel,
        out_shape=jax.ShapeDtypeStruct((2,) + packed.shape, f32),
        in_specs=[VMEM] * 2,
        out_specs=VMEM,
        compiler_params=little,
        name="join",
    )(packed, handed)
    theirs = swap(packed, 0, 1)
    lefts, columns, factors = pl.pallas_call(
        powers_kernel,
        out_shape=[
            jax.ShapeDtypeStruct(lefts_shape, jnp.bfloat16),
            jax.ShapeDtypeStruct(split[1:], f32),
            jax.ShapeDtypeStruct((classes, LANES), f32),
        ],
        in_specs=[HBM, HBM, VMEM],
        out_specs=[VMEM] * 3,
        scratch_shapes=[prop_v, small, DMA((2,))],
        compiler_params=most,
        cost_estimate=pl.CostEstimate(flops=10**9, bytes_accessed=10**6, transcendentals=0),
        name="powers",
    )(propagator, coupling, packed)
    distance = 1
    after = factors
    while 2 * distance < cls_count:
        distance *= 2
        packed = pl.pallas_call(
            add_kernel,
            out_shape=jax.ShapeDtypeStruct(packed.shape, f32),
            in_specs=[VMEM] * 3,
            out_specs=VMEM,
            compiler_params=little,
            name="add",
        )(packed, theirs, after)
        theirs = swap(packed, 0, distance)
    shells = pl.pallas_call(
        apply_kernel,
        out_shape=jax.ShapeDtypeStruct(split, f32),
        in_specs=[HBM, VMEM, VMEM, VMEM],
        out_specs=VMEM,
        scratch_shapes=[pltpu.VMEM(split, f32), DMA((chunks,))],
        compiler_params=most,
        cost_estimate=pl.CostEstimate(flops=10**9, bytes_accessed=melt.size * 4, transcendentals=0),
        name="apply",
    )(melt.reshape(nodes * classes, cells), lefts, factors, packed)
    fields = pl.pallas_call(
        functools.partial(combine_kernel, cls_count),
        out_shape=jax.ShapeDtypeStruct((2, FIELDS, chunks, LANES), f32),
        in_specs=[VMEM, VMEM, VMEM],
        out_specs=VMEM,
        scratch_shapes=[pltpu.VMEM((2, chunks, LANES), f32)],
        compiler_params=little,
        name="combine",
    )(packed, theirs, shells)
    held = fields
    for bit in chip_bits(cell_count):
        held = jnp.concatenate([held, swap(held, bit, 0)], axis=0)
    other = swap_cores(held)
    rows = cell_count * chunks
    return pl.pallas_call(
        finish_kernel,
        out_shape=[jax.ShapeDtypeStruct(melt.shape, f32), jax.ShapeDtypeStruct(pressure.shape, f32)],
        in_specs=[VMEM] * 4,
        out_specs=[HBM, VMEM],
        scratch_shapes=[
            pltpu.VMEM(melt.shape, f32),
            pltpu.VMEM((cell_count, FIELDS, chunks, LANES), f32),
            pltpu.VMEM((SUBSTEPS, rows, LANES), f32),
            pltpu.VMEM((rows, LANES), f32),
            DMA((parts,)),
        ],
        compiler_params=little,
        name="finish",
    )(held, other, shells, columns)


def solution(mesh):
    placed = (P(None, "cls", "cell"), P("cls", "cell"), P(("cell", "cls"), None), P(), P(), P())
    return jax.shard_map(
        shards,
        mesh=mesh,
        in_specs=placed,
        out_specs=(P(None, "cls", "cell"), P(("cell", "cls"), None)),
        check_vma=False,
    )
```

```python
import functools

import jax
import jax.numpy as jnp
from jax import lax
from jax.experimental import pallas as pl
from jax.experimental.pallas import tpu as pltpu
from jax.sharding import PartitionSpec as P

CLASSES = 32
SIDE = 16
SUBSTEPS = 4
COUNT_SCALE = 400.0
LANES = 128
GROUP = 8
FIELDS = 2 * SUBSTEPS


def grow(value, factor, times):
    for _ in range(times):
        value = value * factor
    return value


def iota(shape, dim):
    return lax.broadcasted_iota(jnp.int32, shape, dim)


def split2(x):
    high = x.astype(jnp.bfloat16)
    return high, (x - high.astype(jnp.float32)).astype(jnp.bfloat16)


def dot(a, b):
    return jnp.dot(a, b, preferred_element_type=jnp.float32)


def left_of(x):
    high, low = split2(x)
    return jnp.concatenate([high, high, low], axis=1)


def right_of(x):
    high, low = split2(x)
    return jnp.concatenate([high, low, high], axis=0)


def class_scale(prop):
    rows = [jnp.max(jnp.abs(prop[k]), axis=0, keepdims=True) for k in range(prop.shape[0])]
    return jnp.maximum(1.0, jnp.max(jnp.concatenate(rows, axis=0), axis=1, keepdims=True))


def param_copies(pairs, sems):
    copies = []
    for n, (source, target) in enumerate(pairs):
        own = pl.ds(lax.axis_index("cls") * target.shape[0], target.shape[0])
        copies.append(pltpu.make_async_copy(source.at[own], target, sems.at[n]))
    return copies


def fields_kernel(
    melt_hbm, counts_hbm, pressure_hbm, prop_hbm, coup_hbm, flux_hbm, out, melt, highs, lows, counts, pressure, prop, coup, flux, sems, other_sems
):
    nodes, classes, cells = melt.shape
    first = param_copies([(prop_hbm, prop), (flux_hbm, flux), (coup_hbm, coup)], other_sems)
    for copy in first:
        copy.start()
    parts = nodes // GROUP
    pieces = [
        pltpu.make_async_copy(
            melt_hbm.at[pl.ds(g * GROUP, GROUP)], melt.at[pl.ds(g * GROUP, GROUP)], sems.at[g]
        )
        for g in range(parts)
    ]
    for piece in pieces:
        piece.start()
    rest = [
        pltpu.make_async_copy(counts_hbm, counts, other_sems.at[3]),
        pltpu.make_async_copy(pressure_hbm, pressure, other_sems.at[4]),
    ]
    for copy in rest:
        copy.start()
    for copy in first:
        copy.wait()
    scale = class_scale(prop)
    width = classes * nodes
    table = jnp.concatenate(split2(prop[...].reshape(width, nodes)), axis=1)
    inverse = 1.0 / scale
    mask = iota((classes, width), 1) // nodes == iota((classes, width), 0)
    rows = [flux[...]]
    tall = GROUP * classes
    each = parts // SUBSTEPS
    for t in range(SUBSTEPS):
        wide = jnp.where(mask, jnp.concatenate([rows[-1]] * classes, axis=1), 0.0)
        pairs = dot(jnp.concatenate(split2(wide), axis=0), table)
        row = pairs[:classes] + pairs[classes:]
        rows.append((row[:, :nodes] + row[:, nodes:]) * inverse)
        for g in range(t * each, parts if t == SUBSTEPS - 1 else (t + 1) * each):
            pieces[g].wait()
            here = slice(g * tall, (g + 1) * tall)
            highs[here, :], lows[here, :] = split2(
                melt[g * GROUP : (g + 1) * GROUP].reshape(tall, cells)
            )
    spread_out = (iota((nodes, width), 1) // classes == iota((nodes, width), 0)).astype(jnp.bfloat16)
    parts_of_rows = jnp.concatenate(split2(jnp.concatenate(rows[1:], axis=0)), axis=0)
    dense = dot(parts_of_rows, spread_out)
    same = iota(dense.shape, 0) % classes == iota(dense.shape, 1) % classes
    dense = jnp.where(same, dense, 0.0).astype(jnp.bfloat16)
    count = SUBSTEPS * classes
    fluxes = dot(dense, highs[...])
    fluxes = fluxes[:count] + fluxes[count:] + dot(dense[:count], lows[...])
    spread = [
        grow(jnp.sum(rows[d] * coup[...], axis=1, keepdims=True), scale, d) for d in range(SUBSTEPS)
    ]
    for copy in rest:
        copy.wait()
    counts_n = counts[...].astype(jnp.float32) / (COUNT_SCALE * CLASSES)
    chunks = cells // LANES
    for r in range(chunks):
        here = counts_n[:, r * LANES : (r + 1) * LANES]
        for t in range(SUBSTEPS):
            part = fluxes[t * classes : (t + 1) * classes, r * LANES : (r + 1) * LANES]
            out[t, r : r + 1, :] = jnp.sum(grow(here * part, scale, t + 1), axis=0, keepdims=True)
        for d in range(SUBSTEPS):
            out[SUBSTEPS + d, r : r + 1, :] = jnp.sum(here * spread[d], axis=0, keepdims=True)
    out[2 * SUBSTEPS] = jnp.zeros((chunks, LANES), jnp.float32)
    per = pressure.shape[1] // LANES
    tile = pressure.shape[0] * per
    at = lax.axis_index("cls") * tile
    for i in range(tile):
        out[2 * SUBSTEPS, pl.ds(at + i, 1), :] = pressure[
            i // per : i // per + 1, (i % per) * LANES : (i % per + 1) * LANES
        ]


def powers_kernel(prop_hbm, coup_hbm, _, lefts, columns, factors, prop, coup, param_sems):
    classes, nodes = prop.shape[:2]
    params = param_copies([(prop_hbm, prop), (coup_hbm, coup)], param_sems)
    for copy in params:
        copy.start()
    for copy in params:
        copy.wait()
    scale = class_scale(prop)
    factors[...] = jnp.broadcast_to(scale, factors.shape)
    inverse = 1.0 / scale
    every = range(classes)
    unit = [prop[k] * inverse[k : k + 1, :] for k in every]
    first = [left_of(unit[k]) for k in every]
    square = [dot(first[k], right_of(unit[k])) for k in every]
    second = [left_of(square[k]) for k in every]
    for k in every:
        lefts[k] = left_of(dot(second[k], right_of(square[k])))
    start = jnp.concatenate(
        [jnp.transpose(coup[...]), jnp.zeros((nodes, LANES - classes), jnp.float32)], axis=1
    )
    once = [dot(first[k], right_of(start)) for k in every]
    start = start[:, :classes]
    twice = [
        dot(second[k], right_of(jnp.concatenate([start, once[k][:, :classes]], axis=1))) for k in every
    ]
    lane = iota((nodes, LANES), 1)
    for k in every:
        powers = [
            start[:, k : k + 1],
            once[k][:, k : k + 1],
            twice[k][:, k : k + 1],
            twice[k][:, classes + k : classes + k + 1],
        ]
        value = jnp.zeros((nodes, LANES), jnp.float32)
        for d in range(SUBSTEPS):
            grown = grow(powers[d], scale[k : k + 1, :], d)
            value = jnp.where(lane % SUBSTEPS == SUBSTEPS - 1 - d, grown, value)
        high = value.astype(jnp.bfloat16).astype(jnp.float32)
        value = jnp.where(lane < 2 * SUBSTEPS, high, jnp.where(lane < 3 * SUBSTEPS, value - high, 0.0))
        columns[pl.ds(k, nodes, stride=classes), :] = value


def apply_kernel(melt_hbm, lefts, factors, _, out, melt, sems):
    chunks = melt.shape[0]
    classes, nodes = lefts.shape[:2]
    loads = [
        pltpu.make_async_copy(melt_hbm.at[:, pl.ds(r * LANES, LANES)], melt.at[r], sems.at[r])
        for r in range(chunks)
    ]
    for load in loads:
        load.start()
    together = 2 if chunks % 2 == 0 else 1
    for r in range(0, chunks, together):
        for n in range(together):
            loads[r + n].wait()
        for k in range(classes):
            own = pl.ds(k, nodes, stride=classes)
            x = jnp.concatenate([melt[r + n, own, :] for n in range(together)], axis=1)
            part = grow(dot(lefts[k], right_of(x)), factors[k : k + 1, :1], SUBSTEPS)
            for n in range(together):
                out[r + n, own, :] = part[:, n * LANES : (n + 1) * LANES]


def add_kernel(mine, theirs, _, out):
    out[...] = mine[...] + theirs[...]


def combine_kernel(senders, mine, theirs, _, out, kept):
    total = mine[...] + theirs[...]
    tail = out.shape[1] - 1
    tile = out.shape[2] // senders
    pressure = total[2 * SUBSTEPS]
    wall = 0.5 * pressure
    gas = total[SUBSTEPS - 1] + total[2 * SUBSTEPS - 1] * wall
    kept[...] = gas
    own = kept[pl.ds(lax.axis_index("cls") * tile, tile), :]
    gas_total = jnp.broadcast_to(total_of(gas), gas.shape)
    for n in range(out.shape[0]):
        for t in range(SUBSTEPS - 1):
            out[n, t] = total[t] + total[SUBSTEPS + t] * wall
            out[n, SUBSTEPS - 1 + t] = total[SUBSTEPS + t]
        out[n, tail - 1] = pressure
        out[n, tail] = gas_total
        out[n, tail, :tile, :] = own


def total_of(x):
    tiles = jnp.sum(x.reshape(-1, GROUP, LANES), axis=0)
    return jnp.sum(jnp.sum(tiles, axis=1, keepdims=True), axis=0, keepdims=True)


def laplacian(x, plane):
    rows = x.shape[0]
    row = iota(x.shape, 0)
    lane = iota(x.shape, 1)
    per = plane // LANES
    inside = row % per * LANES + lane
    col = lane % SIDE
    total = jnp.where(col == 0, 0.0, pltpu.roll(x, 1, 1))
    total += jnp.where(col == SIDE - 1, 0.0, pltpu.roll(x, LANES - 1, 1))
    up = pltpu.roll(x, SIDE, 1)
    up = jnp.where(lane < SIDE, pltpu.roll(up, 1, 0), up)
    total += jnp.where(inside < SIDE, 0.0, up)
    down = pltpu.roll(x, LANES - SIDE, 1)
    down = jnp.where(lane >= LANES - SIDE, pltpu.roll(down, rows - 1, 0), down)
    total += jnp.where(inside >= plane - SIDE, 0.0, down)
    total += jnp.where(row < per, 0.0, pltpu.roll(x, per, 0))
    total += jnp.where(row >= rows - per, 0.0, pltpu.roll(x, rows - per, 0))
    return total - 6.0 * x


def finish_kernel(
    mine, theirs, shells, columns, out_hbm, pressure_out, out, walls_all, last, out_sems
):
    nodes, classes, cells = out.shape
    chunks = cells // LANES
    parts = nodes // GROUP
    width = GROUP * classes

    def piece(g):
        return pl.ds(g * GROUP, GROUP)

    plane = pressure_out.shape[1]
    cell = lax.axis_index("cell")
    even = cell % 2 == 0
    blocks = 2 * mine.shape[0]
    rows = blocks * chunks
    per = plane // LANES
    tile = pressure_out.shape[0] * per

    def field_of(f):
        first, second = mine[:, f], theirs[:, f]
        low, high = jnp.where(even, first, second), jnp.where(even, second, first)
        return jnp.stack([low, high], axis=1).reshape(rows, LANES)

    field = field_of(2 * SUBSTEPS - 2)
    answer = field_of(SUBSTEPS - 1)
    answer_total = total_of(answer)
    chamber = None
    walls = []
    for t in range(SUBSTEPS):
        gas = answer * (0.5 * field) if t else field_of(0)
        for s in range(1, t):
            gas = gas + field_of(SUBSTEPS - 1 + t - s) * walls[s]
        if 0 < t < SUBSTEPS - 1:
            gas = gas + field_of(t)
        total = total_of(gas)
        if t == SUBSTEPS - 1:
            rest = jnp.sum(mine[:, 2 * SUBSTEPS - 1] + theirs[:, 2 * SUBSTEPS - 1], axis=0)
            total = total + rest[tile : tile + 1, :1]
        if t:
            field = field + 0.2 * chamber
            gas = gas + answer * (0.1 * chamber)
            total = total + answer_total * (0.1 * chamber)
        walls.append(0.5 * field)
        walls_all[t] = walls[t]
        field = 0.8 * field + 0.15 * laplacian(field, plane) + 0.1 * gas
        chamber = 1.5 - 0.5 * total / (rows * LANES)
    last[...] = field + 0.2 * chamber
    first = cell * chunks
    at = first + lax.axis_index("cls") * tile
    for i in range(tile):
        pressure_out[i // per : i // per + 1, (i % per) * LANES : (i % per + 1) * LANES] = (
            last[pl.ds(at + i, 1), :] + 0.1 * mine[cell // 2, 2 * SUBSTEPS - 1, i : i + 1, :]
        )
    right = []
    for r in range(chunks):
        wall = jnp.concatenate([walls_all[s, pl.ds(first + r, 1), :] for s in range(SUBSTEPS)], axis=0)
        high = wall.astype(jnp.bfloat16).astype(jnp.float32)
        right.append(jnp.concatenate([high, wall - high, high, jnp.zeros_like(high)], axis=0))
    right = jnp.concatenate(right, axis=1).astype(jnp.bfloat16)
    stores = [
        pltpu.make_async_copy(out.at[piece(g)], out_hbm.at[piece(g)], out_sems.at[g]) for g in range(parts)
    ]
    for g in range(parts):
        here = slice(g * width, (g + 1) * width)
        change = dot(columns[here, : 4 * SUBSTEPS].astype(jnp.bfloat16), right)
        for r in range(chunks):
            lanes = slice(r * LANES, (r + 1) * LANES)
            value = shells[r, here, :] + change[:, lanes]
            out[g * GROUP : (g + 1) * GROUP, :, lanes] = value.reshape(GROUP, classes, LANES)
        stores[g].start()
    for store in stores:
        store.wait()


HBM = pl.BlockSpec(memory_space=pltpu.HBM)
VMEM = pl.BlockSpec(memory_space=pltpu.VMEM)
DMA = pltpu.SemaphoreType.DMA


def partner(value, axis, distance):
    return lax.ppermute(value, axis, [(i, i ^ distance) for i in range(lax.axis_size(axis))])


def shards(melt, counts, pressure, propagator, coupling, flux_weights):
    nodes, classes, cells = melt.shape
    chunks = cells // LANES
    f32 = jnp.float32
    split = (chunks, nodes * classes, LANES)
    whole = pltpu.CompilerParams(vmem_limit_bytes=60 * 2**20)
    most = pltpu.CompilerParams(vmem_limit_bytes=48 * 2**20)
    little = pltpu.CompilerParams(vmem_limit_bytes=32 * 2**20)
    cls_count = lax.axis_size("cls")
    cell_count = lax.axis_size("cell")
    prop_v = pltpu.VMEM((classes, nodes, nodes), f32)
    small = pltpu.VMEM((classes, nodes), f32)
    parts = nodes // GROUP
    packed = pl.pallas_call(
        fields_kernel,
        out_shape=jax.ShapeDtypeStruct((FIELDS + 1, chunks, LANES), f32),
        in_specs=[HBM] * 6,
        out_specs=VMEM,
        scratch_shapes=[
            pltpu.VMEM(melt.shape, f32),
            pltpu.VMEM((nodes * classes, cells), jnp.bfloat16),
            pltpu.VMEM((nodes * classes, cells), jnp.bfloat16),
            pltpu.VMEM(counts.shape, counts.dtype),
            pltpu.VMEM(pressure.shape, f32),
            prop_v,
            small,
            small,
            DMA((parts,)),
            DMA((5,)),
        ],
        compiler_params=whole,
        name="fields",
    )(melt, counts, pressure, propagator, coupling, flux_weights)
    lefts_shape = (classes, nodes, 3 * nodes)
    theirs = partner(packed, "cls", 1)
    lefts, columns, factors = pl.pallas_call(
        powers_kernel,
        out_shape=[
            jax.ShapeDtypeStruct(lefts_shape, jnp.bfloat16),
            jax.ShapeDtypeStruct(split[1:], f32),
            jax.ShapeDtypeStruct((classes, LANES), f32),
        ],
        in_specs=[HBM, HBM, VMEM],
        out_specs=[VMEM] * 3,
        scratch_shapes=[prop_v, small, DMA((2,))],
        compiler_params=most,
        cost_estimate=pl.CostEstimate(flops=10**9, bytes_accessed=10**6, transcendentals=0),
        name="powers",
    )(propagator, coupling, packed)
    distance = 1
    after = factors
    while 2 * distance < cls_count:
        distance *= 2
        packed = pl.pallas_call(
            add_kernel,
            out_shape=jax.ShapeDtypeStruct(packed.shape, f32),
            in_specs=[VMEM] * 3,
            out_specs=VMEM,
            compiler_params=little,
            name="add",
        )(packed, theirs, after)
        theirs = partner(packed, "cls", distance)
    shells = pl.pallas_call(
        apply_kernel,
        out_shape=jax.ShapeDtypeStruct(split, f32),
        in_specs=[HBM, VMEM, VMEM, VMEM],
        out_specs=VMEM,
        scratch_shapes=[pltpu.VMEM(split, f32), DMA((chunks,))],
        compiler_params=most,
        cost_estimate=pl.CostEstimate(flops=10**9, bytes_accessed=melt.size * 4, transcendentals=0),
        name="apply",
    )(melt.reshape(nodes * classes, cells), lefts, factors, packed)
    fields = pl.pallas_call(
        functools.partial(combine_kernel, cls_count),
        out_shape=jax.ShapeDtypeStruct((cell_count // 2, FIELDS, chunks, LANES), f32),
        in_specs=[VMEM, VMEM, VMEM],
        out_specs=VMEM,
        scratch_shapes=[pltpu.VMEM((chunks, LANES), f32)],
        compiler_params=little,
        name="combine",
    )(packed, theirs, shells)
    groups = [list(range(core, cell_count, 2)) for core in range(2)]
    own = lax.all_to_all(
        fields, "cell", split_axis=0, concat_axis=0, tiled=True, axis_index_groups=groups
    )
    other = partner(own, "cell", 1)
    rows = cell_count * chunks
    return pl.pallas_call(
        finish_kernel,
        out_shape=[jax.ShapeDtypeStruct(melt.shape, f32), jax.ShapeDtypeStruct(pressure.shape, f32)],
        in_specs=[VMEM] * 4,
        out_specs=[HBM, VMEM],
        scratch_shapes=[
            pltpu.VMEM(melt.shape, f32),
            pltpu.VMEM((SUBSTEPS, rows, LANES), f32),
            pltpu.VMEM((rows, LANES), f32),
            DMA((parts,)),
        ],
        compiler_params=little,
        name="finish",
    )(own, other, shells, columns)


def solution(mesh):
    placed = (P(None, "cls", "cell"), P("cls", "cell"), P(("cell", "cls"), None), P(), P(), P())
    return jax.shard_map(
        shards,
        mesh=mesh,
        in_specs=placed,
        out_specs=(P(None, "cls", "cell"), P(("cell", "cls"), None)),
        check_vma=False,
    )
```

```python
import functools

import jax
import jax.numpy as jnp
from jax import lax
from jax.experimental import pallas as pl
from jax.experimental.pallas import tpu as pltpu
from jax.sharding import PartitionSpec as P

CLASSES = 32
SIDE = 16
SUBSTEPS = 4
COUNT_SCALE = 400.0
LANES = 128
GROUP = 8
FIELDS = 2 * SUBSTEPS


def grow(value, factor, times):
    for _ in range(times):
        value = value * factor
    return value


def iota(shape, dim):
    return lax.broadcasted_iota(jnp.int32, shape, dim)


def split2(x):
    high = x.astype(jnp.bfloat16)
    return high, (x - high.astype(jnp.float32)).astype(jnp.bfloat16)


def dot(a, b):
    return jnp.dot(a, b, preferred_element_type=jnp.float32)


def left_of(x):
    high, low = split2(x)
    return jnp.concatenate([high, high, low], axis=1)


def right_of(x):
    high, low = split2(x)
    return jnp.concatenate([high, low, high], axis=0)


def class_scale(prop):
    rows = [jnp.max(jnp.abs(prop[k]), axis=0, keepdims=True) for k in range(prop.shape[0])]
    return jnp.maximum(1.0, jnp.max(jnp.concatenate(rows, axis=0), axis=1, keepdims=True))


def param_copies(pairs, sems):
    copies = []
    for n, (source, target) in enumerate(pairs):
        own = pl.ds(lax.axis_index("cls") * target.shape[0], target.shape[0])
        copies.append(pltpu.make_async_copy(source.at[own], target, sems.at[n]))
    return copies


def fields_kernel(
    melt_hbm, counts_hbm, pressure_hbm, prop_hbm, coup_hbm, flux_hbm, out, melt, highs, lows, counts, pressure, prop, coup, flux, sems, other_sems
):
    nodes, classes, cells = melt.shape
    first = param_copies([(prop_hbm, prop), (flux_hbm, flux), (coup_hbm, coup)], other_sems)
    for copy in first:
        copy.start()
    parts = nodes // GROUP
    pieces = [
        pltpu.make_async_copy(
            melt_hbm.at[pl.ds(g * GROUP, GROUP)], melt.at[pl.ds(g * GROUP, GROUP)], sems.at[g]
        )
        for g in range(parts)
    ]
    for piece in pieces:
        piece.start()
    rest = [
        pltpu.make_async_copy(counts_hbm, counts, other_sems.at[3]),
        pltpu.make_async_copy(pressure_hbm, pressure, other_sems.at[4]),
    ]
    for copy in rest:
        copy.start()
    for copy in first:
        copy.wait()
    scale = class_scale(prop)
    width = classes * nodes
    table = jnp.concatenate(split2(prop[...].reshape(width, nodes)), axis=1)
    inverse = 1.0 / scale
    mask = iota((classes, width), 1) // nodes == iota((classes, width), 0)
    rows = [flux[...]]
    tall = GROUP * classes
    each = parts // SUBSTEPS
    for t in range(SUBSTEPS):
        wide = jnp.where(mask, jnp.concatenate([rows[-1]] * classes, axis=1), 0.0)
        pairs = dot(jnp.concatenate(split2(wide), axis=0), table)
        row = pairs[:classes] + pairs[classes:]
        rows.append((row[:, :nodes] + row[:, nodes:]) * inverse)
        for g in range(t * each, parts if t == SUBSTEPS - 1 else (t + 1) * each):
            pieces[g].wait()
            here = slice(g * tall, (g + 1) * tall)
            highs[here, :], lows[here, :] = split2(
                melt[g * GROUP : (g + 1) * GROUP].reshape(tall, cells)
            )
    spread_out = (iota((nodes, width), 1) // classes == iota((nodes, width), 0)).astype(jnp.bfloat16)
    parts_of_rows = jnp.concatenate(split2(jnp.concatenate(rows[1:], axis=0)), axis=0)
    dense = dot(parts_of_rows, spread_out)
    same = iota(dense.shape, 0) % classes == iota(dense.shape, 1) % classes
    dense = jnp.where(same, dense, 0.0).astype(jnp.bfloat16)
    count = SUBSTEPS * classes
    fluxes = dot(dense, highs[...])
    fluxes = fluxes[:count] + fluxes[count:] + dot(dense[:count], lows[...])
    spread = [
        grow(jnp.sum(rows[d] * coup[...], axis=1, keepdims=True), scale, d) for d in range(SUBSTEPS)
    ]
    for copy in rest:
        copy.wait()
    counts_n = counts[...].astype(jnp.float32) / (COUNT_SCALE * CLASSES)
    chunks = cells // LANES
    for r in range(chunks):
        here = counts_n[:, r * LANES : (r + 1) * LANES]
        for t in range(SUBSTEPS):
            part = fluxes[t * classes : (t + 1) * classes, r * LANES : (r + 1) * LANES]
            out[t, r : r + 1, :] = jnp.sum(grow(here * part, scale, t + 1), axis=0, keepdims=True)
        for d in range(SUBSTEPS):
            out[SUBSTEPS + d, r : r + 1, :] = jnp.sum(here * spread[d], axis=0, keepdims=True)
    out[2 * SUBSTEPS] = jnp.zeros((chunks, LANES), jnp.float32)
    per = pressure.shape[1] // LANES
    tile = pressure.shape[0] * per
    at = lax.axis_index("cls") * tile
    for i in range(tile):
        out[2 * SUBSTEPS, pl.ds(at + i, 1), :] = pressure[
            i // per : i // per + 1, (i % per) * LANES : (i % per + 1) * LANES
        ]


def powers_kernel(prop_hbm, coup_hbm, _, lefts, columns, factors, prop, coup, param_sems):
    classes, nodes = prop.shape[:2]
    params = param_copies([(prop_hbm, prop), (coup_hbm, coup)], param_sems)
    for copy in params:
        copy.start()
    for copy in params:
        copy.wait()
    scale = class_scale(prop)
    factors[...] = jnp.broadcast_to(scale, factors.shape)
    inverse = 1.0 / scale
    every = range(classes)
    unit = [prop[k] * inverse[k : k + 1, :] for k in every]
    first = [left_of(unit[k]) for k in every]
    square = [dot(first[k], right_of(unit[k])) for k in every]
    second = [left_of(square[k]) for k in every]
    for k in every:
        lefts[k] = left_of(dot(second[k], right_of(square[k])))
    start = jnp.concatenate(
        [jnp.transpose(coup[...]), jnp.zeros((nodes, LANES - classes), jnp.float32)], axis=1
    )
    once = [dot(first[k], right_of(start)) for k in every]
    start = start[:, :classes]
    twice = [
        dot(second[k], right_of(jnp.concatenate([start, once[k][:, :classes]], axis=1))) for k in every
    ]
    lane = iota((nodes, LANES), 1)
    for k in every:
        powers = [
            start[:, k : k + 1],
            once[k][:, k : k + 1],
            twice[k][:, k : k + 1],
            twice[k][:, classes + k : classes + k + 1],
        ]
        value = jnp.zeros((nodes, LANES), jnp.float32)
        for d in range(SUBSTEPS):
            grown = grow(powers[d], scale[k : k + 1, :], d)
            value = jnp.where(lane % SUBSTEPS == SUBSTEPS - 1 - d, grown, value)
        high = value.astype(jnp.bfloat16).astype(jnp.float32)
        value = jnp.where(lane < 2 * SUBSTEPS, high, jnp.where(lane < 3 * SUBSTEPS, value - high, 0.0))
        columns[pl.ds(k, nodes, stride=classes), :] = value


def apply_kernel(melt_hbm, lefts, factors, _, out, melt, sems):
    chunks = melt.shape[0]
    classes, nodes = lefts.shape[:2]
    loads = [
        pltpu.make_async_copy(melt_hbm.at[:, pl.ds(r * LANES, LANES)], melt.at[r], sems.at[r])
        for r in range(chunks)
    ]
    for load in loads:
        load.start()
    together = 2 if chunks % 2 == 0 else 1
    for r in range(0, chunks, together):
        for n in range(together):
            loads[r + n].wait()
        for k in range(classes):
            own = pl.ds(k, nodes, stride=classes)
            x = jnp.concatenate([melt[r + n, own, :] for n in range(together)], axis=1)
            part = grow(dot(lefts[k], right_of(x)), factors[k : k + 1, :1], SUBSTEPS)
            for n in range(together):
                out[r + n, own, :] = part[:, n * LANES : (n + 1) * LANES]


def add_kernel(mine, theirs, _, out):
    out[...] = mine[...] + theirs[...]


def combine_kernel(senders, mine, theirs, _, out_ref, kept):
    out = out_ref.at[0]
    total = mine[...] + theirs[...]
    tail = out.shape[0] - 1
    tile = out.shape[1] // senders
    pressure = total[2 * SUBSTEPS]
    wall = 0.5 * pressure
    for t in range(SUBSTEPS - 1):
        out[t] = total[t] + total[SUBSTEPS + t] * wall
        out[SUBSTEPS - 1 + t] = total[SUBSTEPS + t]
    out[tail - 1] = pressure
    gas = total[SUBSTEPS - 1] + total[2 * SUBSTEPS - 1] * wall
    kept[...] = gas
    out[tail] = jnp.broadcast_to(total_of(gas), gas.shape)
    out[tail, :tile, :] = kept[pl.ds(lax.axis_index("cls") * tile, tile), :]


def total_of(x):
    tiles = jnp.sum(x.reshape(-1, GROUP, LANES), axis=0)
    return jnp.sum(jnp.sum(tiles, axis=1, keepdims=True), axis=0, keepdims=True)


def laplacian(x, plane):
    rows = x.shape[0]
    row = iota(x.shape, 0)
    lane = iota(x.shape, 1)
    per = plane // LANES
    inside = row % per * LANES + lane
    col = lane % SIDE
    total = jnp.where(col == 0, 0.0, pltpu.roll(x, 1, 1))
    total += jnp.where(col == SIDE - 1, 0.0, pltpu.roll(x, LANES - 1, 1))
    up = pltpu.roll(x, SIDE, 1)
    up = jnp.where(lane < SIDE, pltpu.roll(up, 1, 0), up)
    total += jnp.where(inside < SIDE, 0.0, up)
    down = pltpu.roll(x, LANES - SIDE, 1)
    down = jnp.where(lane >= LANES - SIDE, pltpu.roll(down, rows - 1, 0), down)
    total += jnp.where(inside >= plane - SIDE, 0.0, down)
    total += jnp.where(row < per, 0.0, pltpu.roll(x, per, 0))
    total += jnp.where(row >= rows - per, 0.0, pltpu.roll(x, rows - per, 0))
    return total - 6.0 * x


def finish_kernel(
    mine, theirs, shells, columns, out_hbm, pressure_out, out, window, walls_all, last, out_sems
):
    nodes, classes, cells = out.shape
    chunks = cells // LANES
    parts = nodes // GROUP
    width = GROUP * classes

    def piece(g):
        return pl.ds(g * GROUP, GROUP)

    plane = pressure_out.shape[1]
    cell = lax.axis_index("cell")
    blocks = window.shape[0]
    for n, offset in enumerate(offsets(blocks)):
        window[cell ^ offset] = mine[n]
        window[cell ^ 1 ^ offset] = theirs[n]
    rows = blocks * chunks
    per = plane // LANES
    tile = pressure_out.shape[0] * per

    def field_of(f):
        return window[:, f].reshape(rows, LANES)

    field = field_of(2 * SUBSTEPS - 2)
    answer = field_of(SUBSTEPS - 1)
    answer_total = total_of(answer)
    chamber = None
    walls = []
    for t in range(SUBSTEPS):
        gas = answer * (0.5 * field) if t else field_of(0)
        for s in range(1, t):
            gas = gas + field_of(SUBSTEPS - 1 + t - s) * walls[s]
        if 0 < t < SUBSTEPS - 1:
            gas = gas + field_of(t)
        total = total_of(gas)
        if t == SUBSTEPS - 1:
            rest = jnp.sum(window[:, 2 * SUBSTEPS - 1], axis=0)
            total = total + rest[tile : tile + 1, :1]
        if t:
            field = field + 0.2 * chamber
            gas = gas + answer * (0.1 * chamber)
            total = total + answer_total * (0.1 * chamber)
        walls.append(0.5 * field)
        walls_all[t] = walls[t]
        field = 0.8 * field + 0.15 * laplacian(field, plane) + 0.1 * gas
        chamber = 1.5 - 0.5 * total / (rows * LANES)
    last[...] = field + 0.2 * chamber
    first = cell * chunks
    at = first + lax.axis_index("cls") * tile
    for i in range(tile):
        pressure_out[i // per : i // per + 1, (i % per) * LANES : (i % per + 1) * LANES] = (
            last[pl.ds(at + i, 1), :] + 0.1 * mine[0, 2 * SUBSTEPS - 1, i : i + 1, :]
        )
    right = []
    for r in range(chunks):
        wall = jnp.concatenate([walls_all[s, pl.ds(first + r, 1), :] for s in range(SUBSTEPS)], axis=0)
        high = wall.astype(jnp.bfloat16).astype(jnp.float32)
        right.append(jnp.concatenate([high, wall - high, high, jnp.zeros_like(high)], axis=0))
    right = jnp.concatenate(right, axis=1).astype(jnp.bfloat16)
    stores = [
        pltpu.make_async_copy(out.at[piece(g)], out_hbm.at[piece(g)], out_sems.at[g]) for g in range(parts)
    ]
    for g in range(parts):
        here = slice(g * width, (g + 1) * width)
        change = dot(columns[here, : 4 * SUBSTEPS].astype(jnp.bfloat16), right)
        for r in range(chunks):
            lanes = slice(r * LANES, (r + 1) * LANES)
            value = shells[r, here, :] + change[:, lanes]
            out[g * GROUP : (g + 1) * GROUP, :, lanes] = value.reshape(GROUP, classes, LANES)
        stores[g].start()
    for store in stores:
        store.wait()


HBM = pl.BlockSpec(memory_space=pltpu.HBM)
VMEM = pl.BlockSpec(memory_space=pltpu.VMEM)
DMA = pltpu.SemaphoreType.DMA


def stages(count):
    bits = [1 << b for b in range(1, count.bit_length() - 1)]
    pairs = [bits[n : n + 2] for n in range(0, len(bits), 2)]
    return [[sum(pair)] + pair[::-1] if len(pair) > 1 else pair for pair in pairs]


def offsets(count):
    found = [0]
    for stage in stages(count):
        found = found + [m ^ offset for offset in stage[::-1] for m in found]
    return found


def partner(value, axis, distance):
    return lax.ppermute(value, axis, [(i, i ^ distance) for i in range(lax.axis_size(axis))])


def shards(melt, counts, pressure, propagator, coupling, flux_weights):
    nodes, classes, cells = melt.shape
    chunks = cells // LANES
    f32 = jnp.float32
    split = (chunks, nodes * classes, LANES)
    whole = pltpu.CompilerParams(vmem_limit_bytes=60 * 2**20)
    most = pltpu.CompilerParams(vmem_limit_bytes=48 * 2**20)
    little = pltpu.CompilerParams(vmem_limit_bytes=32 * 2**20)
    cls_count = lax.axis_size("cls")
    cell_count = lax.axis_size("cell")
    prop_v = pltpu.VMEM((classes, nodes, nodes), f32)
    small = pltpu.VMEM((classes, nodes), f32)
    parts = nodes // GROUP
    packed = pl.pallas_call(
        fields_kernel,
        out_shape=jax.ShapeDtypeStruct((FIELDS + 1, chunks, LANES), f32),
        in_specs=[HBM] * 6,
        out_specs=VMEM,
        scratch_shapes=[
            pltpu.VMEM(melt.shape, f32),
            pltpu.VMEM((nodes * classes, cells), jnp.bfloat16),
            pltpu.VMEM((nodes * classes, cells), jnp.bfloat16),
            pltpu.VMEM(counts.shape, counts.dtype),
            pltpu.VMEM(pressure.shape, f32),
            prop_v,
            small,
            small,
            DMA((parts,)),
            DMA((5,)),
        ],
        compiler_params=whole,
        name="fields",
    )(melt, counts, pressure, propagator, coupling, flux_weights)
    lefts_shape = (classes, nodes, 3 * nodes)
    theirs = partner(packed, "cls", 1)
    lefts, columns, factors = pl.pallas_call(
        powers_kernel,
        out_shape=[
            jax.ShapeDtypeStruct(lefts_shape, jnp.bfloat16),
            jax.ShapeDtypeStruct(split[1:], f32),
            jax.ShapeDtypeStruct((classes, LANES), f32),
        ],
        in_specs=[HBM, HBM, VMEM],
        out_specs=[VMEM] * 3,
        scratch_shapes=[prop_v, small, DMA((2,))],
        compiler_params=most,
        cost_estimate=pl.CostEstimate(flops=10**9, bytes_accessed=10**6, transcendentals=0),
        name="powers",
    )(propagator, coupling, packed)
    distance = 1
    after = factors
    while 2 * distance < cls_count:
        distance *= 2
        packed = pl.pallas_call(
            add_kernel,
            out_shape=jax.ShapeDtypeStruct(packed.shape, f32),
            in_specs=[VMEM] * 3,
            out_specs=VMEM,
            compiler_params=little,
            name="add",
        )(packed, theirs, after)
        theirs = partner(packed, "cls", distance)
    shells = pl.pallas_call(
        apply_kernel,
        out_shape=jax.ShapeDtypeStruct(split, f32),
        in_specs=[HBM, VMEM, VMEM, VMEM],
        out_specs=VMEM,
        scratch_shapes=[pltpu.VMEM(split, f32), DMA((chunks,))],
        compiler_params=most,
        cost_estimate=pl.CostEstimate(flops=10**9, bytes_accessed=melt.size * 4, transcendentals=0),
        name="apply",
    )(melt.reshape(nodes * classes, cells), lefts, factors, packed)
    fields = pl.pallas_call(
        functools.partial(combine_kernel, cls_count),
        out_shape=jax.ShapeDtypeStruct((1, FIELDS, chunks, LANES), f32),
        in_specs=[VMEM, VMEM, VMEM],
        out_specs=VMEM,
        scratch_shapes=[pltpu.VMEM((chunks, LANES), f32)],
        compiler_params=little,
        name="combine",
    )(packed, theirs, shells)
    held = fields
    for stage in stages(cell_count):
        arrived = [partner(held, "cell", offset) for offset in stage]
        held = jnp.concatenate([held] + arrived[::-1], axis=0)
    other = partner(held, "cell", 1)
    rows = cell_count * chunks
    return pl.pallas_call(
        finish_kernel,
        out_shape=[jax.ShapeDtypeStruct(melt.shape, f32), jax.ShapeDtypeStruct(pressure.shape, f32)],
        in_specs=[VMEM] * 4,
        out_specs=[HBM, VMEM],
        scratch_shapes=[
            pltpu.VMEM(melt.shape, f32),
            pltpu.VMEM((cell_count, FIELDS, chunks, LANES), f32),
            pltpu.VMEM((SUBSTEPS, rows, LANES), f32),
            pltpu.VMEM((rows, LANES), f32),
            DMA((parts,)),
        ],
        compiler_params=little,
        name="finish",
    )(held, other, shells, columns)


def solution(mesh):
    placed = (P(None, "cls", "cell"), P("cls", "cell"), P(("cell", "cls"), None), P(), P(), P())
    return jax.shard_map(
        shards,
        mesh=mesh,
        in_specs=placed,
        out_specs=(P(None, "cls", "cell"), P(("cell", "cls"), None)),
        check_vma=False,
    )
```

```python
import functools

import jax
import jax.numpy as jnp
from jax import lax
from jax.experimental import pallas as pl
from jax.experimental.pallas import tpu as pltpu
from jax.sharding import PartitionSpec as P

CLASSES = 32
SIDE = 16
SUBSTEPS = 4
COUNT_SCALE = 400.0
LANES = 128
GROUP = 8
FIELDS = 2 * SUBSTEPS


def grow(value, factor, times):
    for _ in range(times):
        value = value * factor
    return value


def iota(shape, dim):
    return lax.broadcasted_iota(jnp.int32, shape, dim)


def split2(x):
    high = x.astype(jnp.bfloat16)
    return high, (x - high.astype(jnp.float32)).astype(jnp.bfloat16)


def dot(a, b):
    return jnp.dot(a, b, preferred_element_type=jnp.float32)


def left_of(x):
    high, low = split2(x)
    return jnp.concatenate([high, high, low], axis=1)


def right_of(x):
    high, low = split2(x)
    return jnp.concatenate([high, low, high], axis=0)


def class_scale(prop):
    rows = [jnp.max(jnp.abs(prop[k]), axis=0, keepdims=True) for k in range(prop.shape[0])]
    return jnp.maximum(1.0, jnp.max(jnp.concatenate(rows, axis=0), axis=1, keepdims=True))


def param_copies(pairs, sems):
    copies = []
    for n, (source, target) in enumerate(pairs):
        own = pl.ds(lax.axis_index("cls") * target.shape[0], target.shape[0])
        copies.append(pltpu.make_async_copy(source.at[own], target, sems.at[n]))
    return copies


def fields_kernel(
    melt_hbm, counts_hbm, pressure_hbm, prop_hbm, coup_hbm, flux_hbm, out, melt, highs, lows, counts, pressure, prop, coup, flux, sems, other_sems
):
    nodes, classes, cells = melt.shape
    first = param_copies([(prop_hbm, prop), (flux_hbm, flux), (coup_hbm, coup)], other_sems)
    for copy in first:
        copy.start()
    parts = nodes // GROUP
    pieces = [
        pltpu.make_async_copy(
            melt_hbm.at[pl.ds(g * GROUP, GROUP)], melt.at[pl.ds(g * GROUP, GROUP)], sems.at[g]
        )
        for g in range(parts)
    ]
    for piece in pieces:
        piece.start()
    rest = [
        pltpu.make_async_copy(counts_hbm, counts, other_sems.at[3]),
        pltpu.make_async_copy(pressure_hbm, pressure, other_sems.at[4]),
    ]
    for copy in rest:
        copy.start()
    for copy in first:
        copy.wait()
    scale = class_scale(prop)
    width = classes * nodes
    table = jnp.concatenate(split2(prop[...].reshape(width, nodes)), axis=1)
    inverse = 1.0 / scale
    mask = iota((classes, width), 1) // nodes == iota((classes, width), 0)
    rows = [flux[...]]
    tall = GROUP * classes
    each = parts // SUBSTEPS
    for t in range(SUBSTEPS):
        wide = jnp.where(mask, jnp.concatenate([rows[-1]] * classes, axis=1), 0.0)
        pairs = dot(jnp.concatenate(split2(wide), axis=0), table)
        row = pairs[:classes] + pairs[classes:]
        rows.append((row[:, :nodes] + row[:, nodes:]) * inverse)
        for g in range(t * each, parts if t == SUBSTEPS - 1 else (t + 1) * each):
            pieces[g].wait()
            here = slice(g * tall, (g + 1) * tall)
            highs[here, :], lows[here, :] = split2(
                melt[g * GROUP : (g + 1) * GROUP].reshape(tall, cells)
            )
    spread_out = (iota((nodes, width), 1) // classes == iota((nodes, width), 0)).astype(jnp.bfloat16)
    parts_of_rows = jnp.concatenate(split2(jnp.concatenate(rows[1:], axis=0)), axis=0)
    dense = dot(parts_of_rows, spread_out)
    same = iota(dense.shape, 0) % classes == iota(dense.shape, 1) % classes
    dense = jnp.where(same, dense, 0.0).astype(jnp.bfloat16)
    count = SUBSTEPS * classes
    fluxes = dot(dense, highs[...])
    fluxes = fluxes[:count] + fluxes[count:] + dot(dense[:count], lows[...])
    spread = [
        grow(jnp.sum(rows[d] * coup[...], axis=1, keepdims=True), scale, d) for d in range(SUBSTEPS)
    ]
    for copy in rest:
        copy.wait()
    counts_n = counts[...].astype(jnp.float32) / (COUNT_SCALE * CLASSES)
    chunks = cells // LANES
    for r in range(chunks):
        here = counts_n[:, r * LANES : (r + 1) * LANES]
        for t in range(SUBSTEPS):
            part = fluxes[t * classes : (t + 1) * classes, r * LANES : (r + 1) * LANES]
            out[t, r : r + 1, :] = jnp.sum(grow(here * part, scale, t + 1), axis=0, keepdims=True)
        for d in range(SUBSTEPS):
            out[SUBSTEPS + d, r : r + 1, :] = jnp.sum(here * spread[d], axis=0, keepdims=True)
    out[2 * SUBSTEPS] = jnp.zeros((chunks, LANES), jnp.float32)
    per = pressure.shape[1] // LANES
    tile = pressure.shape[0] * per
    at = lax.axis_index("cls") * tile
    for i in range(tile):
        out[2 * SUBSTEPS, pl.ds(at + i, 1), :] = pressure[
            i // per : i // per + 1, (i % per) * LANES : (i % per + 1) * LANES
        ]


def powers_kernel(prop_hbm, coup_hbm, _, lefts, columns, factors, prop, coup, param_sems):
    classes, nodes = prop.shape[:2]
    params = param_copies([(prop_hbm, prop), (coup_hbm, coup)], param_sems)
    for copy in params:
        copy.start()
    for copy in params:
        copy.wait()
    scale = class_scale(prop)
    factors[...] = jnp.broadcast_to(scale, factors.shape)
    inverse = 1.0 / scale
    every = range(classes)
    unit = [prop[k] * inverse[k : k + 1, :] for k in every]
    first = [left_of(unit[k]) for k in every]
    square = [dot(first[k], right_of(unit[k])) for k in every]
    second = [left_of(square[k]) for k in every]
    for k in every:
        lefts[k] = left_of(dot(second[k], right_of(square[k])))
    start = jnp.concatenate(
        [jnp.transpose(coup[...]), jnp.zeros((nodes, LANES - classes), jnp.float32)], axis=1
    )
    once = [dot(first[k], right_of(start)) for k in every]
    start = start[:, :classes]
    twice = [
        dot(second[k], right_of(jnp.concatenate([start, once[k][:, :classes]], axis=1))) for k in every
    ]
    lane = iota((nodes, LANES), 1)
    for k in every:
        powers = [
            start[:, k : k + 1],
            once[k][:, k : k + 1],
            twice[k][:, k : k + 1],
            twice[k][:, classes + k : classes + k + 1],
        ]
        value = jnp.zeros((nodes, LANES), jnp.float32)
        for d in range(SUBSTEPS):
            grown = grow(powers[d], scale[k : k + 1, :], d)
            value = jnp.where(lane % SUBSTEPS == SUBSTEPS - 1 - d, grown, value)
        high = value.astype(jnp.bfloat16).astype(jnp.float32)
        value = jnp.where(lane < 2 * SUBSTEPS, high, jnp.where(lane < 3 * SUBSTEPS, value - high, 0.0))
        columns[pl.ds(k, nodes, stride=classes), :] = value


def apply_kernel(melt_hbm, lefts, factors, _, out, melt, sems):
    chunks = melt.shape[0]
    classes, nodes = lefts.shape[:2]
    loads = [
        pltpu.make_async_copy(melt_hbm.at[:, pl.ds(r * LANES, LANES)], melt.at[r], sems.at[r])
        for r in range(chunks)
    ]
    for load in loads:
        load.start()
    together = 2 if chunks % 2 == 0 else 1
    for r in range(0, chunks, together):
        for n in range(together):
            loads[r + n].wait()
        for k in range(classes):
            own = pl.ds(k, nodes, stride=classes)
            x = jnp.concatenate([melt[r + n, own, :] for n in range(together)], axis=1)
            part = grow(dot(lefts[k], right_of(x)), factors[k : k + 1, :1], SUBSTEPS)
            for n in range(together):
                out[r + n, own, :] = part[:, n * LANES : (n + 1) * LANES]


def add_kernel(mine, theirs, _, out):
    out[...] = mine[...] + theirs[...]


def combine_kernel(senders, mine, theirs, _, out_ref, kept):
    out = out_ref.at[0]
    total = mine[...] + theirs[...]
    tail = out.shape[0] - 1
    tile = out.shape[1] // senders
    pressure = total[2 * SUBSTEPS]
    wall = 0.5 * pressure
    for t in range(SUBSTEPS - 1):
        out[t] = total[t] + total[SUBSTEPS + t] * wall
        out[SUBSTEPS - 1 + t] = total[SUBSTEPS + t]
    out[tail - 1] = pressure
    gas = total[SUBSTEPS - 1] + total[2 * SUBSTEPS - 1] * wall
    kept[...] = gas
    out[tail] = jnp.broadcast_to(total_of(gas), gas.shape)
    out[tail, :tile, :] = kept[pl.ds(lax.axis_index("cls") * tile, tile), :]


def total_of(x):
    tiles = jnp.sum(x.reshape(-1, GROUP, LANES), axis=0)
    return jnp.sum(jnp.sum(tiles, axis=1, keepdims=True), axis=0, keepdims=True)


def laplacian(x, plane):
    rows = x.shape[0]
    row = iota(x.shape, 0)
    lane = iota(x.shape, 1)
    per = plane // LANES
    inside = row % per * LANES + lane
    col = lane % SIDE
    total = jnp.where(col == 0, 0.0, pltpu.roll(x, 1, 1))
    total += jnp.where(col == SIDE - 1, 0.0, pltpu.roll(x, LANES - 1, 1))
    up = pltpu.roll(x, SIDE, 1)
    up = jnp.where(lane < SIDE, pltpu.roll(up, 1, 0), up)
    total += jnp.where(inside < SIDE, 0.0, up)
    down = pltpu.roll(x, LANES - SIDE, 1)
    down = jnp.where(lane >= LANES - SIDE, pltpu.roll(down, rows - 1, 0), down)
    total += jnp.where(inside >= plane - SIDE, 0.0, down)
    total += jnp.where(row < per, 0.0, pltpu.roll(x, per, 0))
    total += jnp.where(row >= rows - per, 0.0, pltpu.roll(x, rows - per, 0))
    return total - 6.0 * x


def finish_kernel(
    mine, theirs, shells, columns, out_hbm, pressure_out, out, window, walls_all, last, out_sems
):
    nodes, classes, cells = out.shape
    chunks = cells // LANES
    parts = nodes // GROUP
    width = GROUP * classes

    def piece(g):
        return pl.ds(g * GROUP, GROUP)

    plane = pressure_out.shape[1]
    cell = lax.axis_index("cell")
    blocks = window.shape[0]
    for n, offset in enumerate(offsets(blocks)):
        window[cell ^ offset] = mine[n]
        window[cell ^ 1 ^ offset] = theirs[n]
    rows = blocks * chunks
    per = plane // LANES
    tile = pressure_out.shape[0] * per

    def field_of(f):
        return window[:, f].reshape(rows, LANES)

    field = field_of(2 * SUBSTEPS - 2)
    answer = field_of(SUBSTEPS - 1)
    answer_total = total_of(answer)
    chamber = None
    walls = []
    for t in range(SUBSTEPS):
        gas = answer * (0.5 * field) if t else field_of(0)
        for s in range(1, t):
            gas = gas + field_of(SUBSTEPS - 1 + t - s) * walls[s]
        if 0 < t < SUBSTEPS - 1:
            gas = gas + field_of(t)
        total = total_of(gas)
        if t == SUBSTEPS - 1:
            rest = jnp.sum(window[:, 2 * SUBSTEPS - 1], axis=0)
            total = total + rest[tile : tile + 1, :1]
        if t:
            field = field + 0.2 * chamber
            gas = gas + answer * (0.1 * chamber)
            total = total + answer_total * (0.1 * chamber)
        walls.append(0.5 * field)
        walls_all[t] = walls[t]
        field = 0.8 * field + 0.15 * laplacian(field, plane) + 0.1 * gas
        chamber = 1.5 - 0.5 * total / (rows * LANES)
    last[...] = field + 0.2 * chamber
    first = cell * chunks
    at = first + lax.axis_index("cls") * tile
    for i in range(tile):
        pressure_out[i // per : i // per + 1, (i % per) * LANES : (i % per + 1) * LANES] = (
            last[pl.ds(at + i, 1), :] + 0.1 * mine[0, 2 * SUBSTEPS - 1, i : i + 1, :]
        )
    right = []
    for r in range(chunks):
        wall = jnp.concatenate([walls_all[s, pl.ds(first + r, 1), :] for s in range(SUBSTEPS)], axis=0)
        high = wall.astype(jnp.bfloat16).astype(jnp.float32)
        right.append(jnp.concatenate([high, wall - high, high, jnp.zeros_like(high)], axis=0))
    right = jnp.concatenate(right, axis=1).astype(jnp.bfloat16)
    stores = [
        pltpu.make_async_copy(out.at[piece(g)], out_hbm.at[piece(g)], out_sems.at[g]) for g in range(parts)
    ]
    for g in range(parts):
        here = slice(g * width, (g + 1) * width)
        change = dot(columns[here, : 4 * SUBSTEPS].astype(jnp.bfloat16), right)
        for r in range(chunks):
            lanes = slice(r * LANES, (r + 1) * LANES)
            value = shells[r, here, :] + change[:, lanes]
            out[g * GROUP : (g + 1) * GROUP, :, lanes] = value.reshape(GROUP, classes, LANES)
        stores[g].start()
    for store in stores:
        store.wait()


HBM = pl.BlockSpec(memory_space=pltpu.HBM)
VMEM = pl.BlockSpec(memory_space=pltpu.VMEM)
DMA = pltpu.SemaphoreType.DMA


def stages(count):
    bits = [1 << b for b in range(1, count.bit_length() - 1)]
    pairs = [bits[n : n + 2] for n in range(0, len(bits), 2)]
    return [pair + [sum(pair)] if len(pair) > 1 else pair for pair in pairs]


def offsets(count):
    found = [0]
    for stage in stages(count):
        found = found + [m ^ offset for offset in stage for m in found]
    return found


def partner(value, axis, distance):
    return lax.ppermute(value, axis, [(i, i ^ distance) for i in range(lax.axis_size(axis))])


def shards(melt, counts, pressure, propagator, coupling, flux_weights):
    nodes, classes, cells = melt.shape
    chunks = cells // LANES
    f32 = jnp.float32
    split = (chunks, nodes * classes, LANES)
    whole = pltpu.CompilerParams(vmem_limit_bytes=60 * 2**20)
    most = pltpu.CompilerParams(vmem_limit_bytes=48 * 2**20)
    little = pltpu.CompilerParams(vmem_limit_bytes=32 * 2**20)
    cls_count = lax.axis_size("cls")
    cell_count = lax.axis_size("cell")
    prop_v = pltpu.VMEM((classes, nodes, nodes), f32)
    small = pltpu.VMEM((classes, nodes), f32)
    parts = nodes // GROUP
    packed = pl.pallas_call(
        fields_kernel,
        out_shape=jax.ShapeDtypeStruct((FIELDS + 1, chunks, LANES), f32),
        in_specs=[HBM] * 6,
        out_specs=VMEM,
        scratch_shapes=[
            pltpu.VMEM(melt.shape, f32),
            pltpu.VMEM((nodes * classes, cells), jnp.bfloat16),
            pltpu.VMEM((nodes * classes, cells), jnp.bfloat16),
            pltpu.VMEM(counts.shape, counts.dtype),
            pltpu.VMEM(pressure.shape, f32),
            prop_v,
            small,
            small,
            DMA((parts,)),
            DMA((5,)),
        ],
        compiler_params=whole,
        name="fields",
    )(melt, counts, pressure, propagator, coupling, flux_weights)
    lefts_shape = (classes, nodes, 3 * nodes)
    theirs = partner(packed, "cls", 1)
    lefts, columns, factors = pl.pallas_call(
        powers_kernel,
        out_shape=[
            jax.ShapeDtypeStruct(lefts_shape, jnp.bfloat16),
            jax.ShapeDtypeStruct(split[1:], f32),
            jax.ShapeDtypeStruct((classes, LANES), f32),
        ],
        in_specs=[HBM, HBM, VMEM],
        out_specs=[VMEM] * 3,
        scratch_shapes=[prop_v, small, DMA((2,))],
        compiler_params=most,
        cost_estimate=pl.CostEstimate(flops=10**9, bytes_accessed=10**6, transcendentals=0),
        name="powers",
    )(propagator, coupling, packed)
    distance = 1
    after = factors
    while 2 * distance < cls_count:
        distance *= 2
        packed = pl.pallas_call(
            add_kernel,
            out_shape=jax.ShapeDtypeStruct(packed.shape, f32),
            in_specs=[VMEM] * 3,
            out_specs=VMEM,
            compiler_params=little,
            name="add",
        )(packed, theirs, after)
        theirs = partner(packed, "cls", distance)
    shells = pl.pallas_call(
        apply_kernel,
        out_shape=jax.ShapeDtypeStruct(split, f32),
        in_specs=[HBM, VMEM, VMEM, VMEM],
        out_specs=VMEM,
        scratch_shapes=[pltpu.VMEM(split, f32), DMA((chunks,))],
        compiler_params=most,
        cost_estimate=pl.CostEstimate(flops=10**9, bytes_accessed=melt.size * 4, transcendentals=0),
        name="apply",
    )(melt.reshape(nodes * classes, cells), lefts, factors, packed)
    fields = pl.pallas_call(
        functools.partial(combine_kernel, cls_count),
        out_shape=jax.ShapeDtypeStruct((1, FIELDS, chunks, LANES), f32),
        in_specs=[VMEM, VMEM, VMEM],
        out_specs=VMEM,
        scratch_shapes=[pltpu.VMEM((chunks, LANES), f32)],
        compiler_params=little,
        name="combine",
    )(packed, theirs, shells)
    held = fields
    for stage in stages(cell_count):
        arrived = [partner(held, "cell", offset) for offset in stage]
        held = jnp.concatenate([held] + arrived, axis=0)
    other = partner(held, "cell", 1)
    rows = cell_count * chunks
    return pl.pallas_call(
        finish_kernel,
        out_shape=[jax.ShapeDtypeStruct(melt.shape, f32), jax.ShapeDtypeStruct(pressure.shape, f32)],
        in_specs=[VMEM] * 4,
        out_specs=[HBM, VMEM],
        scratch_shapes=[
            pltpu.VMEM(melt.shape, f32),
            pltpu.VMEM((cell_count, FIELDS, chunks, LANES), f32),
            pltpu.VMEM((SUBSTEPS, rows, LANES), f32),
            pltpu.VMEM((rows, LANES), f32),
            DMA((parts,)),
        ],
        compiler_params=little,
        name="finish",
    )(held, other, shells, columns)


def solution(mesh):
    placed = (P(None, "cls", "cell"), P("cls", "cell"), P(("cell", "cls"), None), P(), P(), P())
    return jax.shard_map(
        shards,
        mesh=mesh,
        in_specs=placed,
        out_specs=(P(None, "cls", "cell"), P(("cell", "cls"), None)),
        check_vma=False,
    )
```

```python
import functools

import jax
import jax.numpy as jnp
from jax import lax
from jax.experimental import pallas as pl
from jax.experimental.pallas import tpu as pltpu
from jax.sharding import PartitionSpec as P

CLASSES = 32
SIDE = 16
SUBSTEPS = 4
COUNT_SCALE = 400.0
LANES = 128
GROUP = 8
FIELDS = 2 * SUBSTEPS


def grow(value, factor, times):
    for _ in range(times):
        value = value * factor
    return value


def iota(shape, dim):
    return lax.broadcasted_iota(jnp.int32, shape, dim)


def split2(x):
    high = x.astype(jnp.bfloat16)
    return high, (x - high.astype(jnp.float32)).astype(jnp.bfloat16)


def dot(a, b):
    return jnp.dot(a, b, preferred_element_type=jnp.float32)


def left_of(x):
    high, low = split2(x)
    return jnp.concatenate([high, high, low], axis=1)


def right_of(x):
    high, low = split2(x)
    return jnp.concatenate([high, low, high], axis=0)


def class_scale(prop):
    rows = [jnp.max(jnp.abs(prop[k]), axis=0, keepdims=True) for k in range(prop.shape[0])]
    return jnp.maximum(1.0, jnp.max(jnp.concatenate(rows, axis=0), axis=1, keepdims=True))


def param_copies(pairs, sems):
    copies = []
    for n, (source, target) in enumerate(pairs):
        own = pl.ds(lax.axis_index("cls") * target.shape[0], target.shape[0])
        copies.append(pltpu.make_async_copy(source.at[own], target, sems.at[n]))
    return copies


def fields_kernel(
    melt_hbm, counts_hbm, pressure_hbm, prop_hbm, coup_hbm, flux_hbm, out, melt, highs, lows, counts, pressure, prop, coup, flux, sems, other_sems
):
    nodes, classes, cells = melt.shape
    first = param_copies([(prop_hbm, prop), (flux_hbm, flux), (coup_hbm, coup)], other_sems)
    for copy in first:
        copy.start()
    parts = nodes // GROUP
    pieces = [
        pltpu.make_async_copy(
            melt_hbm.at[pl.ds(g * GROUP, GROUP)], melt.at[pl.ds(g * GROUP, GROUP)], sems.at[g]
        )
        for g in range(parts)
    ]
    for piece in pieces:
        piece.start()
    rest = [
        pltpu.make_async_copy(counts_hbm, counts, other_sems.at[3]),
        pltpu.make_async_copy(pressure_hbm, pressure, other_sems.at[4]),
    ]
    for copy in rest:
        copy.start()
    for copy in first:
        copy.wait()
    scale = class_scale(prop)
    width = classes * nodes
    table = jnp.concatenate(split2(prop[...].reshape(width, nodes)), axis=1)
    inverse = 1.0 / scale
    mask = iota((classes, width), 1) // nodes == iota((classes, width), 0)
    rows = [flux[...]]
    tall = GROUP * classes
    each = parts // SUBSTEPS
    for t in range(SUBSTEPS):
        wide = jnp.where(mask, jnp.concatenate([rows[-1]] * classes, axis=1), 0.0)
        pairs = dot(jnp.concatenate(split2(wide), axis=0), table)
        row = pairs[:classes] + pairs[classes:]
        rows.append((row[:, :nodes] + row[:, nodes:]) * inverse)
        for g in range(t * each, parts if t == SUBSTEPS - 1 else (t + 1) * each):
            pieces[g].wait()
            here = slice(g * tall, (g + 1) * tall)
            highs[here, :], lows[here, :] = split2(
                melt[g * GROUP : (g + 1) * GROUP].reshape(tall, cells)
            )
    spread_out = (iota((nodes, width), 1) // classes == iota((nodes, width), 0)).astype(jnp.bfloat16)
    parts_of_rows = jnp.concatenate(split2(jnp.concatenate(rows[1:], axis=0)), axis=0)
    dense = dot(parts_of_rows, spread_out)
    same = iota(dense.shape, 0) % classes == iota(dense.shape, 1) % classes
    dense = jnp.where(same, dense, 0.0).astype(jnp.bfloat16)
    count = SUBSTEPS * classes
    fluxes = dot(dense, highs[...])
    fluxes = fluxes[:count] + fluxes[count:] + dot(dense[:count], lows[...])
    spread = [
        grow(jnp.sum(rows[d] * coup[...], axis=1, keepdims=True), scale, d) for d in range(SUBSTEPS)
    ]
    for copy in rest:
        copy.wait()
    counts_n = counts[...].astype(jnp.float32) / (COUNT_SCALE * CLASSES)
    chunks = cells // LANES
    for r in range(chunks):
        here = counts_n[:, r * LANES : (r + 1) * LANES]
        for t in range(SUBSTEPS):
            part = fluxes[t * classes : (t + 1) * classes, r * LANES : (r + 1) * LANES]
            out[t, r : r + 1, :] = jnp.sum(grow(here * part, scale, t + 1), axis=0, keepdims=True)
        for d in range(SUBSTEPS):
            out[SUBSTEPS + d, r : r + 1, :] = jnp.sum(here * spread[d], axis=0, keepdims=True)
    out[2 * SUBSTEPS] = jnp.zeros((chunks, LANES), jnp.float32)
    per = pressure.shape[1] // LANES
    tile = pressure.shape[0] * per
    at = lax.axis_index("cls") * tile
    for i in range(tile):
        out[2 * SUBSTEPS, pl.ds(at + i, 1), :] = pressure[
            i // per : i // per + 1, (i % per) * LANES : (i % per + 1) * LANES
        ]


def powers_kernel(prop_hbm, coup_hbm, _, lefts, columns, factors, prop, coup, param_sems):
    classes, nodes = prop.shape[:2]
    params = param_copies([(prop_hbm, prop), (coup_hbm, coup)], param_sems)
    for copy in params:
        copy.start()
    for copy in params:
        copy.wait()
    scale = class_scale(prop)
    factors[...] = jnp.broadcast_to(scale, factors.shape)
    inverse = 1.0 / scale
    every = range(classes)
    unit = [prop[k] * inverse[k : k + 1, :] for k in every]
    first = [left_of(unit[k]) for k in every]
    square = [dot(first[k], right_of(unit[k])) for k in every]
    second = [left_of(square[k]) for k in every]
    for k in every:
        lefts[k] = left_of(dot(second[k], right_of(square[k])))
    start = jnp.concatenate(
        [jnp.transpose(coup[...]), jnp.zeros((nodes, LANES - classes), jnp.float32)], axis=1
    )
    once = [dot(first[k], right_of(start)) for k in every]
    start = start[:, :classes]
    twice = [
        dot(second[k], right_of(jnp.concatenate([start, once[k][:, :classes]], axis=1))) for k in every
    ]
    lane = iota((nodes, LANES), 1)
    for k in every:
        powers = [
            start[:, k : k + 1],
            once[k][:, k : k + 1],
            twice[k][:, k : k + 1],
            twice[k][:, classes + k : classes + k + 1],
        ]
        value = jnp.zeros((nodes, LANES), jnp.float32)
        for d in range(SUBSTEPS):
            grown = grow(powers[d], scale[k : k + 1, :], d)
            value = jnp.where(lane % SUBSTEPS == SUBSTEPS - 1 - d, grown, value)
        high = value.astype(jnp.bfloat16).astype(jnp.float32)
        value = jnp.where(lane < 2 * SUBSTEPS, high, jnp.where(lane < 3 * SUBSTEPS, value - high, 0.0))
        columns[pl.ds(k, nodes, stride=classes), :] = value


def apply_kernel(melt_hbm, lefts, factors, _, out, melt, sems):
    chunks = melt.shape[0]
    classes, nodes = lefts.shape[:2]
    loads = [
        pltpu.make_async_copy(melt_hbm.at[:, pl.ds(r * LANES, LANES)], melt.at[r], sems.at[r])
        for r in range(chunks)
    ]
    for load in loads:
        load.start()
    together = 2 if chunks % 2 == 0 else 1
    for r in range(0, chunks, together):
        for n in range(together):
            loads[r + n].wait()
        for k in range(classes):
            own = pl.ds(k, nodes, stride=classes)
            x = jnp.concatenate([melt[r + n, own, :] for n in range(together)], axis=1)
            part = grow(dot(lefts[k], right_of(x)), factors[k : k + 1, :1], SUBSTEPS)
            for n in range(together):
                out[r + n, own, :] = part[:, n * LANES : (n + 1) * LANES]


def add_kernel(mine, theirs, _, out):
    out[...] = mine[...] + theirs[...]


def combine_kernel(senders, mine, theirs, _, out_ref, kept):
    out = out_ref.at[0]
    total = mine[...] + theirs[...]
    tail = out.shape[0] - 1
    tile = out.shape[1] // senders
    pressure = total[2 * SUBSTEPS]
    wall = 0.5 * pressure
    for t in range(SUBSTEPS - 1):
        out[t] = total[t] + total[SUBSTEPS + t] * wall
        out[SUBSTEPS - 1 + t] = total[SUBSTEPS + t]
    out[tail - 1] = pressure
    gas = total[SUBSTEPS - 1] + total[2 * SUBSTEPS - 1] * wall
    kept[...] = gas
    out[tail] = jnp.broadcast_to(total_of(gas), gas.shape)
    out[tail, :tile, :] = kept[pl.ds(lax.axis_index("cls") * tile, tile), :]


def total_of(x):
    tiles = jnp.sum(x.reshape(-1, GROUP, LANES), axis=0)
    return jnp.sum(jnp.sum(tiles, axis=1, keepdims=True), axis=0, keepdims=True)


def laplacian(x, plane):
    rows = x.shape[0]
    row = iota(x.shape, 0)
    lane = iota(x.shape, 1)
    per = plane // LANES
    inside = row % per * LANES + lane
    col = lane % SIDE
    total = jnp.where(col == 0, 0.0, pltpu.roll(x, 1, 1))
    total += jnp.where(col == SIDE - 1, 0.0, pltpu.roll(x, LANES - 1, 1))
    up = pltpu.roll(x, SIDE, 1)
    up = jnp.where(lane < SIDE, pltpu.roll(up, 1, 0), up)
    total += jnp.where(inside < SIDE, 0.0, up)
    down = pltpu.roll(x, LANES - SIDE, 1)
    down = jnp.where(lane >= LANES - SIDE, pltpu.roll(down, rows - 1, 0), down)
    total += jnp.where(inside >= plane - SIDE, 0.0, down)
    total += jnp.where(row < per, 0.0, pltpu.roll(x, per, 0))
    total += jnp.where(row >= rows - per, 0.0, pltpu.roll(x, rows - per, 0))
    return total - 6.0 * x


def finish_kernel(count, *refs):
    mine, theirs = refs[:count], refs[count : 2 * count]
    shells, columns, out_hbm, pressure_out, out, window, walls_all, last, out_sems = refs[2 * count :]
    nodes, classes, cells = out.shape
    chunks = cells // LANES
    parts = nodes // GROUP
    width = GROUP * classes

    def piece(g):
        return pl.ds(g * GROUP, GROUP)

    plane = pressure_out.shape[1]
    cell = lax.axis_index("cell")
    blocks = window.shape[0]
    for n, offset in enumerate(offsets(blocks)):
        part, slot = n // mine[0].shape[0], n % mine[0].shape[0]
        window[cell ^ offset] = mine[part][slot]
        window[cell ^ 1 ^ offset] = theirs[part][slot]
    rows = blocks * chunks
    per = plane // LANES
    tile = pressure_out.shape[0] * per

    def field_of(f):
        return window[:, f].reshape(rows, LANES)

    field = field_of(2 * SUBSTEPS - 2)
    answer = field_of(SUBSTEPS - 1)
    answer_total = total_of(answer)
    chamber = None
    walls = []
    for t in range(SUBSTEPS):
        gas = answer * (0.5 * field) if t else field_of(0)
        for s in range(1, t):
            gas = gas + field_of(SUBSTEPS - 1 + t - s) * walls[s]
        if 0 < t < SUBSTEPS - 1:
            gas = gas + field_of(t)
        total = total_of(gas)
        if t == SUBSTEPS - 1:
            rest = jnp.sum(window[:, 2 * SUBSTEPS - 1], axis=0)
            total = total + rest[tile : tile + 1, :1]
        if t:
            field = field + 0.2 * chamber
            gas = gas + answer * (0.1 * chamber)
            total = total + answer_total * (0.1 * chamber)
        walls.append(0.5 * field)
        walls_all[t] = walls[t]
        field = 0.8 * field + 0.15 * laplacian(field, plane) + 0.1 * gas
        chamber = 1.5 - 0.5 * total / (rows * LANES)
    last[...] = field + 0.2 * chamber
    first = cell * chunks
    at = first + lax.axis_index("cls") * tile
    for i in range(tile):
        pressure_out[i // per : i // per + 1, (i % per) * LANES : (i % per + 1) * LANES] = (
            last[pl.ds(at + i, 1), :] + 0.1 * mine[0][0, 2 * SUBSTEPS - 1, i : i + 1, :]
        )
    right = []
    for r in range(chunks):
        wall = jnp.concatenate([walls_all[s, pl.ds(first + r, 1), :] for s in range(SUBSTEPS)], axis=0)
        high = wall.astype(jnp.bfloat16).astype(jnp.float32)
        right.append(jnp.concatenate([high, wall - high, high, jnp.zeros_like(high)], axis=0))
    right = jnp.concatenate(right, axis=1).astype(jnp.bfloat16)
    stores = [
        pltpu.make_async_copy(out.at[piece(g)], out_hbm.at[piece(g)], out_sems.at[g]) for g in range(parts)
    ]
    for g in range(parts):
        here = slice(g * width, (g + 1) * width)
        change = dot(columns[here, : 4 * SUBSTEPS].astype(jnp.bfloat16), right)
        for r in range(chunks):
            lanes = slice(r * LANES, (r + 1) * LANES)
            value = shells[r, here, :] + change[:, lanes]
            out[g * GROUP : (g + 1) * GROUP, :, lanes] = value.reshape(GROUP, classes, LANES)
        stores[g].start()
    for store in stores:
        store.wait()


HBM = pl.BlockSpec(memory_space=pltpu.HBM)
VMEM = pl.BlockSpec(memory_space=pltpu.VMEM)
DMA = pltpu.SemaphoreType.DMA


def stages(count):
    bits = [1 << b for b in range(1, count.bit_length() - 1)]
    pairs = [bits[n : n + 2] for n in range(0, len(bits), 2)]
    return [[sum(pair)] + pair[::-1] if len(pair) > 1 else pair for pair in pairs]


def offsets(count):
    found = [0]
    for stage in stages(count):
        found = found + [m ^ offset for offset in stage[::-1] for m in found]
    return found


def partner(value, axis, distance):
    return lax.ppermute(value, axis, [(i, i ^ distance) for i in range(lax.axis_size(axis))])


def shards(melt, counts, pressure, propagator, coupling, flux_weights):
    nodes, classes, cells = melt.shape
    chunks = cells // LANES
    f32 = jnp.float32
    split = (chunks, nodes * classes, LANES)
    whole = pltpu.CompilerParams(vmem_limit_bytes=60 * 2**20)
    most = pltpu.CompilerParams(vmem_limit_bytes=48 * 2**20)
    little = pltpu.CompilerParams(vmem_limit_bytes=32 * 2**20)
    cls_count = lax.axis_size("cls")
    cell_count = lax.axis_size("cell")
    prop_v = pltpu.VMEM((classes, nodes, nodes), f32)
    small = pltpu.VMEM((classes, nodes), f32)
    parts = nodes // GROUP
    packed = pl.pallas_call(
        fields_kernel,
        out_shape=jax.ShapeDtypeStruct((FIELDS + 1, chunks, LANES), f32),
        in_specs=[HBM] * 6,
        out_specs=VMEM,
        scratch_shapes=[
            pltpu.VMEM(melt.shape, f32),
            pltpu.VMEM((nodes * classes, cells), jnp.bfloat16),
            pltpu.VMEM((nodes * classes, cells), jnp.bfloat16),
            pltpu.VMEM(counts.shape, counts.dtype),
            pltpu.VMEM(pressure.shape, f32),
            prop_v,
            small,
            small,
            DMA((parts,)),
            DMA((5,)),
        ],
        compiler_params=whole,
        name="fields",
    )(melt, counts, pressure, propagator, coupling, flux_weights)
    lefts_shape = (classes, nodes, 3 * nodes)
    theirs = partner(packed, "cls", 1)
    lefts, columns, factors = pl.pallas_call(
        powers_kernel,
        out_shape=[
            jax.ShapeDtypeStruct(lefts_shape, jnp.bfloat16),
            jax.ShapeDtypeStruct(split[1:], f32),
            jax.ShapeDtypeStruct((classes, LANES), f32),
        ],
        in_specs=[HBM, HBM, VMEM],
        out_specs=[VMEM] * 3,
        scratch_shapes=[prop_v, small, DMA((2,))],
        compiler_params=most,
        cost_estimate=pl.CostEstimate(flops=10**9, bytes_accessed=10**6, transcendentals=0),
        name="powers",
    )(propagator, coupling, packed)
    distance = 1
    after = factors
    while 2 * distance < cls_count:
        distance *= 2
        packed = pl.pallas_call(
            add_kernel,
            out_shape=jax.ShapeDtypeStruct(packed.shape, f32),
            in_specs=[VMEM] * 3,
            out_specs=VMEM,
            compiler_params=little,
            name="add",
        )(packed, theirs, after)
        theirs = partner(packed, "cls", distance)
    shells = pl.pallas_call(
        apply_kernel,
        out_shape=jax.ShapeDtypeStruct(split, f32),
        in_specs=[HBM, VMEM, VMEM, VMEM],
        out_specs=VMEM,
        scratch_shapes=[pltpu.VMEM(split, f32), DMA((chunks,))],
        compiler_params=most,
        cost_estimate=pl.CostEstimate(flops=10**9, bytes_accessed=melt.size * 4, transcendentals=0),
        name="apply",
    )(melt.reshape(nodes * classes, cells), lefts, factors, packed)
    fields = pl.pallas_call(
        functools.partial(combine_kernel, cls_count),
        out_shape=jax.ShapeDtypeStruct((1, FIELDS, chunks, LANES), f32),
        in_specs=[VMEM, VMEM, VMEM],
        out_specs=VMEM,
        scratch_shapes=[pltpu.VMEM((chunks, LANES), f32)],
        compiler_params=little,
        name="combine",
    )(packed, theirs, shells)
    pieces = [fields]
    for stage in stages(cell_count):
        held = jnp.concatenate(pieces, axis=0) if len(pieces) > 1 else pieces[0]
        pieces = [held] + [partner(held, "cell", offset) for offset in stage][::-1]
    pieces = pieces + [partner(piece, "cell", 1) for piece in pieces]
    rows = cell_count * chunks
    return pl.pallas_call(
        functools.partial(finish_kernel, len(pieces) // 2),
        out_shape=[jax.ShapeDtypeStruct(melt.shape, f32), jax.ShapeDtypeStruct(pressure.shape, f32)],
        in_specs=[VMEM] * (len(pieces) + 2),
        out_specs=[HBM, VMEM],
        scratch_shapes=[
            pltpu.VMEM(melt.shape, f32),
            pltpu.VMEM((cell_count, FIELDS, chunks, LANES), f32),
            pltpu.VMEM((SUBSTEPS, rows, LANES), f32),
            pltpu.VMEM((rows, LANES), f32),
            DMA((parts,)),
        ],
        compiler_params=little,
        name="finish",
    )(*pieces, shells, columns)


def solution(mesh):
    placed = (P(None, "cls", "cell"), P("cls", "cell"), P(("cell", "cls"), None), P(), P(), P())
    return jax.shard_map(
        shards,
        mesh=mesh,
        in_specs=placed,
        out_specs=(P(None, "cls", "cell"), P(("cell", "cls"), None)),
        check_vma=False,
    )
```

```python
import functools

import jax
import jax.numpy as jnp
from jax import lax
from jax.experimental import pallas as pl
from jax.experimental.pallas import tpu as pltpu
from jax.sharding import PartitionSpec as P

CLASSES = 32
SIDE = 16
SUBSTEPS = 4
COUNT_SCALE = 400.0
LANES = 128
GROUP = 8
FIELDS = 2 * SUBSTEPS


def grow(value, factor, times):
    for _ in range(times):
        value = value * factor
    return value


def iota(shape, dim):
    return lax.broadcasted_iota(jnp.int32, shape, dim)


def split2(x):
    high = x.astype(jnp.bfloat16)
    return high, (x - high.astype(jnp.float32)).astype(jnp.bfloat16)


def dot(a, b):
    return jnp.dot(a, b, preferred_element_type=jnp.float32)


def left_of(x):
    high, low = split2(x)
    return jnp.concatenate([high, high, low], axis=1)


def right_of(x):
    high, low = split2(x)
    return jnp.concatenate([high, low, high], axis=0)


def class_scale(prop):
    rows = [jnp.max(jnp.abs(prop[k]), axis=0, keepdims=True) for k in range(prop.shape[0])]
    return jnp.maximum(1.0, jnp.max(jnp.concatenate(rows, axis=0), axis=1, keepdims=True))


def param_copies(pairs, sems):
    copies = []
    for n, (source, target) in enumerate(pairs):
        own = pl.ds(lax.axis_index("cls") * target.shape[0], target.shape[0])
        copies.append(pltpu.make_async_copy(source.at[own], target, sems.at[n]))
    return copies


def fields_kernel(
    melt_hbm, counts_hbm, pressure_hbm, prop_hbm, coup_hbm, flux_hbm, out, melt, highs, lows, counts, pressure, prop, coup, flux, sems, other_sems
):
    nodes, classes, cells = melt.shape
    first = param_copies([(prop_hbm, prop), (flux_hbm, flux), (coup_hbm, coup)], other_sems)
    for copy in first:
        copy.start()
    parts = nodes // GROUP
    pieces = [
        pltpu.make_async_copy(
            melt_hbm.at[pl.ds(g * GROUP, GROUP)], melt.at[pl.ds(g * GROUP, GROUP)], sems.at[g]
        )
        for g in range(parts)
    ]
    for piece in pieces:
        piece.start()
    rest = [
        pltpu.make_async_copy(counts_hbm, counts, other_sems.at[3]),
        pltpu.make_async_copy(pressure_hbm, pressure, other_sems.at[4]),
    ]
    for copy in rest:
        copy.start()
    for copy in first:
        copy.wait()
    scale = class_scale(prop)
    width = classes * nodes
    table = jnp.concatenate(split2(prop[...].reshape(width, nodes)), axis=1)
    inverse = 1.0 / scale
    mask = iota((classes, width), 1) // nodes == iota((classes, width), 0)
    rows = [flux[...]]
    tall = GROUP * classes
    each = parts // SUBSTEPS
    for t in range(SUBSTEPS):
        wide = jnp.where(mask, jnp.concatenate([rows[-1]] * classes, axis=1), 0.0)
        pairs = dot(jnp.concatenate(split2(wide), axis=0), table)
        row = pairs[:classes] + pairs[classes:]
        rows.append((row[:, :nodes] + row[:, nodes:]) * inverse)
        for g in range(max(t - 1, 0) * each, parts if t == SUBSTEPS - 1 else t * each):
            pieces[g].wait()
            here = slice(g * tall, (g + 1) * tall)
            highs[here, :], lows[here, :] = split2(
                melt[g * GROUP : (g + 1) * GROUP].reshape(tall, cells)
            )
    spread_out = (iota((nodes, width), 1) // classes == iota((nodes, width), 0)).astype(jnp.bfloat16)
    parts_of_rows = jnp.concatenate(split2(jnp.concatenate(rows[1:], axis=0)), axis=0)
    dense = dot(parts_of_rows, spread_out)
    same = iota(dense.shape, 0) % classes == iota(dense.shape, 1) % classes
    dense = jnp.where(same, dense, 0.0).astype(jnp.bfloat16)
    count = SUBSTEPS * classes
    fluxes = dot(dense, highs[...])
    fluxes = fluxes[:count] + fluxes[count:] + dot(dense[:count], lows[...])
    spread = [
        grow(jnp.sum(rows[d] * coup[...], axis=1, keepdims=True), scale, d) for d in range(SUBSTEPS)
    ]
    for copy in rest:
        copy.wait()
    counts_n = counts[...].astype(jnp.float32) / (COUNT_SCALE * CLASSES)
    chunks = cells // LANES
    for r in range(chunks):
        here = counts_n[:, r * LANES : (r + 1) * LANES]
        for t in range(SUBSTEPS):
            part = fluxes[t * classes : (t + 1) * classes, r * LANES : (r + 1) * LANES]
            out[t, r : r + 1, :] = jnp.sum(grow(here * part, scale, t + 1), axis=0, keepdims=True)
        for d in range(SUBSTEPS):
            out[SUBSTEPS + d, r : r + 1, :] = jnp.sum(here * spread[d], axis=0, keepdims=True)
    out[2 * SUBSTEPS] = jnp.zeros((chunks, LANES), jnp.float32)
    per = pressure.shape[1] // LANES
    tile = pressure.shape[0] * per
    at = lax.axis_index("cls") * tile
    for i in range(tile):
        out[2 * SUBSTEPS, pl.ds(at + i, 1), :] = pressure[
            i // per : i // per + 1, (i % per) * LANES : (i % per + 1) * LANES
        ]


def powers_kernel(prop_hbm, coup_hbm, _, lefts, columns, factors, prop, coup, param_sems):
    classes, nodes = prop.shape[:2]
    params = param_copies([(prop_hbm, prop), (coup_hbm, coup)], param_sems)
    for copy in params:
        copy.start()
    for copy in params:
        copy.wait()
    scale = class_scale(prop)
    factors[...] = jnp.broadcast_to(scale, factors.shape)
    inverse = 1.0 / scale
    every = range(classes)
    unit = [prop[k] * inverse[k : k + 1, :] for k in every]
    first = [left_of(unit[k]) for k in every]
    square = [dot(first[k], right_of(unit[k])) for k in every]
    second = [left_of(square[k]) for k in every]
    for k in every:
        lefts[k] = left_of(dot(second[k], right_of(square[k])))
    start = jnp.concatenate(
        [jnp.transpose(coup[...]), jnp.zeros((nodes, LANES - classes), jnp.float32)], axis=1
    )
    once = [dot(first[k], right_of(start)) for k in every]
    start = start[:, :classes]
    twice = [
        dot(second[k], right_of(jnp.concatenate([start, once[k][:, :classes]], axis=1))) for k in every
    ]
    lane = iota((nodes, LANES), 1)
    for k in every:
        powers = [
            start[:, k : k + 1],
            once[k][:, k : k + 1],
            twice[k][:, k : k + 1],
            twice[k][:, classes + k : classes + k + 1],
        ]
        value = jnp.zeros((nodes, LANES), jnp.float32)
        for d in range(SUBSTEPS):
            grown = grow(powers[d], scale[k : k + 1, :], d)
            value = jnp.where(lane % SUBSTEPS == SUBSTEPS - 1 - d, grown, value)
        high = value.astype(jnp.bfloat16).astype(jnp.float32)
        value = jnp.where(lane < 2 * SUBSTEPS, high, jnp.where(lane < 3 * SUBSTEPS, value - high, 0.0))
        columns[pl.ds(k, nodes, stride=classes), :] = value


def apply_kernel(melt_hbm, lefts, factors, _, out, melt, sems):
    chunks = melt.shape[0]
    classes, nodes = lefts.shape[:2]
    loads = [
        pltpu.make_async_copy(melt_hbm.at[:, pl.ds(r * LANES, LANES)], melt.at[r], sems.at[r])
        for r in range(chunks)
    ]
    for load in loads:
        load.start()
    together = 2 if chunks % 2 == 0 else 1
    for r in range(0, chunks, together):
        for n in range(together):
            loads[r + n].wait()
        for k in range(classes):
            own = pl.ds(k, nodes, stride=classes)
            x = jnp.concatenate([melt[r + n, own, :] for n in range(together)], axis=1)
            part = grow(dot(lefts[k], right_of(x)), factors[k : k + 1, :1], SUBSTEPS)
            for n in range(together):
                out[r + n, own, :] = part[:, n * LANES : (n + 1) * LANES]


def add_kernel(mine, theirs, _, out):
    out[...] = mine[...] + theirs[...]


def combine_kernel(senders, mine, theirs, _, out_ref, kept):
    out = out_ref.at[0]
    total = mine[...] + theirs[...]
    tail = out.shape[0] - 1
    tile = out.shape[1] // senders
    pressure = total[2 * SUBSTEPS]
    wall = 0.5 * pressure
    for t in range(SUBSTEPS - 1):
        out[t] = total[t] + total[SUBSTEPS + t] * wall
        out[SUBSTEPS - 1 + t] = total[SUBSTEPS + t]
    out[tail - 1] = pressure
    gas = total[SUBSTEPS - 1] + total[2 * SUBSTEPS - 1] * wall
    kept[...] = gas
    out[tail] = jnp.broadcast_to(total_of(gas), gas.shape)
    out[tail, :tile, :] = kept[pl.ds(lax.axis_index("cls") * tile, tile), :]


def total_of(x):
    tiles = jnp.sum(x.reshape(-1, GROUP, LANES), axis=0)
    return jnp.sum(jnp.sum(tiles, axis=1, keepdims=True), axis=0, keepdims=True)


def laplacian(x, plane):
    rows = x.shape[0]
    row = iota(x.shape, 0)
    lane = iota(x.shape, 1)
    per = plane // LANES
    inside = row % per * LANES + lane
    col = lane % SIDE
    total = jnp.where(col == 0, 0.0, pltpu.roll(x, 1, 1))
    total += jnp.where(col == SIDE - 1, 0.0, pltpu.roll(x, LANES - 1, 1))
    up = pltpu.roll(x, SIDE, 1)
    up = jnp.where(lane < SIDE, pltpu.roll(up, 1, 0), up)
    total += jnp.where(inside < SIDE, 0.0, up)
    down = pltpu.roll(x, LANES - SIDE, 1)
    down = jnp.where(lane >= LANES - SIDE, pltpu.roll(down, rows - 1, 0), down)
    total += jnp.where(inside >= plane - SIDE, 0.0, down)
    total += jnp.where(row < per, 0.0, pltpu.roll(x, per, 0))
    total += jnp.where(row >= rows - per, 0.0, pltpu.roll(x, rows - per, 0))
    return total - 6.0 * x


def finish_kernel(count, *refs):
    mine, theirs = refs[:count], refs[count : 2 * count]
    shells, columns, out_hbm, pressure_out, out, window, walls_all, last, out_sems = refs[2 * count :]
    nodes, classes, cells = out.shape
    chunks = cells // LANES
    parts = nodes // GROUP
    width = GROUP * classes

    def piece(g):
        return pl.ds(g * GROUP, GROUP)

    plane = pressure_out.shape[1]
    cell = lax.axis_index("cell")
    blocks = window.shape[0]
    for n, offset in enumerate(offsets(blocks)):
        part, slot = n // mine[0].shape[0], n % mine[0].shape[0]
        window[cell ^ offset] = mine[part][slot]
        window[cell ^ 1 ^ offset] = theirs[part][slot]
    rows = blocks * chunks
    per = plane // LANES
    tile = pressure_out.shape[0] * per

    def field_of(f):
        return window[:, f].reshape(rows, LANES)

    field = field_of(2 * SUBSTEPS - 2)
    answer = field_of(SUBSTEPS - 1)
    answer_total = total_of(answer)
    chamber = None
    walls = []
    for t in range(SUBSTEPS):
        gas = answer * (0.5 * field) if t else field_of(0)
        for s in range(1, t):
            gas = gas + field_of(SUBSTEPS - 1 + t - s) * walls[s]
        if 0 < t < SUBSTEPS - 1:
            gas = gas + field_of(t)
        total = total_of(gas)
        if t == SUBSTEPS - 1:
            rest = jnp.sum(window[:, 2 * SUBSTEPS - 1], axis=0)
            total = total + rest[tile : tile + 1, :1]
        if t:
            field = field + 0.2 * chamber
            gas = gas + answer * (0.1 * chamber)
            total = total + answer_total * (0.1 * chamber)
        walls.append(0.5 * field)
        walls_all[t] = walls[t]
        field = 0.8 * field + 0.15 * laplacian(field, plane) + 0.1 * gas
        chamber = 1.5 - 0.5 * total / (rows * LANES)
    last[...] = field + 0.2 * chamber
    first = cell * chunks
    at = first + lax.axis_index("cls") * tile
    for i in range(tile):
        pressure_out[i // per : i // per + 1, (i % per) * LANES : (i % per + 1) * LANES] = (
            last[pl.ds(at + i, 1), :] + 0.1 * mine[0][0, 2 * SUBSTEPS - 1, i : i + 1, :]
        )
    right = []
    for r in range(chunks):
        wall = jnp.concatenate([walls_all[s, pl.ds(first + r, 1), :] for s in range(SUBSTEPS)], axis=0)
        high = wall.astype(jnp.bfloat16).astype(jnp.float32)
        right.append(jnp.concatenate([high, wall - high, high, jnp.zeros_like(high)], axis=0))
    right = jnp.concatenate(right, axis=1).astype(jnp.bfloat16)
    stores = [
        pltpu.make_async_copy(out.at[piece(g)], out_hbm.at[piece(g)], out_sems.at[g]) for g in range(parts)
    ]
    for g in range(parts):
        here = slice(g * width, (g + 1) * width)
        change = dot(columns[here, : 4 * SUBSTEPS].astype(jnp.bfloat16), right)
        for r in range(chunks):
            lanes = slice(r * LANES, (r + 1) * LANES)
            value = shells[r, here, :] + change[:, lanes]
            out[g * GROUP : (g + 1) * GROUP, :, lanes] = value.reshape(GROUP, classes, LANES)
        stores[g].start()
    for store in stores:
        store.wait()


HBM = pl.BlockSpec(memory_space=pltpu.HBM)
VMEM = pl.BlockSpec(memory_space=pltpu.VMEM)
DMA = pltpu.SemaphoreType.DMA


def stages(count):
    bits = [1 << b for b in range(1, count.bit_length() - 1)]
    pairs = [bits[n : n + 2] for n in range(0, len(bits), 2)]
    return [[sum(pair)] + pair[::-1] if len(pair) > 1 else pair for pair in pairs]


def offsets(count):
    found = [0]
    for stage in stages(count):
        found = found + [m ^ offset for offset in stage[::-1] for m in found]
    return found


def partner(value, axis, distance):
    return lax.ppermute(value, axis, [(i, i ^ distance) for i in range(lax.axis_size(axis))])


def shards(melt, counts, pressure, propagator, coupling, flux_weights):
    nodes, classes, cells = melt.shape
    chunks = cells // LANES
    f32 = jnp.float32
    split = (chunks, nodes * classes, LANES)
    whole = pltpu.CompilerParams(vmem_limit_bytes=60 * 2**20)
    most = pltpu.CompilerParams(vmem_limit_bytes=48 * 2**20)
    little = pltpu.CompilerParams(vmem_limit_bytes=32 * 2**20)
    cls_count = lax.axis_size("cls")
    cell_count = lax.axis_size("cell")
    prop_v = pltpu.VMEM((classes, nodes, nodes), f32)
    small = pltpu.VMEM((classes, nodes), f32)
    parts = nodes // GROUP
    packed = pl.pallas_call(
        fields_kernel,
        out_shape=jax.ShapeDtypeStruct((FIELDS + 1, chunks, LANES), f32),
        in_specs=[HBM] * 6,
        out_specs=VMEM,
        scratch_shapes=[
            pltpu.VMEM(melt.shape, f32),
            pltpu.VMEM((nodes * classes, cells), jnp.bfloat16),
            pltpu.VMEM((nodes * classes, cells), jnp.bfloat16),
            pltpu.VMEM(counts.shape, counts.dtype),
            pltpu.VMEM(pressure.shape, f32),
            prop_v,
            small,
            small,
            DMA((parts,)),
            DMA((5,)),
        ],
        compiler_params=whole,
        name="fields",
    )(melt, counts, pressure, propagator, coupling, flux_weights)
    lefts_shape = (classes, nodes, 3 * nodes)
    theirs = partner(packed, "cls", 1)
    lefts, columns, factors = pl.pallas_call(
        powers_kernel,
        out_shape=[
            jax.ShapeDtypeStruct(lefts_shape, jnp.bfloat16),
            jax.ShapeDtypeStruct(split[1:], f32),
            jax.ShapeDtypeStruct((classes, LANES), f32),
        ],
        in_specs=[HBM, HBM, VMEM],
        out_specs=[VMEM] * 3,
        scratch_shapes=[prop_v, small, DMA((2,))],
        compiler_params=most,
        cost_estimate=pl.CostEstimate(flops=10**9, bytes_accessed=10**6, transcendentals=0),
        name="powers",
    )(propagator, coupling, packed)
    distance = 1
    after = factors
    while 2 * distance < cls_count:
        distance *= 2
        packed = pl.pallas_call(
            add_kernel,
            out_shape=jax.ShapeDtypeStruct(packed.shape, f32),
            in_specs=[VMEM] * 3,
            out_specs=VMEM,
            compiler_params=little,
            name="add",
        )(packed, theirs, after)
        theirs = partner(packed, "cls", distance)
    shells = pl.pallas_call(
        apply_kernel,
        out_shape=jax.ShapeDtypeStruct(split, f32),
        in_specs=[HBM, VMEM, VMEM, VMEM],
        out_specs=VMEM,
        scratch_shapes=[pltpu.VMEM(split, f32), DMA((chunks,))],
        compiler_params=most,
        cost_estimate=pl.CostEstimate(flops=10**9, bytes_accessed=melt.size * 4, transcendentals=0),
        name="apply",
    )(melt.reshape(nodes * classes, cells), lefts, factors, packed)
    fields = pl.pallas_call(
        functools.partial(combine_kernel, cls_count),
        out_shape=jax.ShapeDtypeStruct((1, FIELDS, chunks, LANES), f32),
        in_specs=[VMEM, VMEM, VMEM],
        out_specs=VMEM,
        scratch_shapes=[pltpu.VMEM((chunks, LANES), f32)],
        compiler_params=little,
        name="combine",
    )(packed, theirs, shells)
    pieces = [fields]
    for stage in stages(cell_count):
        held = jnp.concatenate(pieces, axis=0) if len(pieces) > 1 else pieces[0]
        pieces = [held] + [partner(held, "cell", offset) for offset in stage][::-1]
    pieces = pieces + [partner(piece, "cell", 1) for piece in pieces]
    rows = cell_count * chunks
    return pl.pallas_call(
        functools.partial(finish_kernel, len(pieces) // 2),
        out_shape=[jax.ShapeDtypeStruct(melt.shape, f32), jax.ShapeDtypeStruct(pressure.shape, f32)],
        in_specs=[VMEM] * (len(pieces) + 2),
        out_specs=[HBM, VMEM],
        scratch_shapes=[
            pltpu.VMEM(melt.shape, f32),
            pltpu.VMEM((cell_count, FIELDS, chunks, LANES), f32),
            pltpu.VMEM((SUBSTEPS, rows, LANES), f32),
            pltpu.VMEM((rows, LANES), f32),
            DMA((parts,)),
        ],
        compiler_params=little,
        name="finish",
    )(*pieces, shells, columns)


def solution(mesh):
    placed = (P(None, "cls", "cell"), P("cls", "cell"), P(("cell", "cls"), None), P(), P(), P())
    return jax.shard_map(
        shards,
        mesh=mesh,
        in_specs=placed,
        out_specs=(P(None, "cls", "cell"), P(("cell", "cls"), None)),
        check_vma=False,
    )
```
